512 devices in a mesh: lang: 16 (over z), dp: 4 (over y), fsdp: 8 (over x, core).
Axes of the slice: x: 4, y: 4, z: 16, core: 2. Of those that a mesh axis runs over, the one named last changes fastest.
Arguments:
- tokens: bfloat16 [16, 1536, 2048], P('lang', ('dp', 'fsdp')), may hold values from -48 to 48
- cotangent: bfloat16 [16, 1536, 2048], P('lang', ('dp', 'fsdp')), may hold values from -48 to 48
- lengths: int32 [16, 12], P('lang'), may hold values from 32 to 128
- up_weight: bfloat16 [2048, 8192], P(None, ('dp', 'fsdp')), may hold values from -0.125 to 0.125
- down_weight: bfloat16 [8192, 2048], P(('dp', 'fsdp')), may hold values from -0.0625 to 0.0625
- targets: float32 [16, 16], replicated, may hold values from 0 to 0.5
- accept: int32 [16, 16], replicated, may hold values 0 or 1
Outputs:
- up_update: float32 [2048, 8192], P('lang', ('dp', 'fsdp'))
- down_update: float32 [8192, 2048], P(('dp', 'fsdp'), 'lang')
- new_targets: float32 [16, 16], replicated
The draws below stay inside these ranges and needn't reach their ends.
All inputs are finite; a program needn't handle non-finite values.
Results may differ from the reference program's by a relative error of at most 0.0065.
Values may be sent and summed in bfloat16 or wider, within the bound.
A program may use at most 64 MiB of HBM per device.

```python
import jax
import jax.numpy as jnp
from jax import lax

D = 2048
FF = 8192
SEQ = 128
LANGS = 16
LTOK = 1536
NSEQ = 12


def mixed_field(own, common, shares, slopes):
    ramp = jnp.arange(D, dtype=jnp.float32)[None, None, :] / D
    profile = jnp.exp(slopes * ramp)
    mixed = jnp.sqrt(shares) * common + jnp.sqrt(1.0 - shares) * own
    return (mixed * profile).astype(jnp.bfloat16)


def draw_tokens(key, part):
    key = jax.random.fold_in(key, 11)
    key_own, key_common, key_share, key_slope = jax.random.split(key, 4)
    own = jnp.clip(jax.random.normal(key_own, (LANGS, LTOK, D), jnp.float32), -6.0, 6.0)
    common = jnp.clip(jax.random.normal(key_common, (1, LTOK, D), jnp.float32), -6.0, 6.0)
    shares = jax.random.uniform(key_share, (LANGS, 1, 1), jnp.float32, 0.2, 0.6)
    slopes = jax.random.uniform(key_slope, (LANGS, 1, 1), jnp.float32, 0.3, 1.5)
    return mixed_field(own, common, shares, slopes)


def draw_cotangent(key, part):
    key = jax.random.fold_in(key, 12)
    key_own, key_common, key_share, key_slope = jax.random.split(key, 4)
    own = jnp.clip(jax.random.normal(key_own, (LANGS, LTOK, D), jnp.float32), -6.0, 6.0)
    common = jnp.clip(jax.random.normal(key_common, (1, LTOK, D), jnp.float32), -6.0, 6.0)
    shares = jax.random.uniform(key_share, (LANGS, 1, 1), jnp.float32, 0.2, 0.6)
    slopes = jax.random.uniform(key_slope, (LANGS, 1, 1), jnp.float32, 0.3, 1.5)
    return mixed_field(own, common, shares, slopes)


def set_ends(drawn, key, smallest, top_value):
    longest = drawn.shape.index(max(drawn.shape))
    spots = []
    for shift in (0, 1):
        where = [jax.random.randint(jax.random.fold_in(key, axis), (), 0, length) for axis, length in enumerate(drawn.shape)]
        where[longest] = (where[longest] + shift) % drawn.shape[longest]
        spots.append(tuple(where))
    return drawn.at[spots[0]].set(smallest).at[spots[1]].set(top_value)


def steps_of(stream_key, shape, cuts, smallest, high):
    loudness = 1.0
    for dim, shards_of in cuts:
        steps = jax.random.uniform(jax.random.fold_in(jax.random.fold_in(stream_key, 6), dim), (shards_of,), jnp.float32, smallest / len(cuts), high / len(cuts))
        loudness = loudness * jnp.repeat(jnp.exp(steps), shape[dim] // shards_of).reshape((-1,) + (1,) * (len(shape) - 1 - dim))
    return loudness


def normal_values(rng, dims, spread, reach, pieces=(), kind=jnp.bfloat16):
    values = jax.random.normal(rng, dims, jnp.float32) * spread
    if len(pieces) > 0:
        values = steps_of(rng, dims, pieces, -0.22, 0.18) * values
    return jnp.clip(values, min=-reach, max=reach).astype(kind)


def setup_inputs(seed: int = 0) -> dict:
    streams_of = jax.random.split(jax.random.key(seed), 8)
    tokens = draw_tokens(jax.random.fold_in(streams_of[7], 71), 0)
    cotangent = draw_cotangent(jax.random.fold_in(streams_of[7], 71), 0)
    lengths = set_ends(jax.random.randint(streams_of[2], (LANGS, NSEQ), SEQ // 4, SEQ + 1), jax.random.fold_in(streams_of[2], 1), SEQ // 4, SEQ).astype(jnp.int32)
    up_weight = normal_values(streams_of[3], (D, FF), D ** -0.5, 0.125, ((1, 32),))
    down_weight = normal_values(streams_of[4], (FF, D), FF ** -0.5, 0.0625, ((0, 32),))
    targets = jnp.clip(jax.random.uniform(streams_of[5], (LANGS, LANGS), jnp.float32, 0.0, 0.5), 0.0, 0.5)
    accept = set_ends((jax.random.randint(streams_of[6], (LANGS, LANGS), 0, 4) < 3).astype(jnp.int32), jax.random.fold_in(streams_of[6], 1), 0, 1)
    return {"tokens": tokens, "cotangent": cotangent, "lengths": lengths, "up_weight": up_weight, "down_weight": down_weight, "targets": targets, "accept": accept}


ema_rate = 0.01
clip_level = 0.25

def gelu_tanh(values):
    return jax.nn.gelu(values, approximate=True)

def token_grads(inputs, upstream, seq_lengths, first, w_up, w_down):
    row_count = inputs.shape[0]
    row_index = first + jnp.arange(row_count, dtype=jnp.int32)
    seq_of = row_index // SEQ
    position = row_index % SEQ
    chosen = (seq_of[:, None] == jnp.arange(seq_lengths.shape[0], dtype=jnp.int32)[None, :]).astype(jnp.int32)
    seq_limit = lax.optimization_barrier(jnp.sum(chosen * seq_lengths[None, :], axis=1))
    keep_mask = (position < seq_limit).astype(upstream.dtype)
    masked = upstream * keep_mask[:, None]
    preact = jnp.dot(inputs, w_up, preferred_element_type=jnp.float32)
    hidden, backward = jax.vjp(gelu_tanh, preact)
    hidden = hidden.astype(jnp.bfloat16)
    hidden_grad = lax.dot_general(masked, w_down, (((1,), (1,)), ((), ())), preferred_element_type=jnp.float32)
    preact_grad = backward(hidden_grad)[0].astype(jnp.bfloat16)
    g_up = lax.dot_general(inputs, preact_grad, (((0,), (0,)), ((), ())), preferred_element_type=jnp.float32)
    g_dt = lax.dot_general(masked, hidden, (((0,), (0,)), ((), ())), preferred_element_type=jnp.float32)
    return (g_up, g_dt)

def vaccinate(gram_sums, targets, accept):
    groups = gram_sums.shape[0]
    identity = jnp.eye(groups, dtype=jnp.float32)
    diagonal = jnp.diagonal(gram_sums)
    cos_pairs = gram_sums / jnp.sqrt(diagonal[:, None] * diagonal[None, :])
    allowed = accept.astype(jnp.float32) * (1.0 - identity)
    target_roots = jnp.sqrt(1.0 - targets * targets)
    high = lax.Precision.HIGHEST

    def project(target, coeffs):
        onehot = (jnp.arange(groups, dtype=jnp.int32) == target).astype(jnp.float32)
        column = jnp.dot(gram_sums, onehot, precision=high)
        inner_prod = jnp.dot(coeffs, column, precision=high)
        norm_sq = lax.optimization_barrier(jnp.sum(jnp.dot(coeffs, gram_sums, precision=high) * coeffs, axis=1))
        own_norm = jnp.dot(column, onehot, precision=high)
        cosine = inner_prod / jnp.sqrt(norm_sq * own_norm)
        target_col = jnp.dot(targets, onehot, precision=high)
        target_root = jnp.dot(target_roots, onehot, precision=high)
        gate_col = jnp.dot(allowed, onehot, precision=high)
        sine = jnp.sqrt(jnp.maximum(1.0 - cosine * cosine, 0.0))
        step_size = jnp.sqrt(norm_sq) * (target_col * sine - cosine * target_root) / (jnp.sqrt(own_norm) * target_root)
        applied = jnp.where(gate_col > 0.5, step_size, 0.0)
        return coeffs + applied[:, None] * onehot[None, :]
    coeffs = lax.fori_loop(0, groups, project, identity)
    weights = lax.optimization_barrier(jnp.sum(coeffs, axis=0))
    new_targets = (1.0 - ema_rate) * targets + ema_rate * cos_pairs
    return (weights, new_targets)

def reference(tokens, cotangent, lengths, up_weight, down_weight, targets, accept):

    def per_language(packed):
        inputs, upstream, seq_lengths = packed
        g_up, g_dt = token_grads(inputs, upstream, seq_lengths, 0, up_weight, down_weight)
        return (g_up.astype(jnp.bfloat16), g_dt.astype(jnp.bfloat16))
    grads_up, grads_dt = lax.map(per_language, (tokens, cotangent, lengths))
    groups = grads_up.shape[0]
    flat_up = grads_up.reshape(groups, -1)
    flat_dt = grads_dt.reshape(groups, -1)
    gram_sums = jnp.dot(flat_up, flat_up.T, preferred_element_type=jnp.float32) + jnp.dot(flat_dt, flat_dt.T, preferred_element_type=jnp.float32)
    weights, new_targets = vaccinate(gram_sums, targets, accept)

    def accumulate(language, totals):
        return (totals[0] + weights[language] * grads_up[language].astype(jnp.float32), totals[1] + weights[language] * grads_dt[language].astype(jnp.float32))
    initial = (jnp.zeros(grads_up.shape[1:], jnp.float32), jnp.zeros(grads_dt.shape[1:], jnp.float32))
    combined_up, combined_dt = lax.fori_loop(0, groups, accumulate, initial)
    mean_square = (jnp.sum(combined_up * combined_up) + jnp.sum(combined_dt * combined_dt)) / (2.0 * D * FF)
    factor = jnp.minimum(1.0, clip_level / jnp.sqrt(mean_square + 1e-06))
    return (factor * combined_up, (factor * combined_dt).T, new_targets)
```

```python
import functools

import jax
import jax.numpy as jnp
from jax import lax
from jax.experimental import pallas as pl
from jax.experimental.pallas import tpu as pltpu
from jax.sharding import PartitionSpec as P

D = 2048
FF = 8192
SEQ = 128
LTOK = 1536
LANGS = 16
NY = 4
NX = 4
NF = 8
ROWS = 48
HID = 256
DS = 128
HALF = D // 2

ema_rate = 0.01
clip_level = 0.25
MESH = pl.DeviceIdType.MESH

OFFSETS = (0, 3, 1, 2)
ARRIVALS = (
    (0, 1), (0, 2), (1, 0), (2, 0), (0, 3), (1, 1), (2, 1), (1, 2), (2, 2),
    (3, 0), (1, 3), (2, 3), (3, 1), (3, 2), (3, 3),
)


class Gather:
    def __init__(self, own, buf, first, pos, core, send, recv, sib_send, sib_recv):
        self.own, self.buf, self.first, self.pos, self.core = own, buf, first, pos, core
        self.send, self.recv, self.sib_send, self.sib_recv = send, recv, sib_send, sib_recv
        self.started = []

    def place(self, second_role, first_role):
        first = lax.rem(self.pos[self.first] + OFFSETS[first_role], 4)
        other = "y" if self.first == "x" else "x"
        second = lax.rem(self.pos[other] + OFFSETS[second_role], 4)
        return (first, second) if self.first == "x" else (second, first)

    def rows(self, x, y, core):
        return pl.ds(pl.multiple_of((y * NF + x * 2 + core) * ROWS, 16), ROWS)

    def target(self, ring, step):
        axis = self.first if ring == 0 else ("y" if self.first == "x" else "x")
        index = lax.rem(self.pos[axis] + step, 4)
        return {"fsdp": index * 2 + self.core} if axis == "x" else {"dp": index}

    def part(self, roles, half):
        x, y = self.place(*roles)
        rows = self.rows(x, y, self.core)
        if half is None:
            return self.buf.at[rows, :]
        return self.buf.at[rows, pl.ds(half * HALF, HALF)]

    def copy(self, roles, half, ring, step, send_index, there):
        dst = self.part(roles, half)
        src = self.own if roles == (0, 0) else dst
        copy = pltpu.make_async_remote_copy(
            src_ref=src,
            dst_ref=dst,
            send_sem=self.send.at[send_index],
            recv_sem=self.recv.at[there],
            device_id=self.target(ring, step),
            device_id_type=MESH,
        )
        copy.start()
        self.started.append(copy)

    def to_sibling(self, roles):
        dst = self.part(roles, None)
        src = self.own if roles == (0, 0) else dst
        index = roles[0] * 4 + roles[1]
        copy = pltpu.make_async_remote_copy(
            src_ref=src,
            dst_ref=dst,
            send_sem=self.sib_send.at[index],
            recv_sem=self.sib_recv.at[index],
            device_id={"fsdp": self.pos["x"] * 2 + (1 - self.core)},
            device_id_type=MESH,
        )
        copy.start()
        self.started.append(copy)

    def ready(self, roles):
        second, first = roles
        if second == 0:
            if first == 0:
                self.copy(roles, None, 0, 1, 0, 2 * 1)
                self.copy(roles, None, 0, 3, 1, 2 * 2)
            elif first == 1:
                self.copy(roles, 0, 0, 1, 2, 2 * 3)
            elif first == 2:
                self.copy(roles, 1, 0, 3, 3, 2 * 3 + 1)
            base = 4 + 4 * first
            self.copy(roles, None, 1, 1, base, 2 * (4 * 1 + first))
            self.copy(roles, None, 1, 3, base + 1, 2 * (4 * 2 + first))
        elif second == 1:
            self.copy(roles, 0, 1, 1, 4 + 4 * first + 2, 2 * (4 * 3 + first))
        elif second == 2:
            self.copy(roles, 1, 1, 3, 4 + 4 * first + 3, 2 * (4 * 3 + first) + 1)
        self.to_sibling(roles)

    def arrive(self, roles):
        halves = (0, 1) if 3 in roles and (roles[0] == 3 or roles == (0, 3)) else (None,)
        for half in halves:
            ref = self.part(roles, half)
            pltpu.make_async_remote_copy(
                src_ref=ref,
                dst_ref=ref,
                send_sem=self.send.at[0],
                recv_sem=self.recv.at[2 * (4 * roles[0] + roles[1]) + (half or 0)],
                device_id=self.target(0, 1),
                device_id_type=MESH,
            ).wait_recv()

    def from_sibling(self, roles):
        x, y = self.place(*roles)
        ref = self.buf.at[self.rows(x, y, 1 - self.core), :]
        index = roles[0] * 4 + roles[1]
        pltpu.make_async_remote_copy(
            src_ref=ref,
            dst_ref=ref,
            send_sem=self.sib_send.at[index],
            recv_sem=self.sib_recv.at[index],
            device_id={"fsdp": self.pos["x"] * 2 + (1 - self.core)},
            device_id_type=MESH,
        ).wait_recv()


def distance_of(k):
    m = 8 - (k + 1) // 2
    return jnp.where(lax.rem(k, 2) == 1, m, LANGS - m)


def exchange(buf, axis, count, me, send, recv):
    copies = []
    for r in range(1, count):
        copy = pltpu.make_async_remote_copy(
            src_ref=buf.at[me],
            dst_ref=buf.at[me],
            send_sem=send.at[r],
            recv_sem=recv.at[r],
            device_id={axis: lax.rem(me + r, count)},
            device_id_type=MESH,
        )
        copy.start()
        copies.append(copy)
    for r in range(1, count):
        ref = buf.at[lax.rem(me + count - r, count)]
        pltpu.make_async_remote_copy(
            src_ref=ref,
            dst_ref=ref,
            send_sem=send.at[r],
            recv_sem=recv.at[r],
            device_id={axis: lax.rem(me + r, count)},
            device_id_type=MESH,
        ).wait_recv()
    return copies


def vaccinate(gram, targets, accept):
    rows = lax.broadcasted_iota(jnp.int32, (LANGS, LANGS), 0)
    cols = lax.broadcasted_iota(jnp.int32, (LANGS, LANGS), 1)
    identity = (rows == cols).astype(jnp.float32)
    allowed = accept.astype(jnp.float32) * (1.0 - identity)
    diag_col = jnp.sum(gram * identity, axis=1, keepdims=True)
    diag_row = jnp.sum(gram * identity, axis=0, keepdims=True)
    cos_pairs = gram / jnp.sqrt(diag_col * diag_row)
    roots = jnp.sqrt(1.0 - targets * targets)
    coeffs, product = identity, gram
    for j in range(LANGS):
        inner = product[:, j : j + 1]
        norm_sq = jnp.sum(product * coeffs, axis=1, keepdims=True)
        own = gram[j : j + 1, j : j + 1]
        cosine = inner / jnp.sqrt(norm_sq * own)
        root = roots[:, j : j + 1]
        sine = jnp.sqrt(jnp.maximum(1.0 - cosine * cosine, 0.0))
        step = (
            jnp.sqrt(norm_sq) * (targets[:, j : j + 1] * sine - cosine * root) / (jnp.sqrt(own) * root)
        )
        step = jnp.where(allowed[:, j : j + 1] > 0.5, step, 0.0)
        coeffs = coeffs + step * identity[j : j + 1, :]
        product = product + step * gram[j : j + 1, :]
    weights_row = jnp.sum(coeffs, axis=0, keepdims=True)
    weights_col = jnp.sum(identity * weights_row, axis=1, keepdims=True)
    quad = jnp.sum(weights_col * gram * weights_row, axis=(0, 1), keepdims=True)
    mean_square = jnp.maximum(quad, 0.0) / (2.0 * D * FF)
    factor = jnp.minimum(1.0, clip_level / jnp.sqrt(mean_square + 1e-06))
    new_targets = (1.0 - ema_rate) * targets + ema_rate * cos_pairs
    return weights_col * factor, new_targets


def kernel(
    tok_ref, cot_ref, len_ref, wup_hbm, wdn_hbm, tgt_ref, acc_ref,
    up_out, dn_out, nt_out,
    x_buf, c_buf, wup, wdn, wdn_t, p_t, h_t, outbox, inbox, pairs, st1, st2, st3, wv, comb,
    local_sem,
    t_send, t_recv, t_sib_send, t_sib_recv,
    c_send, c_recv, c_sib_send, c_sib_recv,
    a_send, a_recv, s1_send, s1_recv, s2_send, s2_recv, s3_send, s3_recv,
):
    z, y, f = lax.axis_index("lang"), lax.axis_index("dp"), lax.axis_index("fsdp")
    x, core = f // 2, lax.rem(f, 2)

    barrier = pltpu.get_barrier_semaphore()
    for axis, count, me in (("fsdp", NF, f), ("dp", NY, y), ("lang", LANGS, z)):
        for r in range(1, count):
            pl.semaphore_signal(
                barrier, inc=1, device_id={axis: lax.rem(me + r, count)}, device_id_type=MESH
            )

    pos = {"x": x, "y": y}
    tok, cot = tok_ref.at[0], cot_ref.at[0]
    tokens = Gather(tok, x_buf, "x", pos, core, t_send, t_recv, t_sib_send, t_sib_recv)
    upstream = Gather(cot, c_buf, "y", pos, core, c_send, c_recv, c_sib_send, c_sib_recv)
    mine = tokens.rows(x, y, core)
    local = [
        pltpu.make_async_copy(wdn_hbm, wdn, local_sem.at[0]),
        pltpu.make_async_copy(wup_hbm, wup, local_sem.at[1]),
        pltpu.make_async_copy(tok, x_buf.at[mine, :], local_sem.at[2]),
        pltpu.make_async_copy(cot, c_buf.at[mine, :], local_sem.at[3]),
    ]
    for copy in local:
        copy.start()

    pl.semaphore_wait(barrier, (NF - 1) + (NY - 1) + (LANGS - 1))
    tokens.ready((0, 0))
    upstream.ready((0, 0))

    for copy in local:
        copy.wait()

    @pl.loop(0, D // 256)
    def _(i):
        part = pl.ds(pl.multiple_of(i * 256, 256), 256)
        wdn_t[part, :] = wdn[:, part].T

    for roles in ARRIVALS:
        for gather in (tokens, upstream):
            gather.arrive(roles)
            gather.ready(roles)
    for roles in ((0, 0),) + ARRIVALS:
        for gather in (tokens, upstream):
            gather.from_sibling(roles)

    @pl.loop(0, LTOK // 256)
    def _(b):
        part = pl.ds(pl.multiple_of(b * 256, 256), 256)
        v = jnp.dot(x_buf[part, :], wup[...], preferred_element_type=jnp.float32)
        hg = jnp.dot(c_buf[part, :], wdn_t[...], preferred_element_type=jnp.float32)
        row = lax.broadcasted_iota(jnp.int32, (256, HID), 0)
        first, second = len_ref[0, 2 * b], len_ref[0, 2 * b + 1]
        keep = row < jnp.where(row < SEQ, first, second + SEQ)
        k = 0.7978845608028654
        sq = v * v
        t = jnp.tanh(k * (v + 0.044715 * (sq * v)))
        cdf = 0.5 * (1.0 + t)
        slope = cdf + 0.5 * v * (1.0 - t * t) * (k * (1.0 + 3.0 * 0.044715 * sq))
        p = jnp.where(keep, hg * slope, 0.0).astype(jnp.bfloat16)
        h = jnp.where(keep, v * cdf, 0.0).astype(jnp.bfloat16)
        p_t[:, part] = p.T
        h_t[:, part] = h.T

    def chunk(owner):
        part = pl.ds(pl.multiple_of(owner * DS, DS), DS)
        up = jnp.dot(p_t[...], x_buf[:, part], preferred_element_type=jnp.float32)
        dn = jnp.dot(h_t[...], c_buf[:, part], preferred_element_type=jnp.float32)
        return up.astype(jnp.bfloat16), dn.astype(jnp.bfloat16)

    def grad_copy(k, block):
        return pltpu.make_async_remote_copy(
            src_ref=outbox.at[k],
            dst_ref=inbox.at[block],
            send_sem=a_send.at[k],
            recv_sem=a_recv.at[k],
            device_id={"lang": lax.rem(z + distance_of(k), LANGS)},
            device_id_type=MESH,
        )

    @pl.loop(0, LANGS - 1)
    def _(k):
        up, dn = chunk(lax.rem(z + distance_of(k), LANGS))
        outbox[k, :, :DS] = up
        outbox[k, :, DS:] = dn
        grad_copy(k, z).start()

    up, dn = chunk(z)
    inbox[z, :, :DS] = up
    inbox[z, :, DS:] = dn

    for copy in tokens.started + upstream.started:
        copy.wait_send()

    @pl.loop(0, LANGS - 1)
    def _(k):
        grad_copy(k, lax.rem(z + LANGS - distance_of(k), LANGS)).wait_recv()

    pairs[...] = jnp.zeros_like(pairs)

    @pl.loop(0, 4)
    def _(g):
        parts = [
            inbox[:, pl.ds(pl.multiple_of(g * 64 + i * 16, 16), 16), :].reshape(256, 256)
            for i in range(4)
        ]
        a = jnp.concatenate(parts, axis=1)
        pairs[...] += lax.dot_general(
            a, a, (((1,), (1,)), ((), ())), preferred_element_type=jnp.float32
        )

    ri = lax.broadcasted_iota(jnp.int32, (256, 256), 0)
    ci = lax.broadcasted_iota(jnp.int32, (256, 256), 1)
    same = jnp.where(lax.rem(ri, 16) == lax.rem(ci, 16), pairs[...], 0.0)
    by_row = jnp.sum(same.reshape(LANGS, 16, 256), axis=1)
    li = lax.broadcasted_iota(jnp.int32, (256, 128), 0) // 16
    lj = lax.broadcasted_iota(jnp.int32, (256, 128), 1)
    select = (li == lj).astype(jnp.float32)
    st1[f] = jnp.dot(
        by_row, select, precision=lax.Precision.HIGHEST, preferred_element_type=jnp.float32
    )
    sends = exchange(st1, "fsdp", NF, f, s1_send, s1_recv)
    st2[y] = jnp.sum(st1[...], axis=0)
    sends += exchange(st2, "dp", NY, y, s2_send, s2_recv)
    st3[z] = jnp.sum(st2[...], axis=0)
    sends += exchange(st3, "lang", LANGS, z, s3_send, s3_recv)
    gram = jnp.sum(st3[...], axis=0)[:, :LANGS]

    weights, new_targets = vaccinate(gram, tgt_ref[...], acc_ref[...])
    nt_out[...] = new_targets
    wv[...] = jnp.broadcast_to(weights, (LANGS, 256))

    @pl.loop(0, 8)
    def _(r):
        rows = pl.ds(pl.multiple_of(r * 32, 32), 32)
        total = jnp.zeros((32, 256), jnp.float32)
        for l in range(LANGS):
            total = total + wv[l : l + 1, :] * inbox[l, rows, :].astype(jnp.float32)
        comb[rows, :] = total

    up_out[...] = comb[:, :DS].T
    dn_out[...] = comb[:, DS:]

    for copy in sends:
        copy.wait_send()

    @pl.loop(0, LANGS - 1)
    def _(k):
        grad_copy(k, z).wait_send()


def on_device(tokens, cotangent, lengths, up_weight, down_weight, targets, accept):
    bf16, f32 = jnp.bfloat16, jnp.float32
    dma = pltpu.SemaphoreType.DMA
    any_space = pl.BlockSpec(memory_space=pl.ANY)
    vmem = pl.BlockSpec(memory_space=pltpu.VMEM)
    return pl.pallas_call(
        kernel,
        out_shape=(
            jax.ShapeDtypeStruct((DS, HID), f32),
            jax.ShapeDtypeStruct((HID, DS), f32),
            jax.ShapeDtypeStruct((LANGS, LANGS), f32),
        ),
        in_specs=[
            any_space, any_space, pl.BlockSpec(memory_space=pltpu.SMEM), any_space, any_space, vmem, vmem,
        ],
        out_specs=(vmem, vmem, vmem),
        scratch_shapes=[
            pltpu.VMEM((LTOK, D), bf16),
            pltpu.VMEM((LTOK, D), bf16),
            pltpu.VMEM((D, HID), bf16),
            pltpu.VMEM((HID, D), bf16),
            pltpu.VMEM((D, HID), bf16),
            pltpu.VMEM((HID, LTOK), bf16),
            pltpu.VMEM((HID, LTOK), bf16),
            pltpu.VMEM((LANGS - 1, HID, 2 * DS), bf16),
            pltpu.VMEM((LANGS, HID, 2 * DS), bf16),
            pltpu.VMEM((256, 256), f32),
            pltpu.VMEM((NF, LANGS, 128), f32),
            pltpu.VMEM((NY, LANGS, 128), f32),
            pltpu.VMEM((LANGS, LANGS, 128), f32),
            pltpu.VMEM((LANGS, 256), f32),
            pltpu.VMEM((HID, 2 * DS), f32),
            dma((4,)),
            dma((20,)), dma((32,)), dma((16,)), dma((16,)),
            dma((20,)), dma((32,)), dma((16,)), dma((16,)),
            dma((LANGS - 1,)), dma((LANGS - 1,)),
            dma((NF,)), dma((NF,)), dma((NY,)), dma((NY,)), dma((LANGS,)), dma((LANGS,)),
        ],
        compiler_params=pltpu.CompilerParams(
            collective_id=0, has_side_effects=True, vmem_limit_bytes=48 * 1024 * 1024
        ),
        cost_estimate=pl.CostEstimate(
            flops=4 * 2 * LTOK * D * HID, bytes_accessed=4 * 1024 * 1024, transcendentals=LTOK * HID
        ),
        name="vaccine_step",
    )(tokens, cotangent, lengths, up_weight, down_weight, targets, accept)


def solution(mesh):
    in_specs = (
        P("lang", ("dp", "fsdp"), None),
        P("lang", ("dp", "fsdp"), None),
        P("lang", None),
        P(None, ("dp", "fsdp")),
        P(("dp", "fsdp"), None),
        P(),
        P(),
    )
    out_specs = (P("lang", ("dp", "fsdp")), P(("dp", "fsdp"), "lang"), P())
    return jax.shard_map(
        on_device, mesh=mesh, in_specs=in_specs, out_specs=out_specs, check_vma=False
    )
```

```python
import functools

import jax
import jax.numpy as jnp
from jax import lax
from jax.experimental import pallas as pl
from jax.experimental.pallas import tpu as pltpu
from jax.sharding import PartitionSpec as P

D = 2048
FF = 8192
SEQ = 128
LTOK = 1536
LANGS = 16
NY = 4
NX = 4
NF = 8
ROWS = 48
HID = 256
DS = 128
HALF = D // 2

ema_rate = 0.01
clip_level = 0.25
MESH = pl.DeviceIdType.MESH

OFFSETS = (0, 3, 1, 2)
ARRIVALS = (
    (0, 1), (0, 2), (1, 0), (2, 0), (0, 3), (1, 1), (2, 1), (1, 2), (2, 2),
    (1, 3), (2, 3), (3, 0), (3, 1), (3, 2), (3, 3),
)
EARLY = 4


class Plane:
    def __init__(self, x, y, core):
        self.x, self.y, self.core = x, y, core
        self.next = {}
        for ring in (0, 1):
            for step in (1, 3):
                dx = jnp.where(core == ring, step, 0)
                self.next[ring, step] = {
                    "dp": lax.rem(y + step - dx, 4),
                    "fsdp": lax.rem(x + dx, 4) * 2 + core,
                }
        self.sibling = {"fsdp": x * 2 + (1 - core)}

    def first_token(self, which, second, first):
        core = self.core if which == 0 else 1 - self.core
        dx = jnp.where(core == 0, OFFSETS[first], OFFSETS[second])
        dy = OFFSETS[first] + OFFSETS[second] - dx
        return (lax.rem(self.y + dy, 4) * NF + lax.rem(self.x + dx, 4) * 2 + core) * ROWS


class Gather:
    def __init__(self, plane, own, buf, start, width, send, recv, sib_send, sib_recv):
        self.plane, self.own, self.buf, self.start, self.width = plane, own, buf, start, width
        self.send, self.recv, self.sib_send, self.sib_recv = send, recv, sib_send, sib_recv
        self.started = []

    def part(self, roles, half):
        if half is None:
            return self.buf.at[0, roles[0], roles[1], :, pl.ds(self.start, self.width)]
        width = self.width // 2
        return self.buf.at[0, roles[0], roles[1], :, pl.ds(self.start + half * width, width)]

    def copy(self, roles, half, ring, step, send_index, there):
        src = self.own if roles == (0, 0) else self.part(roles, half)
        copy = pltpu.make_async_remote_copy(
            src_ref=src,
            dst_ref=self.part(there, half),
            send_sem=self.send.at[send_index],
            recv_sem=self.recv.at[2 * (4 * there[0] + there[1]) + (half or 0)],
            device_id=self.plane.next[ring, step],
            device_id_type=MESH,
        )
        copy.start()
        self.started.append(copy)

    def sibling_copy(self, second):
        cols = pl.ds(self.start, self.width)
        return pltpu.make_async_remote_copy(
            src_ref=self.buf.at[0, second, :, :, cols],
            dst_ref=self.buf.at[1, second, :, :, cols],
            send_sem=self.sib_send.at[second],
            recv_sem=self.sib_recv.at[second],
            device_id=self.plane.sibling,
            device_id_type=MESH,
        )

    def to_sibling(self, second):
        copy = self.sibling_copy(second)
        copy.start()
        self.started.append(copy)

    def from_sibling(self, second):
        self.sibling_copy(second).wait_recv()

    def ready(self, roles):
        second, first = roles
        base = 4 + 4 * first
        if second == 0:
            if first == 0:
                self.copy(roles, None, 0, 1, 0, (0, 1))
                self.copy(roles, None, 0, 3, 1, (0, 2))
            elif first == 1:
                self.copy(roles, 0, 0, 1, 2, (0, 3))
            elif first == 2:
                self.copy(roles, 1, 0, 3, 3, (0, 3))
            self.copy(roles, None, 1, 1, base, (1, first))
            self.copy(roles, None, 1, 3, base + 1, (2, first))
        elif second == 1:
            self.copy(roles, 0, 1, 1, base + 2, (3, first))
        elif second == 2:
            self.copy(roles, 1, 1, 3, base + 3, (3, first))

    def arrive(self, roles):
        for half in (0, 1) if roles[0] == 3 or roles == (0, 3) else (None,):
            ref = self.part(roles, half)
            pltpu.make_async_remote_copy(
                src_ref=ref,
                dst_ref=ref,
                send_sem=self.send.at[0],
                recv_sem=self.recv.at[2 * (4 * roles[0] + roles[1]) + (half or 0)],
                device_id=self.plane.next[0, 1],
                device_id_type=MESH,
            ).wait_recv()

    def step(self, roles):
        self.arrive(roles)
        self.ready(roles)
        if roles in ((0, 3), (1, 3), (2, 3), (3, 3)):
            self.to_sibling(roles[0])


def distance_of(k):
    m = 8 - (k + 1) // 2
    return jnp.where(lax.rem(k, 2) == 1, m, LANGS - m)


def exchange(buf, axis, count, me, send, recv):
    copies = []
    for r in range(1, count):
        copy = pltpu.make_async_remote_copy(
            src_ref=buf.at[me],
            dst_ref=buf.at[me],
            send_sem=send.at[r],
            recv_sem=recv.at[r],
            device_id={axis: lax.rem(me + r, count)},
            device_id_type=MESH,
        )
        copy.start()
        copies.append(copy)
    for r in range(1, count):
        ref = buf.at[lax.rem(me + count - r, count)]
        pltpu.make_async_remote_copy(
            src_ref=ref,
            dst_ref=ref,
            send_sem=send.at[r],
            recv_sem=recv.at[r],
            device_id={axis: lax.rem(me + r, count)},
            device_id_type=MESH,
        ).wait_recv()
    return copies


def vaccinate(gram, targets, accept):
    rows = lax.broadcasted_iota(jnp.int32, (LANGS, LANGS), 0)
    cols = lax.broadcasted_iota(jnp.int32, (LANGS, LANGS), 1)
    identity = (rows == cols).astype(jnp.float32)
    allowed = accept.astype(jnp.float32) * (1.0 - identity)
    diag_col = jnp.sum(gram * identity, axis=1, keepdims=True)
    diag_row = jnp.sum(gram * identity, axis=0, keepdims=True)
    cos_pairs = gram / jnp.sqrt(diag_col * diag_row)
    roots = jnp.sqrt(1.0 - targets * targets)
    coeffs, product = identity, gram
    for j in range(LANGS):
        inner = product[:, j : j + 1]
        norm_sq = jnp.sum(product * coeffs, axis=1, keepdims=True)
        own = gram[j : j + 1, j : j + 1]
        cosine = inner / jnp.sqrt(norm_sq * own)
        root = roots[:, j : j + 1]
        sine = jnp.sqrt(jnp.maximum(1.0 - cosine * cosine, 0.0))
        step = (
            jnp.sqrt(norm_sq) * (targets[:, j : j + 1] * sine - cosine * root) / (jnp.sqrt(own) * root)
        )
        step = jnp.where(allowed[:, j : j + 1] > 0.5, step, 0.0)
        coeffs = coeffs + step * identity[j : j + 1, :]
        product = product + step * gram[j : j + 1, :]
    weights_row = jnp.sum(coeffs, axis=0, keepdims=True)
    weights_col = jnp.sum(identity * weights_row, axis=1, keepdims=True)
    quad = jnp.sum(weights_col * gram * weights_row, axis=(0, 1), keepdims=True)
    mean_square = jnp.maximum(quad, 0.0) / (2.0 * D * FF)
    factor = jnp.minimum(1.0, clip_level / jnp.sqrt(mean_square + 1e-06))
    new_targets = (1.0 - ema_rate) * targets + ema_rate * cos_pairs
    return weights_col * factor, new_targets


def kernel(
    tok_ref, cot_ref, len_hbm, wup_hbm, wdn_hbm, tgt_hbm, acc_hbm,
    up_out, dn_out, nt_out,
    x_buf, c_buf, wup, wdn, wdn_t, tgt, acc, lens, v_buf, hp, h_t, p_t,
    out_dn, out_up, in_dn, in_up, pairs, st1, st2, st3, wv, comb,
    local_sem, cols_sem,
    t_send, t_recv, t_sib_send, t_sib_recv,
    e_send, e_recv, e_sib_send, e_sib_recv,
    l_send, l_recv, l_sib_send, l_sib_recv,
    d_send, d_recv, u_send, u_recv, s1_send, s1_recv, s2_send, s2_recv, s3_send, s3_recv,
):
    z, y, f = lax.axis_index("lang"), lax.axis_index("dp"), lax.axis_index("fsdp")
    x, core = f // 2, lax.rem(f, 2)

    barrier = pltpu.get_barrier_semaphore()
    for axis, count, me in (("fsdp", NF, f), ("dp", NY, y), ("lang", LANGS, z)):
        for r in range(1, count):
            pl.semaphore_signal(
                barrier, inc=1, device_id={axis: lax.rem(me + r, count)}, device_id_type=MESH
            )

    def owner(k):
        return lax.rem(z + (distance_of(k) if not isinstance(k, int) or k < 15 else 0), LANGS)

    def columns(block):
        return pl.ds(pl.multiple_of(block * DS, DS), DS)

    plane = Plane(x, y, core)
    tok, cot = tok_ref.at[0], cot_ref.at[0]
    cot_copies = [
        pltpu.make_async_copy(
            cot.at[:, columns(owner(k))], c_buf.at[0, 0, 0, :, pl.ds(k * DS, DS)], cols_sem.at[k]
        )
        for k in range(LANGS)
    ]
    local = [
        pltpu.make_async_copy(tok, x_buf.at[0, 0, 0], local_sem.at[0]),
        pltpu.make_async_copy(wdn_hbm, wdn, local_sem.at[1]),
        pltpu.make_async_copy(wup_hbm, wup, local_sem.at[2]),
        pltpu.make_async_copy(tgt_hbm, tgt, local_sem.at[3]),
        pltpu.make_async_copy(acc_hbm, acc, local_sem.at[4]),
        pltpu.make_async_copy(len_hbm, lens, local_sem.at[5]),
    ]
    for copy in cot_copies + local:
        copy.start()

    early = EARLY * DS
    tokens = Gather(plane, tok, x_buf, 0, D, t_send, t_recv, t_sib_send, t_sib_recv)
    first = Gather(
        plane, c_buf.at[0, 0, 0, :, pl.ds(0, early)], c_buf, 0, early,
        e_send, e_recv, e_sib_send, e_sib_recv,
    )
    rest = Gather(
        plane, c_buf.at[0, 0, 0, :, pl.ds(early, D - early)], c_buf, early, D - early,
        l_send, l_recv, l_sib_send, l_sib_recv,
    )

    pl.semaphore_wait(barrier, (NF - 1) + (NY - 1) + (LANGS - 1))
    tokens.ready((0, 0))
    for copy in cot_copies:
        copy.wait()
    first.ready((0, 0))
    for copy in local:
        copy.wait()

    for k in range(LANGS):
        wdn_t[pl.ds(k * DS, DS), :] = wdn[:, columns(owner(k))].T

    def activate(which, second):
        base = (which * 4 + second) * 192
        v_buf[pl.ds(base, 192), :] = jnp.dot(
            x_buf[which, second].reshape(192, D), wup[...], preferred_element_type=jnp.float32
        )
        for i in range(4):
            token = plane.first_token(which, second, i)
            slot = token // SEQ
            offset = token - slot * SEQ
            here, after = lens[0, slot], lens[0, jnp.minimum(slot + 1, 11)]
            place = lax.broadcasted_iota(jnp.int32, (ROWS, HID), 0) + offset
            keep = place < jnp.where(place < SEQ, here, after + SEQ)
            rows = pl.ds(base + i * ROWS, ROWS)
            v = v_buf[rows, :]
            k = 0.7978845608028654
            sq = v * v
            t = jnp.tanh(k * (v + 0.044715 * (sq * v)))
            cdf = 0.5 * (1.0 + t)
            slope = cdf + 0.5 * v * (1.0 - t * t) * (k * (1.0 + 3.0 * 0.044715 * sq))
            hp[rows, :] = jnp.where(keep, v * cdf, 0.0).astype(jnp.bfloat16)
            v_buf[rows, :] = jnp.where(keep, slope, 0.0)

    def turn(dst, start, count):
        for i in range(start, start + count):
            dst[:, pl.ds(i * 128, 128)] = hp[pl.ds(i * 128, 128), :].T

    for n, roles in enumerate(ARRIVALS):
        tokens.step(roles)
        first.step(roles)
        if roles == (2, 1):
            tokens.from_sibling(0)
            activate(0, 0)
            rest.ready((0, 0))
        elif roles == (2, 2):
            activate(1, 0)
        elif roles == (2, 3):
            activate(0, 1)
        elif roles == (3, 0):
            tokens.from_sibling(1)
            activate(1, 1)
        elif roles == (3, 1):
            activate(0, 2)
        elif roles == (3, 2):
            tokens.from_sibling(2)
            activate(1, 2)
    turn(h_t, 0, 3)
    turn(h_t, 6, 3)
    activate(0, 3)
    tokens.from_sibling(3)
    activate(1, 3)
    turn(h_t, 3, 3)
    turn(h_t, 9, 3)
    for second in range(4):
        first.from_sibling(second)

    def down(k):
        return jnp.dot(
            h_t[...],
            c_buf[:, :, :, :, columns(k)].reshape(LTOK, DS),
            preferred_element_type=jnp.float32,
        ).astype(jnp.bfloat16)

    def grad_copy(out, inbox, k, block, send, recv):
        return pltpu.make_async_remote_copy(
            src_ref=out.at[k],
            dst_ref=inbox.at[block],
            send_sem=send.at[k],
            recv_sem=recv.at[k],
            device_id={"lang": owner(k)},
            device_id_type=MESH,
        )

    @pl.loop(0, EARLY)
    def _(k):
        out_dn[k] = down(k)
        grad_copy(out_dn, in_dn, k, z, d_send, d_recv).start()

    for roles in ARRIVALS:
        rest.step(roles)
    for second in range(4):
        rest.from_sibling(second)

    @pl.loop(EARLY, LANGS - 1)
    def _(k):
        out_dn[k] = down(k)
        grad_copy(out_dn, in_dn, k, z, d_send, d_recv).start()

    in_dn[z] = down(LANGS - 1)

    for group in range(8):
        hg = jnp.dot(
            c_buf[group // 4, group % 4].reshape(192, D), wdn_t[...], preferred_element_type=jnp.float32
        )
        rows = pl.ds(group * 192, 192)
        hp[rows, :] = (hg * v_buf[rows, :]).astype(jnp.bfloat16)
    turn(p_t, 0, 12)

    def up(block):
        return jnp.dot(
            p_t[...],
            x_buf[:, :, :, :, columns(block)].reshape(LTOK, DS),
            preferred_element_type=jnp.float32,
        ).astype(jnp.bfloat16)

    @pl.loop(0, LANGS - 1)
    def _(k):
        out_up[k] = up(owner(k))
        grad_copy(out_up, in_up, k, z, u_send, u_recv).start()

    in_up[z] = up(z)

    for copy in tokens.started + first.started + rest.started:
        copy.wait_send()

    pairs[...] = jnp.zeros_like(pairs)

    for inbox, out, send, recv in ((in_dn, out_dn, d_send, d_recv), (in_up, out_up, u_send, u_recv)):

        @pl.loop(0, LANGS - 1)
        def _(k):
            source = lax.rem(z + LANGS - distance_of(k), LANGS)
            grad_copy(out, inbox, k, source, send, recv).wait_recv()

        @pl.loop(0, 2)
        def _(g):
            a = jnp.concatenate(
                [
                    inbox[:, pl.ds(pl.multiple_of(g * 128 + i * 16, 16), 16), :].reshape(256, DS)
                    for i in range(8)
                ],
                axis=1,
            )
            pairs[...] += lax.dot_general(
                a, a, (((1,), (1,)), ((), ())), preferred_element_type=jnp.float32
            )

    ri = lax.broadcasted_iota(jnp.int32, (256, 256), 0)
    ci = lax.broadcasted_iota(jnp.int32, (256, 256), 1)
    same = jnp.where(lax.rem(ri, 16) == lax.rem(ci, 16), pairs[...], 0.0)
    by_row = jnp.sum(same.reshape(LANGS, 16, 256), axis=1)
    li = lax.broadcasted_iota(jnp.int32, (256, 128), 0) // 16
    lj = lax.broadcasted_iota(jnp.int32, (256, 128), 1)
    select = (li == lj).astype(jnp.float32)
    st1[f] = jnp.dot(
        by_row, select, precision=lax.Precision.HIGHEST, preferred_element_type=jnp.float32
    )
    sends = exchange(st1, "fsdp", NF, f, s1_send, s1_recv)
    st2[y] = jnp.sum(st1[...], axis=0)
    sends += exchange(st2, "dp", NY, y, s2_send, s2_recv)
    st3[z] = jnp.sum(st2[...], axis=0)
    sends += exchange(st3, "lang", LANGS, z, s3_send, s3_recv)
    gram = jnp.sum(st3[...], axis=0)[:, :LANGS]

    weights, new_targets = vaccinate(gram, tgt[...], acc[...])
    nt_out[...] = new_targets
    wv[...] = jnp.broadcast_to(weights, (LANGS, DS))

    for inbox, half in ((in_up, 0), (in_dn, 1)):

        @pl.loop(0, 4)
        def _(r):
            rows = pl.ds(pl.multiple_of(r * 64, 64), 64)
            total = jnp.zeros((64, DS), jnp.float32)
            for l in range(LANGS):
                total = total + wv[l : l + 1, :] * inbox[l, rows, :].astype(jnp.float32)
            if half == 0:
                comb[rows, :] = total
            else:
                dn_out[rows, :] = total

    up_out[...] = comb[...].T

    for copy in sends:
        copy.wait_send()

    @pl.loop(0, LANGS - 1)
    def _(k):
        grad_copy(out_dn, in_dn, k, z, d_send, d_recv).wait_send()
        grad_copy(out_up, in_up, k, z, u_send, u_recv).wait_send()


def on_device(tokens, cotangent, lengths, up_weight, down_weight, targets, accept):
    bf16, f32 = jnp.bfloat16, jnp.float32
    dma = pltpu.SemaphoreType.DMA
    any_space = pl.BlockSpec(memory_space=pl.ANY)
    vmem = pl.BlockSpec(memory_space=pltpu.VMEM)
    return pl.pallas_call(
        kernel,
        out_shape=(
            jax.ShapeDtypeStruct((DS, HID), f32),
            jax.ShapeDtypeStruct((HID, DS), f32),
            jax.ShapeDtypeStruct((LANGS, LANGS), f32),
        ),
        in_specs=[any_space] * 7,
        out_specs=(vmem, vmem, vmem),
        scratch_shapes=[
            pltpu.VMEM((2, 4, 4, ROWS, D), bf16),
            pltpu.VMEM((2, 4, 4, ROWS, D), bf16),
            pltpu.VMEM((D, HID), bf16),
            pltpu.VMEM((HID, D), bf16),
            pltpu.VMEM((D, HID), bf16),
            pltpu.VMEM((LANGS, LANGS), f32),
            pltpu.VMEM((LANGS, LANGS), jnp.int32),
            pltpu.SMEM((1, 12), jnp.int32),
            pltpu.VMEM((LTOK, HID), f32),
            pltpu.VMEM((LTOK, HID), bf16),
            pltpu.VMEM((HID, LTOK), bf16),
            pltpu.VMEM((HID, LTOK), bf16),
            pltpu.VMEM((LANGS - 1, HID, DS), bf16),
            pltpu.VMEM((LANGS - 1, HID, DS), bf16),
            pltpu.VMEM((LANGS, HID, DS), bf16),
            pltpu.VMEM((LANGS, HID, DS), bf16),
            pltpu.VMEM((256, 256), f32),
            pltpu.VMEM((NF, LANGS, 128), f32),
            pltpu.VMEM((NY, LANGS, 128), f32),
            pltpu.VMEM((LANGS, LANGS, 128), f32),
            pltpu.VMEM((LANGS, DS), f32),
            pltpu.VMEM((HID, DS), f32),
            dma((6,)), dma((LANGS,)),
            dma((20,)), dma((32,)), dma((4,)), dma((4,)),
            dma((20,)), dma((32,)), dma((4,)), dma((4,)),
            dma((20,)), dma((32,)), dma((4,)), dma((4,)),
            dma((LANGS - 1,)), dma((LANGS - 1,)), dma((LANGS - 1,)), dma((LANGS - 1,)),
            dma((NF,)), dma((NF,)), dma((NY,)), dma((NY,)), dma((LANGS,)), dma((LANGS,)),
        ],
        compiler_params=pltpu.CompilerParams(
            collective_id=0, has_side_effects=True, vmem_limit_bytes=60 * 1024 * 1024
        ),
        cost_estimate=pl.CostEstimate(
            flops=4 * 2 * LTOK * D * HID, bytes_accessed=4 * 1024 * 1024, transcendentals=LTOK * HID
        ),
        name="vaccine_step",
    )(tokens, cotangent, lengths, up_weight, down_weight, targets, accept)


def solution(mesh):
    in_specs = (
        P("lang", ("dp", "fsdp"), None),
        P("lang", ("dp", "fsdp"), None),
        P("lang", None),
        P(None, ("dp", "fsdp")),
        P(("dp", "fsdp"), None),
        P(),
        P(),
    )
    out_specs = (P("lang", ("dp", "fsdp")), P(("dp", "fsdp"), "lang"), P())
    return jax.shard_map(
        on_device, mesh=mesh, in_specs=in_specs, out_specs=out_specs, check_vma=False
    )
```

```python
import functools

import jax
import jax.numpy as jnp
from jax import lax
from jax.experimental import pallas as pl
from jax.experimental.pallas import tpu as pltpu
from jax.sharding import PartitionSpec as P

D = 2048
FF = 8192
SEQ = 128
LTOK = 1536
LANGS = 16
NY = 4
NX = 4
NF = 8
ROWS = 48
HID = 256
DS = 128
HALF = D // 2

ema_rate = 0.01
clip_level = 0.25
MESH = pl.DeviceIdType.MESH

OFFSETS = (0, 3, 1, 2)
ARRIVALS = (
    (0, 1), (0, 2), (1, 0), (2, 0), (0, 3), (1, 1), (2, 1), (1, 2), (2, 2),
    (1, 3), (2, 3), (3, 0), (3, 1), (3, 2), (3, 3),
)
EARLY = 4


class Plane:
    def __init__(self, x, y, core):
        self.x, self.y, self.core = x, y, core
        self.next = {}
        for ring in (0, 1):
            for step in (1, 3):
                dx = jnp.where(core == ring, step, 0)
                self.next[ring, step] = {
                    "dp": lax.rem(y + step - dx, 4),
                    "fsdp": lax.rem(x + dx, 4) * 2 + core,
                }
        self.sibling = {"fsdp": x * 2 + (1 - core)}

    def first_token(self, which, second, first):
        core = self.core if which == 0 else 1 - self.core
        dx = jnp.where(core == 0, OFFSETS[first], OFFSETS[second])
        dy = OFFSETS[first] + OFFSETS[second] - dx
        return (lax.rem(self.y + dy, 4) * NF + lax.rem(self.x + dx, 4) * 2 + core) * ROWS


class Gather:
    def __init__(self, plane, own, buf, start, width, send, recv, sib_send, sib_recv):
        self.plane, self.own, self.buf, self.start, self.width = plane, own, buf, start, width
        self.send, self.recv, self.sib_send, self.sib_recv = send, recv, sib_send, sib_recv
        self.started = []

    def part(self, roles, half):
        if half is None:
            return self.buf.at[0, roles[0], roles[1], :, pl.ds(self.start, self.width)]
        width = self.width // 2
        return self.buf.at[0, roles[0], roles[1], :, pl.ds(self.start + half * width, width)]

    def copy(self, roles, half, ring, step, send_index, there):
        src = self.own if roles == (0, 0) else self.part(roles, half)
        copy = pltpu.make_async_remote_copy(
            src_ref=src,
            dst_ref=self.part(there, half),
            send_sem=self.send.at[send_index],
            recv_sem=self.recv.at[2 * (4 * there[0] + there[1]) + (half or 0)],
            device_id=self.plane.next[ring, step],
            device_id_type=MESH,
        )
        copy.start()
        self.started.append(copy)

    def sibling_copy(self, second):
        cols = pl.ds(self.start, self.width)
        return pltpu.make_async_remote_copy(
            src_ref=self.buf.at[0, second, :, :, cols],
            dst_ref=self.buf.at[1, second, :, :, cols],
            send_sem=self.sib_send.at[second],
            recv_sem=self.sib_recv.at[second],
            device_id=self.plane.sibling,
            device_id_type=MESH,
        )

    def to_sibling(self, second):
        copy = self.sibling_copy(second)
        copy.start()
        self.started.append(copy)

    def from_sibling(self, second):
        self.sibling_copy(second).wait_recv()

    def ready(self, roles):
        second, first = roles
        base = 4 + 4 * first
        if second == 0:
            if first == 0:
                self.copy(roles, None, 0, 1, 0, (0, 1))
                self.copy(roles, None, 0, 3, 1, (0, 2))
            elif first == 1:
                self.copy(roles, 0, 0, 1, 2, (0, 3))
            elif first == 2:
                self.copy(roles, 1, 0, 3, 3, (0, 3))
            self.copy(roles, None, 1, 1, base, (1, first))
            self.copy(roles, None, 1, 3, base + 1, (2, first))
        elif second == 1:
            self.copy(roles, 0, 1, 1, base + 2, (3, first))
        elif second == 2:
            self.copy(roles, 1, 1, 3, base + 3, (3, first))

    def arrive(self, roles):
        for half in (0, 1) if roles[0] == 3 or roles == (0, 3) else (None,):
            ref = self.part(roles, half)
            pltpu.make_async_remote_copy(
                src_ref=ref,
                dst_ref=ref,
                send_sem=self.send.at[0],
                recv_sem=self.recv.at[2 * (4 * roles[0] + roles[1]) + (half or 0)],
                device_id=self.plane.next[0, 1],
                device_id_type=MESH,
            ).wait_recv()

    def step(self, roles):
        self.arrive(roles)
        self.ready(roles)
        if roles in ((0, 3), (1, 3), (2, 3), (3, 3)):
            self.to_sibling(roles[0])


def distance_of(k, sign):
    m = 8 - (k + 1) // 2
    return jnp.where(lax.rem(k, 2) == sign, LANGS - m, m)


def exchange(buf, axis, count, me, send, recv):
    copies = []
    for r in range(1, count):
        copy = pltpu.make_async_remote_copy(
            src_ref=buf.at[me],
            dst_ref=buf.at[me],
            send_sem=send.at[r],
            recv_sem=recv.at[r],
            device_id={axis: lax.rem(me + r, count)},
            device_id_type=MESH,
        )
        copy.start()
        copies.append(copy)
    for r in range(1, count):
        ref = buf.at[lax.rem(me + count - r, count)]
        pltpu.make_async_remote_copy(
            src_ref=ref,
            dst_ref=ref,
            send_sem=send.at[r],
            recv_sem=recv.at[r],
            device_id={axis: lax.rem(me + r, count)},
            device_id_type=MESH,
        ).wait_recv()
    return copies


def vaccinate(gram, targets_t, accept_t):
    rows = lax.broadcasted_iota(jnp.int32, (LANGS, LANGS), 0)
    cols = lax.broadcasted_iota(jnp.int32, (LANGS, LANGS), 1)
    identity = (rows == cols).astype(jnp.float32)
    roots = jnp.sqrt(1.0 - targets_t * targets_t)
    diag_col = jnp.sum(gram * identity, axis=1, keepdims=True)
    diag_row = jnp.sum(gram * identity, axis=0, keepdims=True)
    cos_pairs = gram / jnp.sqrt(diag_col * diag_row)
    inverse = 1.0 / jnp.sqrt(diag_col)
    scale = inverse / roots
    allowed = accept_t.astype(jnp.float32) * (1.0 - identity)
    coeffs, product = identity, gram
    for j in range(LANGS):
        norm_sq = jnp.sum(product * coeffs, axis=0, keepdims=True)
        over_norm = lax.rsqrt(norm_sq)
        cosine = product[j : j + 1, :] * inverse[j : j + 1, :] * over_norm
        sine = jnp.sqrt(jnp.maximum(1.0 - cosine * cosine, 0.0))
        step = (
            (norm_sq * over_norm)
            * (targets_t[j : j + 1, :] * sine - cosine * roots[j : j + 1, :])
            * scale[j : j + 1, :]
        )
        step = jnp.where(allowed[j : j + 1, :] > 0.5, step, 0.0)
        coeffs = jnp.where(rows == j, coeffs + step, coeffs)
        product = product + gram[:, j : j + 1] * step
    weights = jnp.sum(coeffs, axis=1, keepdims=True)
    along = jnp.sum(product, axis=1, keepdims=True)
    quad = jnp.sum(weights * along, axis=0, keepdims=True)
    mean_square = jnp.maximum(quad, 0.0) / (2.0 * D * FF)
    factor = jnp.minimum(1.0, clip_level / jnp.sqrt(mean_square + 1e-06))
    return weights * factor, cos_pairs


def kernel(
    tok_ref, cot_ref, len_hbm, wup_hbm, wdn_hbm, tgt_hbm, acc_hbm,
    up_out, dn_out, nt_out,
    x_buf, c_buf, wup, wdn, wdn_t, tgt, acc, lens, v_buf, hp, h_t, p_t,
    out_dn, out_up, in_dn, in_up, relay, pairs, st1, st2, st3, wv, comb,
    local_sem, cols_sem,
    t_send, t_recv, t_sib_send, t_sib_recv,
    e_send, e_recv, e_sib_send, e_sib_recv,
    l_send, l_recv, l_sib_send, l_sib_recv,
    d_send, d_recv, u_send, u_recv, r_send, r_recv, s1_send, s1_recv, s2_send, s2_recv, s3_send, s3_recv,
):
    z, y, f = lax.axis_index("lang"), lax.axis_index("dp"), lax.axis_index("fsdp")
    x, core = f // 2, lax.rem(f, 2)

    barrier = pltpu.get_barrier_semaphore()
    for axis, count, me in (("fsdp", NF, f), ("dp", NY, y), ("lang", LANGS, z)):
        for r in range(1, count):
            pl.semaphore_signal(
                barrier, inc=1, device_id={axis: lax.rem(me + r, count)}, device_id_type=MESH
            )

    def owner(k, sign):
        return lax.rem(z + (distance_of(k, sign) if not isinstance(k, int) or k < 15 else 0), LANGS)

    def columns(block):
        return pl.ds(pl.multiple_of(block * DS, DS), DS)

    plane = Plane(x, y, core)
    tok, cot = tok_ref.at[0], cot_ref.at[0]
    cot_copies = [
        pltpu.make_async_copy(
            cot.at[:, columns(owner(k, 1))], c_buf.at[0, 0, 0, :, pl.ds(k * DS, DS)], cols_sem.at[k]
        )
        for k in range(LANGS)
    ]
    local = [
        pltpu.make_async_copy(tok, x_buf.at[0, 0, 0], local_sem.at[0]),
        pltpu.make_async_copy(wdn_hbm, wdn, local_sem.at[1]),
        pltpu.make_async_copy(wup_hbm, wup, local_sem.at[2]),
        pltpu.make_async_copy(tgt_hbm, tgt, local_sem.at[3]),
        pltpu.make_async_copy(acc_hbm, acc, local_sem.at[4]),
        pltpu.make_async_copy(len_hbm, lens, local_sem.at[5]),
    ]
    for copy in cot_copies + local:
        copy.start()

    early = EARLY * DS
    tokens = Gather(plane, tok, x_buf, 0, D, t_send, t_recv, t_sib_send, t_sib_recv)
    first = Gather(
        plane, c_buf.at[0, 0, 0, :, pl.ds(0, early)], c_buf, 0, early,
        e_send, e_recv, e_sib_send, e_sib_recv,
    )
    rest = Gather(
        plane, c_buf.at[0, 0, 0, :, pl.ds(early, D - early)], c_buf, early, D - early,
        l_send, l_recv, l_sib_send, l_sib_recv,
    )

    pl.semaphore_wait(barrier, (NF - 1) + (NY - 1) + (LANGS - 1))
    tokens.ready((0, 0))
    for copy in cot_copies:
        copy.wait()
    first.ready((0, 0))
    for copy in local:
        copy.wait()

    for k in range(LANGS):
        wdn_t[pl.ds(k * DS, DS), :] = wdn[:, columns(owner(k, 1))].T

    def activate(which, second):
        base = (which * 4 + second) * 192
        v_buf[pl.ds(base, 192), :] = jnp.dot(
            x_buf[which, second].reshape(192, D), wup[...], preferred_element_type=jnp.float32
        )
        for i in range(4):
            token = plane.first_token(which, second, i)
            slot = token // SEQ
            offset = token - slot * SEQ
            here, after = lens[0, slot], lens[0, jnp.minimum(slot + 1, 11)]
            place = lax.broadcasted_iota(jnp.int32, (ROWS, HID), 0) + offset
            keep = place < jnp.where(place < SEQ, here, after + SEQ)
            rows = pl.ds(base + i * ROWS, ROWS)
            v = v_buf[rows, :]
            k = 0.7978845608028654
            sq = v * v
            t = jnp.tanh(k * (v + 0.044715 * (sq * v)))
            cdf = 0.5 * (1.0 + t)
            slope = cdf + 0.5 * v * (1.0 - t * t) * (k * (1.0 + 3.0 * 0.044715 * sq))
            hp[rows, :] = jnp.where(keep, v * cdf, 0.0).astype(jnp.bfloat16)
            v_buf[rows, :] = jnp.where(keep, slope, 0.0)

    def turn(dst, start, count):
        for i in range(start, start + count):
            dst[:, pl.ds(i * 128, 128)] = hp[pl.ds(i * 128, 128), :].T

    for n, roles in enumerate(ARRIVALS):
        tokens.step(roles)
        first.step(roles)
        if roles == (2, 1):
            tokens.from_sibling(0)
            activate(0, 0)
            rest.ready((0, 0))
        elif roles == (2, 2):
            activate(1, 0)
        elif roles == (2, 3):
            activate(0, 1)
        elif roles == (3, 0):
            tokens.from_sibling(1)
            activate(1, 1)
        elif roles == (3, 1):
            activate(0, 2)
        elif roles == (3, 2):
            tokens.from_sibling(2)
            activate(1, 2)
    turn(h_t, 0, 3)
    turn(h_t, 6, 3)
    activate(0, 3)
    tokens.from_sibling(3)
    activate(1, 3)
    turn(h_t, 3, 3)
    turn(h_t, 9, 3)
    for second in range(4):
        first.from_sibling(second)

    def down(k):
        return jnp.dot(
            h_t[...],
            c_buf[:, :, :, :, columns(k)].reshape(LTOK, DS),
            preferred_element_type=jnp.float32,
        ).astype(jnp.bfloat16)

    def remote(src, dst, send, recv, to):
        return pltpu.make_async_remote_copy(
            src_ref=src, dst_ref=dst, send_sem=send, recv_sem=recv, device_id={"lang": to}, device_id_type=MESH
        )

    def grad_copy(sign, k, block):
        out, inbox = (out_dn, in_dn) if sign else (out_up, in_up)
        send, recv = (d_send, d_recv) if sign else (u_send, u_recv)
        return remote(out.at[k], inbox.at[block], send.at[k], recv.at[k], owner(k, sign))

    def to_relay(sign):
        out, send = (out_dn, d_send) if sign else (out_up, u_send)
        to = lax.rem(z + (4 if sign else 12), LANGS)
        return remote(out.at[0], relay.at[sign], send.at[0], r_recv.at[sign], to)

    def from_relay(sign):
        inbox, recv = (in_dn, d_recv) if sign else (in_up, u_recv)
        source, to = lax.rem(z + (12 if sign else 4), LANGS), lax.rem(z + (4 if sign else 12), LANGS)
        return remote(relay.at[sign], inbox.at[source], r_send.at[sign], recv.at[0], to)

    out_dn[0] = down(0)
    to_relay(1).start()

    @pl.loop(1, EARLY)
    def _(k):
        out_dn[k] = down(k)
        grad_copy(1, k, z).start()

    for roles in ARRIVALS:
        rest.step(roles)
    for second in range(4):
        rest.from_sibling(second)

    @pl.loop(EARLY, LANGS - 1)
    def _(k):
        out_dn[k] = down(k)
        grad_copy(1, k, z).start()

    in_dn[z] = down(LANGS - 1)

    for group in range(8):
        hg = jnp.dot(
            c_buf[group // 4, group % 4].reshape(192, D), wdn_t[...], preferred_element_type=jnp.float32
        )
        rows = pl.ds(group * 192, 192)
        hp[rows, :] = (hg * v_buf[rows, :]).astype(jnp.bfloat16)
    turn(p_t, 0, 12)

    def up(block):
        return jnp.dot(
            p_t[...],
            x_buf[:, :, :, :, columns(block)].reshape(LTOK, DS),
            preferred_element_type=jnp.float32,
        ).astype(jnp.bfloat16)

    to_relay(1).wait_recv()
    from_relay(1).start()
    out_up[0] = up(owner(0, 0))
    to_relay(0).start()

    @pl.loop(1, 7)
    def _(k):
        out_up[k] = up(owner(k, 0))
        grad_copy(0, k, z).start()

    in_up[z] = up(z)
    to_relay(0).wait_recv()
    from_relay(0).start()

    @pl.loop(7, LANGS - 1)
    def _(k):
        out_up[k] = up(owner(k, 0))
        grad_copy(0, k, z).start()

    for copy in tokens.started + first.started + rest.started:
        copy.wait_send()

    pairs[...] = jnp.zeros_like(pairs)
    targets_t = tgt[...].T
    accept_t = acc[...].T

    for sign, inbox in ((1, in_dn), (0, in_up)):

        @pl.loop(0, LANGS - 1)
        def _(k):
            grad_copy(sign, k, lax.rem(z + LANGS - distance_of(k, sign), LANGS)).wait_recv()

        @pl.loop(0, 2)
        def _(g):
            a = jnp.concatenate(
                [
                    inbox[:, pl.ds(pl.multiple_of(g * 128 + i * 16, 16), 16), :].reshape(256, DS)
                    for i in range(8)
                ],
                axis=1,
            )
            pairs[...] += lax.dot_general(
                a, a, (((1,), (1,)), ((), ())), preferred_element_type=jnp.float32
            )

    ri = lax.broadcasted_iota(jnp.int32, (256, 256), 0)
    ci = lax.broadcasted_iota(jnp.int32, (256, 256), 1)
    same = jnp.where(lax.rem(ri, 16) == lax.rem(ci, 16), pairs[...], 0.0)
    by_row = jnp.sum(same.reshape(LANGS, 16, 256), axis=1)
    li = lax.broadcasted_iota(jnp.int32, (256, 128), 0) // 16
    lj = lax.broadcasted_iota(jnp.int32, (256, 128), 1)
    select = (li == lj).astype(jnp.float32)
    st1[f] = jnp.dot(
        by_row, select, precision=lax.Precision.HIGHEST, preferred_element_type=jnp.float32
    )
    sends = exchange(st1, "fsdp", NF, f, s1_send, s1_recv)
    st2[y] = jnp.sum(st1[...], axis=0)
    sends += exchange(st2, "dp", NY, y, s2_send, s2_recv)
    st3[z] = jnp.sum(st2[...], axis=0)
    sends += exchange(st3, "lang", LANGS, z, s3_send, s3_recv)
    gram = jnp.sum(st3[...], axis=0)[:, :LANGS]

    weights, cos_pairs = vaccinate(gram, targets_t, accept_t)
    nt_out[...] = (1.0 - ema_rate) * tgt[...] + ema_rate * cos_pairs
    wv[...] = jnp.broadcast_to(weights, (LANGS, DS))

    for inbox, half in ((in_up, 0), (in_dn, 1)):

        @pl.loop(0, 4)
        def _(r):
            rows = pl.ds(pl.multiple_of(r * 64, 64), 64)
            total = jnp.zeros((64, DS), jnp.float32)
            for l in range(LANGS):
                total = total + wv[l : l + 1, :] * inbox[l, rows, :].astype(jnp.float32)
            if half == 0:
                comb[rows, :] = total
            else:
                dn_out[rows, :] = total

    up_out[...] = comb[...].T

    for copy in sends:
        copy.wait_send()

    @pl.loop(0, LANGS - 1)
    def _(k):
        grad_copy(1, k, z).wait_send()
        grad_copy(0, k, z).wait_send()

    from_relay(0).wait_send()
    from_relay(1).wait_send()


def on_device(tokens, cotangent, lengths, up_weight, down_weight, targets, accept):
    bf16, f32 = jnp.bfloat16, jnp.float32
    dma = pltpu.SemaphoreType.DMA
    hbm = pl.BlockSpec(memory_space=pl.ANY)
    vmem = pl.BlockSpec(memory_space=pltpu.VMEM)
    return pl.pallas_call(
        kernel,
        out_shape=(
            jax.ShapeDtypeStruct((DS, HID), f32),
            jax.ShapeDtypeStruct((HID, DS), f32),
            jax.ShapeDtypeStruct((LANGS, LANGS), f32),
        ),
        in_specs=[hbm] * 7,
        out_specs=(vmem, vmem, vmem),
        scratch_shapes=[
            pltpu.VMEM((2, 4, 4, ROWS, D), bf16),
            pltpu.VMEM((2, 4, 4, ROWS, D), bf16),
            pltpu.VMEM((D, HID), bf16),
            pltpu.VMEM((HID, D), bf16),
            pltpu.VMEM((D, HID), bf16),
            pltpu.VMEM((LANGS, LANGS), f32),
            pltpu.VMEM((LANGS, LANGS), jnp.int32),
            pltpu.SMEM((1, 12), jnp.int32),
            pltpu.VMEM((LTOK, HID), f32),
            pltpu.VMEM((LTOK, HID), bf16),
            pltpu.VMEM((HID, LTOK), bf16),
            pltpu.VMEM((HID, LTOK), bf16),
            pltpu.VMEM((LANGS - 1, HID, DS), bf16),
            pltpu.VMEM((LANGS - 1, HID, DS), bf16),
            pltpu.VMEM((LANGS, HID, DS), bf16),
            pltpu.VMEM((LANGS, HID, DS), bf16),
            pltpu.VMEM((2, HID, DS), bf16),
            pltpu.VMEM((256, 256), f32),
            pltpu.VMEM((NF, LANGS, 128), f32),
            pltpu.VMEM((NY, LANGS, 128), f32),
            pltpu.VMEM((LANGS, LANGS, 128), f32),
            pltpu.VMEM((LANGS, DS), f32),
            pltpu.VMEM((HID, DS), f32),
            dma((6,)), dma((LANGS,)),
            dma((20,)), dma((32,)), dma((4,)), dma((4,)),
            dma((20,)), dma((32,)), dma((4,)), dma((4,)),
            dma((20,)), dma((32,)), dma((4,)), dma((4,)),
            dma((LANGS - 1,)), dma((LANGS - 1,)), dma((LANGS - 1,)), dma((LANGS - 1,)),
            dma((2,)), dma((2,)),
            dma((NF,)), dma((NF,)), dma((NY,)), dma((NY,)), dma((LANGS,)), dma((LANGS,)),
        ],
        compiler_params=pltpu.CompilerParams(
            collective_id=0, has_side_effects=True, vmem_limit_bytes=60 * 1024 * 1024
        ),
        cost_estimate=pl.CostEstimate(
            flops=4 * 2 * LTOK * D * HID, bytes_accessed=4 * 1024 * 1024, transcendentals=LTOK * HID
        ),
        name="vaccine_step",
    )(tokens, cotangent, lengths, up_weight, down_weight, targets, accept)


def solution(mesh):
    in_specs = (
        P("lang", ("dp", "fsdp"), None),
        P("lang", ("dp", "fsdp"), None),
        P("lang", None),
        P(None, ("dp", "fsdp")),
        P(("dp", "fsdp"), None),
        P(),
        P(),
    )
    out_specs = (P("lang", ("dp", "fsdp")), P(("dp", "fsdp"), "lang"), P())
    return jax.shard_map(
        on_device, mesh=mesh, in_specs=in_specs, out_specs=out_specs, check_vma=False
    )
```

```python
import functools

import jax
import jax.numpy as jnp
from jax import lax
from jax.experimental import pallas as pl
from jax.experimental.pallas import tpu as pltpu
from jax.sharding import PartitionSpec as P

D = 2048
FF = 8192
SEQ = 128
LTOK = 1536
LANGS = 16
NY = 4
NX = 4
NF = 8
ROWS = 48
HID = 256
DS = 128
HALF = D // 2

ema_rate = 0.01
clip_level = 0.25
MESH = pl.DeviceIdType.MESH

OFFSETS = (0, 3, 1, 2)
ARRIVALS = (
    (0, 1), (0, 2), (1, 0), (2, 0), (0, 3), (1, 1), (2, 1), (1, 2), (2, 2),
    (1, 3), (2, 3), (3, 0), (3, 1), (3, 2), (3, 3),
)
EARLY = 4


class Plane:
    def __init__(self, x, y, core):
        self.x, self.y, self.core = x, y, core
        self.next = {}
        for ring in (0, 1):
            for step in (1, 3):
                dx = jnp.where(core == ring, step, 0)
                self.next[ring, step] = {
                    "dp": lax.rem(y + step - dx, 4),
                    "fsdp": lax.rem(x + dx, 4) * 2 + core,
                }
        self.sibling = {"fsdp": x * 2 + (1 - core)}

    def first_token(self, which, second, first):
        core = self.core if which == 0 else 1 - self.core
        dx = jnp.where(core == 0, OFFSETS[first], OFFSETS[second])
        dy = OFFSETS[first] + OFFSETS[second] - dx
        return (lax.rem(self.y + dy, 4) * NF + lax.rem(self.x + dx, 4) * 2 + core) * ROWS


class Gather:
    def __init__(self, plane, own, buf, start, width, send, recv, sib_send, sib_recv):
        self.plane, self.own, self.buf, self.start, self.width = plane, own, buf, start, width
        self.send, self.recv, self.sib_send, self.sib_recv = send, recv, sib_send, sib_recv
        self.started = []

    def part(self, roles, half):
        if half is None:
            return self.buf.at[0, roles[0], roles[1], :, pl.ds(self.start, self.width)]
        width = self.width // 2
        return self.buf.at[0, roles[0], roles[1], :, pl.ds(self.start + half * width, width)]

    def copy(self, roles, half, ring, step, send_index, there):
        src = self.own if roles == (0, 0) else self.part(roles, half)
        copy = pltpu.make_async_remote_copy(
            src_ref=src,
            dst_ref=self.part(there, half),
            send_sem=self.send.at[send_index],
            recv_sem=self.recv.at[2 * (4 * there[0] + there[1]) + (half or 0)],
            device_id=self.plane.next[ring, step],
            device_id_type=MESH,
        )
        copy.start()
        self.started.append(copy)

    def sibling_copy(self, second):
        cols = pl.ds(self.start, self.width)
        return pltpu.make_async_remote_copy(
            src_ref=self.buf.at[0, second, :, :, cols],
            dst_ref=self.buf.at[1, second, :, :, cols],
            send_sem=self.sib_send.at[second],
            recv_sem=self.sib_recv.at[second],
            device_id=self.plane.sibling,
            device_id_type=MESH,
        )

    def to_sibling(self, second):
        copy = self.sibling_copy(second)
        copy.start()
        self.started.append(copy)

    def from_sibling(self, second):
        self.sibling_copy(second).wait_recv()

    def ready(self, roles):
        second, first = roles
        base = 4 + 4 * first
        if second == 0:
            if first == 0:
                self.copy(roles, None, 0, 1, 0, (0, 1))
                self.copy(roles, None, 0, 3, 1, (0, 2))
            elif first == 1:
                self.copy(roles, 0, 0, 1, 2, (0, 3))
            elif first == 2:
                self.copy(roles, 1, 0, 3, 3, (0, 3))
            self.copy(roles, None, 1, 1, base, (1, first))
            self.copy(roles, None, 1, 3, base + 1, (2, first))
        elif second == 1:
            self.copy(roles, 0, 1, 1, base + 2, (3, first))
        elif second == 2:
            self.copy(roles, 1, 1, 3, base + 3, (3, first))

    def arrive(self, roles):
        for half in (0, 1) if roles[0] == 3 or roles == (0, 3) else (None,):
            ref = self.part(roles, half)
            pltpu.make_async_remote_copy(
                src_ref=ref,
                dst_ref=ref,
                send_sem=self.send.at[0],
                recv_sem=self.recv.at[2 * (4 * roles[0] + roles[1]) + (half or 0)],
                device_id=self.plane.next[0, 1],
                device_id_type=MESH,
            ).wait_recv()

    def step(self, roles):
        self.arrive(roles)
        self.ready(roles)
        if roles in ((0, 3), (1, 3), (2, 3), (3, 3)):
            self.to_sibling(roles[0])


def distance_of(k, sign):
    m = 8 - (k + 1) // 2
    return jnp.where(lax.rem(k, 2) == sign, LANGS - m, m)


def exchange(buf, axis, count, me, send, recv):
    copies = []
    for r in range(1, count):
        copy = pltpu.make_async_remote_copy(
            src_ref=buf.at[me],
            dst_ref=buf.at[me],
            send_sem=send.at[r],
            recv_sem=recv.at[r],
            device_id={axis: lax.rem(me + r, count)},
            device_id_type=MESH,
        )
        copy.start()
        copies.append(copy)
    for r in range(1, count):
        ref = buf.at[lax.rem(me + count - r, count)]
        pltpu.make_async_remote_copy(
            src_ref=ref,
            dst_ref=ref,
            send_sem=send.at[r],
            recv_sem=recv.at[r],
            device_id={axis: lax.rem(me + r, count)},
            device_id_type=MESH,
        ).wait_recv()
    return copies


def vaccinate(gram, targets_t, accept_t):
    rows = lax.broadcasted_iota(jnp.int32, (LANGS, LANGS), 0)
    cols = lax.broadcasted_iota(jnp.int32, (LANGS, LANGS), 1)
    identity = (rows == cols).astype(jnp.float32)
    roots = jnp.sqrt(1.0 - targets_t * targets_t)
    diag_col = jnp.sum(gram * identity, axis=1, keepdims=True)
    diag_row = jnp.sum(gram * identity, axis=0, keepdims=True)
    cos_pairs = gram / jnp.sqrt(diag_col * diag_row)
    inverse = 1.0 / jnp.sqrt(diag_col)
    scale = inverse / roots
    allowed = accept_t.astype(jnp.float32) * (1.0 - identity)
    coeffs, product = identity, gram
    for j in range(LANGS):
        norm_sq = jnp.sum(product * coeffs, axis=0, keepdims=True)
        over_norm = lax.rsqrt(norm_sq)
        cosine = product[j : j + 1, :] * inverse[j : j + 1, :] * over_norm
        sine = jnp.sqrt(jnp.maximum(1.0 - cosine * cosine, 0.0))
        step = (
            (norm_sq * over_norm)
            * (targets_t[j : j + 1, :] * sine - cosine * roots[j : j + 1, :])
            * scale[j : j + 1, :]
        )
        step = jnp.where(allowed[j : j + 1, :] > 0.5, step, 0.0)
        coeffs = jnp.where(rows == j, coeffs + step, coeffs)
        product = product + gram[:, j : j + 1] * step
    weights = jnp.sum(coeffs, axis=1, keepdims=True)
    along = jnp.sum(product, axis=1, keepdims=True)
    quad = jnp.sum(weights * along, axis=0, keepdims=True)
    mean_square = jnp.maximum(quad, 0.0) / (2.0 * D * FF)
    factor = jnp.minimum(1.0, clip_level / jnp.sqrt(mean_square + 1e-06))
    return weights * factor, cos_pairs


def kernel(
    tok_ref, cot_ref, len_hbm, wup_hbm, wdn_hbm,
    up_out, dn_out, gram_out,
    x_buf, c_buf, wup, wdn, wdn_t, lens, v_buf, hp, h_t, p_t,
    out_dn, out_up, in_dn, in_up, relay, pairs,
    local_sem, cols_sem,
    t_send, t_recv, t_sib_send, t_sib_recv,
    e_send, e_recv, e_sib_send, e_sib_recv,
    l_send, l_recv, l_sib_send, l_sib_recv,
    d_send, d_recv, u_send, u_recv, r_send, r_recv,
):
    z, y, f = lax.axis_index("lang"), lax.axis_index("dp"), lax.axis_index("fsdp")
    x, core = f // 2, lax.rem(f, 2)

    barrier = pltpu.get_barrier_semaphore()
    for axis, count, me in (("fsdp", NF, f), ("dp", NY, y), ("lang", LANGS, z)):
        for r in range(1, count):
            pl.semaphore_signal(
                barrier, inc=1, device_id={axis: lax.rem(me + r, count)}, device_id_type=MESH
            )

    def owner(k, sign):
        return lax.rem(z + (distance_of(k, sign) if not isinstance(k, int) or k < 15 else 0), LANGS)

    def columns(block):
        return pl.ds(pl.multiple_of(block * DS, DS), DS)

    plane = Plane(x, y, core)
    tok, cot = tok_ref.at[0], cot_ref.at[0]
    cot_copies = [
        pltpu.make_async_copy(
            cot.at[:, columns(owner(k, 1))], c_buf.at[0, 0, 0, :, pl.ds(k * DS, DS)], cols_sem.at[k]
        )
        for k in range(LANGS)
    ]
    local = [
        pltpu.make_async_copy(tok, x_buf.at[0, 0, 0], local_sem.at[0]),
        pltpu.make_async_copy(wdn_hbm, wdn, local_sem.at[1]),
        pltpu.make_async_copy(wup_hbm, wup, local_sem.at[2]),
        pltpu.make_async_copy(len_hbm, lens, local_sem.at[3]),
    ]
    for copy in cot_copies + local:
        copy.start()

    early = EARLY * DS
    tokens = Gather(plane, tok, x_buf, 0, D, t_send, t_recv, t_sib_send, t_sib_recv)
    first = Gather(
        plane, c_buf.at[0, 0, 0, :, pl.ds(0, early)], c_buf, 0, early,
        e_send, e_recv, e_sib_send, e_sib_recv,
    )
    rest = Gather(
        plane, c_buf.at[0, 0, 0, :, pl.ds(early, D - early)], c_buf, early, D - early,
        l_send, l_recv, l_sib_send, l_sib_recv,
    )

    pl.semaphore_wait(barrier, (NF - 1) + (NY - 1) + (LANGS - 1))
    tokens.ready((0, 0))
    for copy in cot_copies:
        copy.wait()
    first.ready((0, 0))
    for copy in local:
        copy.wait()

    wdn_t[pl.ds((LANGS - 1) * DS, DS), :] = wdn[:, columns(z)].T

    @pl.loop(0, LANGS - 1)
    def _(k):
        wdn_t[pl.ds(pl.multiple_of(k * DS, DS), DS), :] = wdn[:, columns(owner(k, 1))].T

    def activate(which, second):
        base = (which * 4 + second) * 192
        v_buf[pl.ds(base, 192), :] = jnp.dot(
            x_buf[which, second].reshape(192, D), wup[...], preferred_element_type=jnp.float32
        )
        for i in range(4):
            token = plane.first_token(which, second, i)
            slot = token // SEQ
            offset = token - slot * SEQ
            here, after = lens[0, slot], lens[0, jnp.minimum(slot + 1, 11)]
            place = lax.broadcasted_iota(jnp.int32, (ROWS, HID), 0) + offset
            keep = place < jnp.where(place < SEQ, here, after + SEQ)
            rows = pl.ds(base + i * ROWS, ROWS)
            v = v_buf[rows, :]
            k = 0.7978845608028654
            sq = v * v
            t = jnp.tanh(k * (v + 0.044715 * (sq * v)))
            cdf = 0.5 * (1.0 + t)
            slope = cdf + 0.5 * v * (1.0 - t * t) * (k * (1.0 + 3.0 * 0.044715 * sq))
            hp[rows, :] = jnp.where(keep, v * cdf, 0.0).astype(jnp.bfloat16)
            v_buf[rows, :] = jnp.where(keep, slope, 0.0)

    def turn(dst, start, count):
        for i in range(start, start + count):
            dst[:, pl.ds(i * 128, 128)] = hp[pl.ds(i * 128, 128), :].T

    for n, roles in enumerate(ARRIVALS):
        tokens.step(roles)
        first.step(roles)
        if roles == (2, 1):
            tokens.from_sibling(0)
            activate(0, 0)
            rest.ready((0, 0))
        elif roles == (2, 2):
            activate(1, 0)
        elif roles == (2, 3):
            activate(0, 1)
        elif roles == (3, 0):
            tokens.from_sibling(1)
            activate(1, 1)
        elif roles == (3, 1):
            activate(0, 2)
        elif roles == (3, 2):
            tokens.from_sibling(2)
            activate(1, 2)
    turn(h_t, 0, 3)
    turn(h_t, 6, 3)
    activate(0, 3)
    tokens.from_sibling(3)
    activate(1, 3)
    turn(h_t, 3, 3)
    turn(h_t, 9, 3)
    for second in range(4):
        first.from_sibling(second)

    def down(k):
        return jnp.dot(
            h_t[...],
            c_buf[:, :, :, :, columns(k)].reshape(LTOK, DS),
            preferred_element_type=jnp.float32,
        ).astype(jnp.bfloat16)

    def remote(src, dst, send, recv, to):
        return pltpu.make_async_remote_copy(
            src_ref=src, dst_ref=dst, send_sem=send, recv_sem=recv, device_id={"lang": to}, device_id_type=MESH
        )

    def grad_copy(sign, k, block):
        out, inbox = (out_dn, in_dn) if sign else (out_up, in_up)
        send, recv = (d_send, d_recv) if sign else (u_send, u_recv)
        return remote(out.at[k], inbox.at[block], send.at[k], recv.at[k], owner(k, sign))

    def to_relay(sign):
        out, send = (out_dn, d_send) if sign else (out_up, u_send)
        to = lax.rem(z + (4 if sign else 12), LANGS)
        return remote(out.at[0], relay.at[sign], send.at[0], r_recv.at[sign], to)

    def from_relay(sign):
        inbox, recv = (in_dn, d_recv) if sign else (in_up, u_recv)
        source, to = lax.rem(z + (12 if sign else 4), LANGS), lax.rem(z + (4 if sign else 12), LANGS)
        return remote(relay.at[sign], inbox.at[source], r_send.at[sign], recv.at[0], to)

    out_dn[0] = down(0)
    to_relay(1).start()

    @pl.loop(1, EARLY)
    def _(k):
        out_dn[k] = down(k)
        grad_copy(1, k, z).start()

    for roles in ARRIVALS:
        rest.step(roles)
    for second in range(4):
        rest.from_sibling(second)

    @pl.loop(EARLY, LANGS - 1)
    def _(k):
        out_dn[k] = down(k)
        grad_copy(1, k, z).start()

    in_dn[z] = down(LANGS - 1)

    @pl.loop(0, 4)
    def _(pair):
        which, second = pair // 2, 2 * lax.rem(pair, 2)
        hg = jnp.dot(
            c_buf[which, pl.ds(second, 2)].reshape(384, D), wdn_t[...], preferred_element_type=jnp.float32
        )
        rows = pl.ds(pl.multiple_of(pair * 384, 128), 384)
        p = (hg * v_buf[rows, :]).astype(jnp.bfloat16)
        p_t[:, rows] = p.T

    def up(block):
        return jnp.dot(
            p_t[...],
            x_buf[:, :, :, :, columns(block)].reshape(LTOK, DS),
            preferred_element_type=jnp.float32,
        ).astype(jnp.bfloat16)

    to_relay(1).wait_recv()
    from_relay(1).start()
    out_up[0] = up(owner(0, 0))
    to_relay(0).start()

    @pl.loop(1, 7)
    def _(k):
        out_up[k] = up(owner(k, 0))
        grad_copy(0, k, z).start()

    in_up[z] = up(z)
    to_relay(0).wait_recv()
    from_relay(0).start()

    @pl.loop(7, LANGS - 1)
    def _(k):
        out_up[k] = up(owner(k, 0))
        grad_copy(0, k, z).start()

    for copy in tokens.started + first.started + rest.started:
        copy.wait_send()

    pairs[...] = jnp.zeros_like(pairs)
    keep = [
        pltpu.make_async_copy(in_dn, dn_out, local_sem.at[4]),
        pltpu.make_async_copy(in_up, up_out, local_sem.at[5]),
    ]

    for sign, inbox in ((1, in_dn), (0, in_up)):

        @pl.loop(0, LANGS - 1)
        def _(k):
            grad_copy(sign, k, lax.rem(z + LANGS - distance_of(k, sign), LANGS)).wait_recv()

        keep[1 - sign].start()

        @pl.loop(0, 2)
        def _(g):
            a = jnp.concatenate(
                [
                    inbox[:, pl.ds(pl.multiple_of(g * 128 + i * 16, 16), 16), :].reshape(256, DS)
                    for i in range(8)
                ],
                axis=1,
            )
            pairs[...] += lax.dot_general(
                a, a, (((1,), (1,)), ((), ())), preferred_element_type=jnp.float32
            )

    ri = lax.broadcasted_iota(jnp.int32, (256, 256), 0)
    ci = lax.broadcasted_iota(jnp.int32, (256, 256), 1)
    same = jnp.where(lax.rem(ri, 16) == lax.rem(ci, 16), pairs[...], 0.0)
    by_row = jnp.sum(same.reshape(LANGS, 16, 256), axis=1)
    li = lax.broadcasted_iota(jnp.int32, (256, 128), 0) // 16
    lj = lax.broadcasted_iota(jnp.int32, (256, 128), 1)
    select = (li == lj).astype(jnp.float32)
    gram_out[...] = jnp.dot(
        by_row, select, precision=lax.Precision.HIGHEST, preferred_element_type=jnp.float32
    )
    for copy in keep:
        copy.wait()

    @pl.loop(0, LANGS - 1)
    def _(k):
        grad_copy(1, k, z).wait_send()
        grad_copy(0, k, z).wait_send()

    from_relay(0).wait_send()
    from_relay(1).wait_send()


def project(
    part_ref, tgt, acc, weights_out, nt_out, st1, st2, st3,
    s1_send, s1_recv, s2_send, s2_recv, s3_send, s3_recv,
):
    z, y, f = lax.axis_index("lang"), lax.axis_index("dp"), lax.axis_index("fsdp")
    barrier = pltpu.get_barrier_semaphore()
    for axis, count, me in (("fsdp", NF, f), ("dp", NY, y), ("lang", LANGS, z)):
        for r in range(1, count):
            pl.semaphore_signal(
                barrier, inc=1, device_id={axis: lax.rem(me + r, count)}, device_id_type=MESH
            )
    targets_t = tgt[...].T
    accept_t = acc[...].T
    st1[f] = part_ref[...]
    pl.semaphore_wait(barrier, (NF - 1) + (NY - 1) + (LANGS - 1))
    sends = exchange(st1, "fsdp", NF, f, s1_send, s1_recv)
    st2[y] = jnp.sum(st1[...], axis=0)
    sends += exchange(st2, "dp", NY, y, s2_send, s2_recv)
    st3[z] = jnp.sum(st2[...], axis=0)
    sends += exchange(st3, "lang", LANGS, z, s3_send, s3_recv)
    gram = jnp.sum(st3[...], axis=0)[:, :LANGS]
    weights, cos_pairs = vaccinate(gram, targets_t, accept_t)
    nt_out[...] = (1.0 - ema_rate) * tgt[...] + ema_rate * cos_pairs
    weights_out[...] = jnp.broadcast_to(weights, (LANGS, DS))
    for copy in sends:
        copy.wait_send()


def combine(up_ref, dn_ref, wv, up_out, dn_out, comb):
    for inbox, half in ((up_ref, 0), (dn_ref, 1)):

        @pl.loop(0, 2)
        def _(r):
            rows = pl.ds(pl.multiple_of(r * 64, 64), 64)
            total = jnp.zeros((64, DS), jnp.float32)
            for l in range(LANGS):
                total = total + wv[l : l + 1, :] * inbox[l, rows, :].astype(jnp.float32)
            if half == 0:
                comb[rows, :] = total
            else:
                dn_out[rows, :] = total

    up_out[...] = comb[...].T


def on_device(tokens, cotangent, lengths, up_weight, down_weight, targets, accept):
    bf16, f32 = jnp.bfloat16, jnp.float32
    dma = pltpu.SemaphoreType.DMA
    hbm = pl.BlockSpec(memory_space=pl.ANY)
    vmem = pl.BlockSpec(memory_space=pltpu.VMEM)
    up_parts, dn_parts, part = pl.pallas_call(
        kernel,
        out_shape=(
            jax.ShapeDtypeStruct((LANGS, HID, DS), bf16),
            jax.ShapeDtypeStruct((LANGS, HID, DS), bf16),
            jax.ShapeDtypeStruct((LANGS, 128), f32),
        ),
        in_specs=[hbm] * 5,
        out_specs=(hbm, hbm, vmem),
        scratch_shapes=[
            pltpu.VMEM((2, 4, 4, ROWS, D), bf16),
            pltpu.VMEM((2, 4, 4, ROWS, D), bf16),
            pltpu.VMEM((D, HID), bf16),
            pltpu.VMEM((HID, D), bf16),
            pltpu.VMEM((D, HID), bf16),
            pltpu.SMEM((1, 12), jnp.int32),
            pltpu.VMEM((LTOK, HID), f32),
            pltpu.VMEM((LTOK, HID), bf16),
            pltpu.VMEM((HID, LTOK), bf16),
            pltpu.VMEM((HID, LTOK), bf16),
            pltpu.VMEM((LANGS - 1, HID, DS), bf16),
            pltpu.VMEM((LANGS - 1, HID, DS), bf16),
            pltpu.VMEM((LANGS, HID, DS), bf16),
            pltpu.VMEM((LANGS, HID, DS), bf16),
            pltpu.VMEM((2, HID, DS), bf16),
            pltpu.VMEM((256, 256), f32),
            dma((6,)), dma((LANGS,)),
            dma((20,)), dma((32,)), dma((4,)), dma((4,)),
            dma((20,)), dma((32,)), dma((4,)), dma((4,)),
            dma((20,)), dma((32,)), dma((4,)), dma((4,)),
            dma((LANGS - 1,)), dma((LANGS - 1,)), dma((LANGS - 1,)), dma((LANGS - 1,)),
            dma((2,)), dma((2,)),
        ],
        compiler_params=pltpu.CompilerParams(
            collective_id=0, has_side_effects=True, vmem_limit_bytes=60 * 1024 * 1024
        ),
        cost_estimate=pl.CostEstimate(
            flops=4 * 2 * LTOK * D * HID, bytes_accessed=4 * 1024 * 1024, transcendentals=LTOK * HID
        ),
        name="grads",
    )(tokens, cotangent, lengths, up_weight, down_weight)
    weights, new_targets = pl.pallas_call(
        project,
        out_shape=(jax.ShapeDtypeStruct((LANGS, DS), f32), jax.ShapeDtypeStruct((LANGS, LANGS), f32)),
        in_specs=[vmem] * 3,
        out_specs=(vmem, vmem),
        scratch_shapes=[
            pltpu.VMEM((NF, LANGS, 128), f32),
            pltpu.VMEM((NY, LANGS, 128), f32),
            pltpu.VMEM((LANGS, LANGS, 128), f32),
            dma((NF,)), dma((NF,)), dma((NY,)), dma((NY,)), dma((LANGS,)), dma((LANGS,)),
        ],
        compiler_params=pltpu.CompilerParams(collective_id=1, has_side_effects=True),
        name="project",
    )(part, targets, accept)
    up_update, down_update = pl.pallas_call(
        combine,
        out_shape=(jax.ShapeDtypeStruct((DS, HID), f32), jax.ShapeDtypeStruct((HID, DS), f32)),
        grid=(2,),
        in_specs=[
            pl.BlockSpec((LANGS, 128, DS), lambda i: (0, i, 0)),
            pl.BlockSpec((LANGS, 128, DS), lambda i: (0, i, 0)),
            pl.BlockSpec((LANGS, DS), lambda i: (0, 0)),
        ],
        out_specs=(
            pl.BlockSpec((DS, 128), lambda i: (0, i)),
            pl.BlockSpec((128, DS), lambda i: (i, 0)),
        ),
        scratch_shapes=[pltpu.VMEM((128, DS), f32)],
        compiler_params=pltpu.CompilerParams(vmem_limit_bytes=60 * 1024 * 1024),
        name="combine",
    )(up_parts, dn_parts, weights)
    return up_update, down_update, new_targets


def solution(mesh):
    in_specs = (
        P("lang", ("dp", "fsdp"), None),
        P("lang", ("dp", "fsdp"), None),
        P("lang", None),
        P(None, ("dp", "fsdp")),
        P(("dp", "fsdp"), None),
        P(),
        P(),
    )
    out_specs = (P("lang", ("dp", "fsdp")), P(("dp", "fsdp"), "lang"), P())
    return jax.shard_map(
        on_device, mesh=mesh, in_specs=in_specs, out_specs=out_specs, check_vma=False
    )
```

```python
import functools

import jax
import jax.numpy as jnp
from jax import lax
from jax.experimental import pallas as pl
from jax.experimental.pallas import tpu as pltpu
from jax.sharding import PartitionSpec as P

D = 2048
FF = 8192
SEQ = 128
LTOK = 1536
LANGS = 16
NY = 4
NX = 4
NF = 8
ROWS = 48
HID = 256
DS = 128
HALF = D // 2

ema_rate = 0.01
clip_level = 0.25
MESH = pl.DeviceIdType.MESH

OFFSETS = (0, 3, 1, 2)
ARRIVALS = (
    (0, 1), (0, 2), (1, 0), (2, 0), (0, 3), (1, 1), (2, 1), (1, 2), (2, 2),
    (1, 3), (2, 3), (3, 0), (3, 1), (3, 2), (3, 3),
)
EARLY = 4


class Plane:
    def __init__(self, x, y, core):
        self.x, self.y, self.core = x, y, core
        self.next = {}
        for ring in (0, 1):
            for step in (1, 3):
                dx = jnp.where(core == ring, step, 0)
                self.next[ring, step] = {
                    "dp": lax.rem(y + step - dx, 4),
                    "fsdp": lax.rem(x + dx, 4) * 2 + core,
                }
        self.sibling = {"fsdp": x * 2 + (1 - core)}


class Gather:
    def __init__(self, plane, own, buf, start, width, send, recv, sib_send, sib_recv):
        self.plane, self.own, self.buf, self.start, self.width = plane, own, buf, start, width
        self.send, self.recv, self.sib_send, self.sib_recv = send, recv, sib_send, sib_recv
        self.started = []

    def part(self, roles, half):
        if half is None:
            return self.buf.at[0, roles[0], roles[1], :, pl.ds(self.start, self.width)]
        width = self.width // 2
        return self.buf.at[0, roles[0], roles[1], :, pl.ds(self.start + half * width, width)]

    def copy(self, roles, half, ring, step, send_index, there):
        src = self.own if roles == (0, 0) else self.part(roles, half)
        copy = pltpu.make_async_remote_copy(
            src_ref=src,
            dst_ref=self.part(there, half),
            send_sem=self.send.at[send_index],
            recv_sem=self.recv.at[2 * (4 * there[0] + there[1]) + (half or 0)],
            device_id=self.plane.next[ring, step],
            device_id_type=MESH,
        )
        copy.start()
        self.started.append(copy)

    def sibling_copy(self, second):
        cols = pl.ds(self.start, self.width)
        return pltpu.make_async_remote_copy(
            src_ref=self.buf.at[0, second, :, :, cols],
            dst_ref=self.buf.at[1, second, :, :, cols],
            send_sem=self.sib_send.at[second],
            recv_sem=self.sib_recv.at[second],
            device_id=self.plane.sibling,
            device_id_type=MESH,
        )

    def to_sibling(self, second):
        copy = self.sibling_copy(second)
        copy.start()
        self.started.append(copy)

    def from_sibling(self, second):
        self.sibling_copy(second).wait_recv()

    def ready(self, roles):
        second, first = roles
        base = 4 + 4 * first
        if second == 0:
            if first == 0:
                self.copy(roles, None, 0, 1, 0, (0, 1))
                self.copy(roles, None, 0, 3, 1, (0, 2))
            elif first == 1:
                self.copy(roles, 0, 0, 1, 2, (0, 3))
            elif first == 2:
                self.copy(roles, 1, 0, 3, 3, (0, 3))
            self.copy(roles, None, 1, 1, base, (1, first))
            self.copy(roles, None, 1, 3, base + 1, (2, first))
        elif second == 1:
            self.copy(roles, 0, 1, 1, base + 2, (3, first))
        elif second == 2:
            self.copy(roles, 1, 1, 3, base + 3, (3, first))

    def arrive(self, roles):
        for half in (0, 1) if roles[0] == 3 or roles == (0, 3) else (None,):
            ref = self.part(roles, half)
            pltpu.make_async_remote_copy(
                src_ref=ref,
                dst_ref=ref,
                send_sem=self.send.at[0],
                recv_sem=self.recv.at[2 * (4 * roles[0] + roles[1]) + (half or 0)],
                device_id=self.plane.next[0, 1],
                device_id_type=MESH,
            ).wait_recv()

    def step(self, roles):
        self.arrive(roles)
        self.ready(roles)
        if roles in ((0, 3), (1, 3), (2, 3), (3, 3)):
            self.to_sibling(roles[0])


def distance_of(k, sign):
    m = 4 - (k + 1) // 2
    return jnp.where(lax.rem(k + sign, 2) == 1, LANGS - m, m)


def exchange(buf, axis, count, me, send, recv):
    copies = []
    for r in range(1, count):
        copy = pltpu.make_async_remote_copy(
            src_ref=buf.at[me],
            dst_ref=buf.at[me],
            send_sem=send.at[r],
            recv_sem=recv.at[r],
            device_id={axis: lax.rem(me + r, count)},
            device_id_type=MESH,
        )
        copy.start()
        copies.append(copy)
    for r in range(1, count):
        ref = buf.at[lax.rem(me + count - r, count)]
        pltpu.make_async_remote_copy(
            src_ref=ref,
            dst_ref=ref,
            send_sem=send.at[r],
            recv_sem=recv.at[r],
            device_id={axis: lax.rem(me + r, count)},
            device_id_type=MESH,
        ).wait_recv()
    return copies


def vaccinate(gram, targets_t, accept_t):
    rows = lax.broadcasted_iota(jnp.int32, (LANGS, LANGS), 0)
    cols = lax.broadcasted_iota(jnp.int32, (LANGS, LANGS), 1)
    identity = (rows == cols).astype(jnp.float32)
    roots = jnp.sqrt(1.0 - targets_t * targets_t)
    diag_col = jnp.sum(gram * identity, axis=1, keepdims=True)
    diag_row = jnp.sum(gram * identity, axis=0, keepdims=True)
    cos_pairs = gram / jnp.sqrt(diag_col * diag_row)
    inverse = 1.0 / jnp.sqrt(diag_col)
    scale = inverse / roots
    allowed = accept_t.astype(jnp.float32) * (1.0 - identity)
    coeffs, product = identity, gram
    for j in range(LANGS):
        norm_sq = jnp.sum(product * coeffs, axis=0, keepdims=True)
        over_norm = lax.rsqrt(norm_sq)
        cosine = product[j : j + 1, :] * inverse[j : j + 1, :] * over_norm
        sine = jnp.sqrt(jnp.maximum(1.0 - cosine * cosine, 0.0))
        step = (
            (norm_sq * over_norm)
            * (targets_t[j : j + 1, :] * sine - cosine * roots[j : j + 1, :])
            * scale[j : j + 1, :]
        )
        step = jnp.where(allowed[j : j + 1, :] > 0.5, step, 0.0)
        coeffs = jnp.where(rows == j, coeffs + step, coeffs)
        product = product + gram[:, j : j + 1] * step
    weights = jnp.sum(coeffs, axis=1, keepdims=True)
    along = jnp.sum(product, axis=1, keepdims=True)
    quad = jnp.sum(weights * along, axis=0, keepdims=True)
    mean_square = jnp.maximum(quad, 0.0) / (2.0 * D * FF)
    factor = jnp.minimum(1.0, clip_level / jnp.sqrt(mean_square + 1e-06))
    return weights * factor, cos_pairs


def kernel(
    tok_ref, cot_ref, len_hbm, wup_hbm, wdn_hbm, tgt_hbm, acc_hbm,
    up_out, dn_out, nt_out,
    x_buf, c_buf, x_two, c_two, wup, wdn, wdn_t, tgt, acc, lens, v_buf, hp, h_t, p_t,
    out_dn, out_up, in_dn, in_up, relay, pairs, st1, st2, st3, wv, comb,
    local_sem, cols_sem, sems,
    d_send, d_recv, u_send, u_recv, i_send, i_recv, r_send, r_recv,
    s1_send, s1_recv, s2_send, s2_recv, s3_send, s3_recv,
):
    z, y, f = lax.axis_index("lang"), lax.axis_index("dp"), lax.axis_index("fsdp")
    x, core = f // 2, lax.rem(f, 2)

    barrier = pltpu.get_barrier_semaphore()
    for axis, count, me in (("fsdp", NF, f), ("dp", NY, y), ("lang", LANGS, z)):
        for r in range(1, count):
            pl.semaphore_signal(
                barrier, inc=1, device_id={axis: lax.rem(me + r, count)}, device_id_type=MESH
            )

    def owner(k, sign):
        return lax.rem(z + distance_of(k, sign), LANGS)

    def columns(block):
        return pl.ds(pl.multiple_of(block * DS, DS), DS)

    def source_columns(k):
        return columns(owner(k, 1) if k < 8 else lax.rem(owner(k - 8, 1) + 8, LANGS))

    plane = Plane(x, y, core)
    tok, cot = tok_ref.at[0], cot_ref.at[0]
    cot_copies = [
        pltpu.make_async_copy(
            cot.at[:, source_columns(k)], c_buf.at[0, 0, 0, :, pl.ds(k * DS, DS)], cols_sem.at[k]
        )
        for k in range(LANGS)
    ]
    lens_copy = pltpu.make_async_copy(len_hbm, lens, local_sem.at[5])
    local = [
        pltpu.make_async_copy(tok, x_buf.at[0, 0, 0], local_sem.at[0]),
        pltpu.make_async_copy(wdn_hbm, wdn, local_sem.at[1]),
        pltpu.make_async_copy(wup_hbm, wup, local_sem.at[2]),
        pltpu.make_async_copy(tgt_hbm, tgt, local_sem.at[3]),
        pltpu.make_async_copy(acc_hbm, acc, local_sem.at[4]),
    ]
    lens_copy.start()
    for copy in cot_copies + local:
        copy.start()

    early = EARLY * DS

    def gathers(number, own, x_ref, c_ref):
        made = []
        for n, (src, buf, start, width) in enumerate(
            (
                (own, x_ref, 0, D),
                (c_ref.at[0, 0, 0, :, pl.ds(0, early)], c_ref, 0, early),
                (c_ref.at[0, 0, 0, :, pl.ds(early, D - early)], c_ref, early, D - early),
            )
        ):
            base = (3 * number + n) * 60
            parts = [sems.at[pl.ds(base + a, b)] for a, b in ((0, 20), (20, 32), (52, 4), (56, 4))]
            made.append(Gather(plane, src, buf, start, width, *parts))
        return made

    tokens, first, rest = gathers(0, tok, x_buf, c_buf)
    tokens2, first2, rest2 = gathers(1, x_two.at[0, 0, 0], x_two, c_two)

    def remote(src, dst, send, recv, to):
        return pltpu.make_async_remote_copy(
            src_ref=src, dst_ref=dst, send_sem=send, recv_sem=recv, device_id={"lang": to}, device_id_type=MESH
        )

    def columns_half(ref, n):
        return ref.at[:, pl.ds(n * HALF, HALF)]

    def leg_to(n):
        return lax.rem(z + (4 if n % 2 == 0 else 12), LANGS)

    def first_leg(n):
        src = columns_half(tok if n < 2 else c_buf.at[0, 0, 0], n % 2)
        return remote(src, relay.at[n], i_send.at[n], i_recv.at[n], leg_to(n))

    def second_leg(n):
        dst = columns_half(x_two.at[0, 0, 0], n) if n < 2 else columns_half(c_two.at[0, 0, 0], 3 - n)
        return remote(relay.at[n], dst, r_send.at[n], r_recv.at[n], leg_to(n))

    def forward(n):
        first_leg(n).wait_recv()
        second_leg(n).start()

    pl.semaphore_wait(barrier, (NF - 1) + (NY - 1) + (LANGS - 1))
    tokens.ready((0, 0))
    first_leg(0).start()
    first_leg(1).start()

    lens_copy.wait()
    for copy in cot_copies:
        copy.wait()
    token = (y * NF + x * 2 + core) * ROWS
    slot = token // SEQ
    here, after = lens[0, slot], lens[0, jnp.minimum(slot + 1, 11)]
    place = lax.broadcasted_iota(jnp.int32, (ROWS, D), 0) + (token - slot * SEQ)
    kept = place < jnp.where(place < SEQ, here, after + SEQ)
    mine = c_buf[0, 0, 0].astype(jnp.float32)
    c_buf[0, 0, 0] = jnp.where(kept, mine, 0.0).astype(jnp.bfloat16)
    first.ready((0, 0))
    first_leg(2).start()
    first_leg(3).start()

    for copy in local:
        copy.wait()

    @pl.loop(0, 8)
    def _(k):
        low = owner(k, 1)
        wdn_t[pl.ds(pl.multiple_of(k * DS, DS), DS), :] = wdn[:, columns(low)].T
        high = lax.rem(low + 8, LANGS)
        wdn_t[pl.ds(pl.multiple_of(HALF + k * DS, DS), DS), :] = wdn[:, columns(high)].T

    def activate(x_ref, which, second):
        base = (which * 4 + second) * 192
        v_buf[pl.ds(base, 192), :] = jnp.dot(
            x_ref[which, second].reshape(192, D), wup[...], preferred_element_type=jnp.float32
        )

        @pl.loop(0, 4)
        def _(i):
            rows = pl.ds(pl.multiple_of(base + i * ROWS, 16), ROWS)
            v = v_buf[rows, :]
            k = 0.7978845608028654
            sq = v * v
            t = jnp.tanh(k * (v + 0.044715 * (sq * v)))
            cdf = 0.5 * (1.0 + t)
            v_buf[rows, :] = cdf + 0.5 * v * (1.0 - t * t) * (k * (1.0 + 3.0 * 0.044715 * sq))
            hp[rows, :] = (v * cdf).astype(jnp.bfloat16)

    def turn(dst, start, count):
        @pl.loop(start, start + count)
        def _(i):
            part = pl.ds(pl.multiple_of(i * 128, 128), 128)
            dst[:, part] = hp[part, :].T

    def down(c_ref, k):
        return jnp.dot(
            h_t[...],
            c_ref[:, :, :, :, columns(k)].reshape(LTOK, DS),
            preferred_element_type=jnp.float32,
        ).astype(jnp.bfloat16)

    def up(x_ref, k):
        return jnp.dot(
            p_t[...],
            x_ref[:, :, :, :, columns(owner(k, 0))].reshape(LTOK, DS),
            preferred_element_type=jnp.float32,
        ).astype(jnp.bfloat16)

    def grad_copy(sign, number, k, source):
        out, inbox = (out_dn, in_dn) if sign else (out_up, in_up)
        send, recv = (d_send, d_recv) if sign else (u_send, u_recv)
        index = number * 7 + k
        return remote(
            out.at[index],
            inbox.at[lax.rem(source + 8 * number, LANGS)],
            send.at[index],
            recv.at[index],
            owner(k, sign),
        )

    def send_down(number, c_ref, start, stop):
        @pl.loop(start, stop)
        def _(k):
            out_dn[number * 7 + k] = down(c_ref, k)
            grad_copy(1, number, k, z).start()

    def send_up(number, x_ref, start, stop):
        @pl.loop(start, stop)
        def _(k):
            out_up[number * 7 + k] = up(x_ref, k)
            grad_copy(0, number, k, z).start()

    def preact_grad(c_ref, pair):
        which, second = pair // 2, 2 * (pair % 2)
        hg = jnp.dot(
            c_ref[which, second : second + 2].reshape(384, D), wdn_t[...], preferred_element_type=jnp.float32
        )
        rows = pl.ds(pair * 384, 384)
        hp[rows, :] = (hg * v_buf[rows, :]).astype(jnp.bfloat16)
        turn(p_t, pair * 3, 3)

    def with_tokens(gather_x, gather_c, x_ref, extra):
        for n, roles in enumerate(ARRIVALS):
            gather_x.step(roles)
            gather_c.step(roles)
            for piece in extra.get(n, ()):
                piece()
            if n == 8:
                gather_x.from_sibling(0)
                activate(x_ref, 0, 0)
            elif n == 9:
                activate(x_ref, 1, 0)
            elif n == 10:
                activate(x_ref, 0, 1)
            elif n == 11:
                gather_x.from_sibling(1)
                activate(x_ref, 1, 1)
            elif n == 12:
                activate(x_ref, 0, 2)
            elif n == 13:
                gather_x.from_sibling(2)
                activate(x_ref, 1, 2)
        turn(h_t, 0, 3)
        turn(h_t, 6, 3)
        activate(x_ref, 0, 3)
        gather_x.from_sibling(3)
        activate(x_ref, 1, 3)
        turn(h_t, 3, 3)
        turn(h_t, 9, 3)
        for second in range(4):
            gather_c.from_sibling(second)

    def begin_two():
        second_leg(0).wait_recv()
        second_leg(1).wait_recv()
        tokens2.ready((0, 0))

    with_tokens(
        tokens, first, x_buf,
        {
            4: [lambda: rest.ready((0, 0))],
            5: [lambda: forward(0), lambda: forward(1)],
            10: [lambda: forward(2), lambda: forward(3)],
        },
    )
    send_down(0, c_buf, 0, EARLY)
    for n, roles in enumerate(ARRIVALS):
        rest.step(roles)
        if n == 8:
            begin_two()
    second_leg(2).wait_recv()
    second_leg(3).wait_recv()
    first2.ready((0, 0))
    for second in range(4):
        rest.from_sibling(second)
    send_down(0, c_buf, EARLY, 7)
    in_dn[z] = down(c_buf, 7)

    def own_up():
        in_up[z] = up(x_buf, 7)

    with_tokens(
        tokens2, first2, x_two,
        {
            0: [functools.partial(preact_grad, c_buf, 0)],
            1: [functools.partial(preact_grad, c_buf, 1)],
            2: [functools.partial(preact_grad, c_buf, 2)],
            3: [functools.partial(preact_grad, c_buf, 3)],
            4: [functools.partial(send_up, 0, x_buf, 0, 2)],
            5: [functools.partial(send_up, 0, x_buf, 2, 4), lambda: rest2.ready((0, 0))],
            6: [functools.partial(send_up, 0, x_buf, 4, 7)],
            7: [own_up],
        },
    )
    send_down(1, c_two, 0, EARLY)
    for n, roles in enumerate(ARRIVALS):
        rest2.step(roles)
        if n == 11:
            rest2.from_sibling(0)
            rest2.from_sibling(1)
            preact_grad(c_two, 0)
        elif n == 12:
            preact_grad(c_two, 2)
    rest2.from_sibling(2)
    rest2.from_sibling(3)
    preact_grad(c_two, 1)
    preact_grad(c_two, 3)
    send_up(1, x_two, 0, 7)
    send_down(1, c_two, EARLY, 7)
    opposite = lax.rem(z + 8, LANGS)
    in_up[opposite] = up(x_two, 7)
    in_dn[opposite] = down(c_two, 7)

    pairs[...] = jnp.zeros_like(pairs)
    targets_t = tgt[...].T
    accept_t = acc[...].T

    for sign, inbox in ((1, in_dn), (0, in_up)):
        for number in range(2):

            @pl.loop(0, 7)
            def _(k):
                grad_copy(sign, number, k, lax.rem(z + LANGS - distance_of(k, sign), LANGS)).wait_recv()

        @pl.loop(0, 2)
        def _(g):
            a = jnp.concatenate(
                [
                    inbox[:, pl.ds(pl.multiple_of(g * 128 + i * 16, 16), 16), :].reshape(256, DS)
                    for i in range(8)
                ],
                axis=1,
            )
            pairs[...] += lax.dot_general(
                a, a, (((1,), (1,)), ((), ())), preferred_element_type=jnp.float32
            )

    ri = lax.broadcasted_iota(jnp.int32, (256, 256), 0)
    ci = lax.broadcasted_iota(jnp.int32, (256, 256), 1)
    same = jnp.where(lax.rem(ri, 16) == lax.rem(ci, 16), pairs[...], 0.0)
    by_row = jnp.sum(same.reshape(LANGS, 16, 256), axis=1)
    li = lax.broadcasted_iota(jnp.int32, (256, 128), 0) // 16
    lj = lax.broadcasted_iota(jnp.int32, (256, 128), 1)
    select = (li == lj).astype(jnp.float32)
    st1[f] = jnp.dot(
        by_row, select, precision=lax.Precision.HIGHEST, preferred_element_type=jnp.float32
    )
    sends = exchange(st1, "fsdp", NF, f, s1_send, s1_recv)
    st2[y] = jnp.sum(st1[...], axis=0)
    sends += exchange(st2, "dp", NY, y, s2_send, s2_recv)
    st3[z] = jnp.sum(st2[...], axis=0)
    sends += exchange(st3, "lang", LANGS, z, s3_send, s3_recv)
    gram = jnp.sum(st3[...], axis=0)[:, :LANGS]

    weights, cos_pairs = vaccinate(gram, targets_t, accept_t)
    nt_out[...] = (1.0 - ema_rate) * tgt[...] + ema_rate * cos_pairs
    wv[...] = jnp.broadcast_to(weights, (LANGS, DS))

    for inbox, half in ((in_up, 0), (in_dn, 1)):

        @pl.loop(0, 4)
        def _(r):
            rows = pl.ds(pl.multiple_of(r * 64, 64), 64)
            total = jnp.zeros((64, DS), jnp.float32)
            for l in range(LANGS):
                total = total + wv[l : l + 1, :] * inbox[l, rows, :].astype(jnp.float32)
            if half == 0:
                comb[rows, :] = total
            else:
                dn_out[rows, :] = total

    up_out[...] = comb[...].T

    for copy in sends:
        copy.wait_send()

    for gather in (tokens, first, rest, tokens2, first2, rest2):
        for copy in gather.started:
            copy.wait_send()
    for n in range(4):
        first_leg(n).wait_send()
        second_leg(n).wait_send()
    for number in range(2):

        @pl.loop(0, 7)
        def _(k):
            grad_copy(1, number, k, z).wait_send()
            grad_copy(0, number, k, z).wait_send()


def on_device(tokens, cotangent, lengths, up_weight, down_weight, targets, accept):
    bf16, f32 = jnp.bfloat16, jnp.float32
    dma = pltpu.SemaphoreType.DMA
    hbm = pl.BlockSpec(memory_space=pl.ANY)
    vmem = pl.BlockSpec(memory_space=pltpu.VMEM)
    return pl.pallas_call(
        kernel,
        out_shape=(
            jax.ShapeDtypeStruct((DS, HID), f32),
            jax.ShapeDtypeStruct((HID, DS), f32),
            jax.ShapeDtypeStruct((LANGS, LANGS), f32),
        ),
        in_specs=[hbm] * 7,
        out_specs=(vmem, vmem, vmem),
        scratch_shapes=[
            pltpu.VMEM((2, 4, 4, ROWS, D), bf16),
            pltpu.VMEM((2, 4, 4, ROWS, D), bf16),
            pltpu.VMEM((2, 4, 4, ROWS, D), bf16),
            pltpu.VMEM((2, 4, 4, ROWS, D), bf16),
            pltpu.VMEM((D, HID), bf16),
            pltpu.VMEM((HID, D), bf16),
            pltpu.VMEM((D, HID), bf16),
            pltpu.VMEM((LANGS, LANGS), f32),
            pltpu.VMEM((LANGS, LANGS), jnp.int32),
            pltpu.SMEM((1, 12), jnp.int32),
            pltpu.VMEM((LTOK, HID), f32),
            pltpu.VMEM((LTOK, HID), bf16),
            pltpu.VMEM((HID, LTOK), bf16),
            pltpu.VMEM((HID, LTOK), bf16),
            pltpu.VMEM((14, HID, DS), bf16),
            pltpu.VMEM((14, HID, DS), bf16),
            pltpu.VMEM((LANGS, HID, DS), bf16),
            pltpu.VMEM((LANGS, HID, DS), bf16),
            pltpu.VMEM((4, ROWS, HALF), bf16),
            pltpu.VMEM((256, 256), f32),
            pltpu.VMEM((NF, LANGS, 128), f32),
            pltpu.VMEM((NY, LANGS, 128), f32),
            pltpu.VMEM((LANGS, LANGS, 128), f32),
            pltpu.VMEM((LANGS, DS), f32),
            pltpu.VMEM((HID, DS), f32),
            dma((6,)), dma((LANGS,)), dma((360,)),
            dma((14,)), dma((14,)), dma((14,)), dma((14,)),
            dma((4,)), dma((4,)), dma((4,)), dma((4,)),
            dma((NF,)), dma((NF,)), dma((NY,)), dma((NY,)), dma((LANGS,)), dma((LANGS,)),
        ],
        compiler_params=pltpu.CompilerParams(
            collective_id=0, has_side_effects=True, vmem_limit_bytes=60 * 1024 * 1024
        ),
        cost_estimate=pl.CostEstimate(
            flops=4 * 2 * LTOK * D * HID, bytes_accessed=4 * 1024 * 1024, transcendentals=LTOK * HID
        ),
        name="vaccine_step",
    )(tokens, cotangent, lengths, up_weight, down_weight, targets, accept)


def solution(mesh):
    in_specs = (
        P("lang", ("dp", "fsdp"), None),
        P("lang", ("dp", "fsdp"), None),
        P("lang", None),
        P(None, ("dp", "fsdp")),
        P(("dp", "fsdp"), None),
        P(),
        P(),
    )
    out_specs = (P("lang", ("dp", "fsdp")), P(("dp", "fsdp"), "lang"), P())
    return jax.shard_map(
        on_device, mesh=mesh, in_specs=in_specs, out_specs=out_specs, check_vma=False
    )
```

```python
import functools

import jax
import jax.numpy as jnp
from jax import lax
from jax.experimental import pallas as pl
from jax.experimental.pallas import tpu as pltpu
from jax.sharding import PartitionSpec as P

D = 2048
FF = 8192
SEQ = 128
LTOK = 1536
LANGS = 16
NY = 4
NX = 4
NF = 8
ROWS = 48
HID = 256
DS = 128
HALF = D // 2

ema_rate = 0.01
clip_level = 0.25
MESH = pl.DeviceIdType.MESH

OFFSETS = (0, 3, 1, 2)
ARRIVALS = (
    (0, 1), (0, 2), (1, 0), (2, 0), (0, 3), (1, 1), (2, 1), (1, 2), (2, 2),
    (1, 3), (2, 3), (3, 0), (3, 1), (3, 2), (3, 3),
)
EARLY = 6


class Plane:
    def __init__(self, x, y, core):
        self.x, self.y, self.core = x, y, core
        self.next = {}
        for ring in (0, 1):
            for step in (1, 3):
                dx = jnp.where(core == ring, step, 0)
                self.next[ring, step] = {
                    "dp": lax.rem(y + step - dx, 4),
                    "fsdp": lax.rem(x + dx, 4) * 2 + core,
                }
        self.sibling = {"fsdp": x * 2 + (1 - core)}


class Gather:
    def __init__(self, plane, own, buf, start, width, send, recv, sib_send, sib_recv):
        self.plane, self.own, self.buf, self.start, self.width = plane, own, buf, start, width
        self.send, self.recv, self.sib_send, self.sib_recv = send, recv, sib_send, sib_recv
        self.started = []

    def part(self, roles, half):
        if half is None:
            return self.buf.at[0, roles[0], roles[1], :, pl.ds(self.start, self.width)]
        width = self.width // 2
        return self.buf.at[0, roles[0], roles[1], :, pl.ds(self.start + half * width, width)]

    def copy(self, roles, half, ring, step, send_index, there):
        src = self.own if roles == (0, 0) else self.part(roles, half)
        copy = pltpu.make_async_remote_copy(
            src_ref=src,
            dst_ref=self.part(there, half),
            send_sem=self.send.at[send_index],
            recv_sem=self.recv.at[2 * (4 * there[0] + there[1]) + (half or 0)],
            device_id=self.plane.next[ring, step],
            device_id_type=MESH,
        )
        copy.start()
        self.started.append(copy)

    def sibling_copy(self, second):
        cols = pl.ds(self.start, self.width)
        return pltpu.make_async_remote_copy(
            src_ref=self.buf.at[0, second, :, :, cols],
            dst_ref=self.buf.at[1, second, :, :, cols],
            send_sem=self.sib_send.at[second],
            recv_sem=self.sib_recv.at[second],
            device_id=self.plane.sibling,
            device_id_type=MESH,
        )

    def to_sibling(self, second):
        copy = self.sibling_copy(second)
        copy.start()
        self.started.append(copy)

    def from_sibling(self, second):
        self.sibling_copy(second).wait_recv()

    def ready(self, roles):
        second, first = roles
        base = 4 + 4 * first
        if second == 0:
            if first == 0:
                self.copy(roles, None, 0, 1, 0, (0, 1))
                self.copy(roles, None, 0, 3, 1, (0, 2))
            elif first == 1:
                self.copy(roles, 0, 0, 1, 2, (0, 3))
            elif first == 2:
                self.copy(roles, 1, 0, 3, 3, (0, 3))
            self.copy(roles, None, 1, 1, base, (1, first))
            self.copy(roles, None, 1, 3, base + 1, (2, first))
        elif second == 1:
            self.copy(roles, 0, 1, 1, base + 2, (3, first))
        elif second == 2:
            self.copy(roles, 1, 1, 3, base + 3, (3, first))

    def arrive(self, roles):
        for half in (0, 1) if roles[0] == 3 or roles == (0, 3) else (None,):
            ref = self.part(roles, half)
            pltpu.make_async_remote_copy(
                src_ref=ref,
                dst_ref=ref,
                send_sem=self.send.at[0],
                recv_sem=self.recv.at[2 * (4 * roles[0] + roles[1]) + (half or 0)],
                device_id=self.plane.next[0, 1],
                device_id_type=MESH,
            ).wait_recv()

    def step(self, roles):
        self.arrive(roles)
        self.ready(roles)
        if roles in ((0, 3), (1, 3), (2, 3), (3, 3)):
            self.to_sibling(roles[0])


NEAR = ((3, 2, 14, 1, 15, 5, 11, 12, 4, 13), (2, 14, 1, 15))
COLUMN_ORDER = (2, 14, 1, 15, 0, 3, 12, 5)
OWN_COLUMNS = 4
COLUMN_OF = {d: i for i, d in enumerate(COLUMN_ORDER + tuple((d + 8) % 16 for d in COLUMN_ORDER))}


def pick(k, values):
    if isinstance(k, int):
        return values[k]
    found = jnp.int32(values[-1])
    for i, value in enumerate(values[:-1]):
        found = jnp.where(k == i, value, found)
    return found


def exchange(buf, axis, count, me, send, recv):
    copies = []
    for r in range(1, count):
        copy = pltpu.make_async_remote_copy(
            src_ref=buf.at[me],
            dst_ref=buf.at[me],
            send_sem=send.at[r],
            recv_sem=recv.at[r],
            device_id={axis: lax.rem(me + r, count)},
            device_id_type=MESH,
        )
        copy.start()
        copies.append(copy)
    for r in range(1, count):
        ref = buf.at[lax.rem(me + count - r, count)]
        pltpu.make_async_remote_copy(
            src_ref=ref,
            dst_ref=ref,
            send_sem=send.at[r],
            recv_sem=recv.at[r],
            device_id={axis: lax.rem(me + r, count)},
            device_id_type=MESH,
        ).wait_recv()
    return copies


def vaccinate(gram, targets_t, accept_t):
    rows = lax.broadcasted_iota(jnp.int32, (LANGS, LANGS), 0)
    cols = lax.broadcasted_iota(jnp.int32, (LANGS, LANGS), 1)
    identity = (rows == cols).astype(jnp.float32)
    roots = jnp.sqrt(1.0 - targets_t * targets_t)
    diag_col = jnp.sum(gram * identity, axis=1, keepdims=True)
    diag_row = jnp.sum(gram * identity, axis=0, keepdims=True)
    cos_pairs = gram / jnp.sqrt(diag_col * diag_row)
    inverse = 1.0 / jnp.sqrt(diag_col)
    scale = inverse / roots
    allowed = accept_t.astype(jnp.float32) * (1.0 - identity)
    coeffs, product = identity, gram
    for j in range(LANGS):
        norm_sq = jnp.sum(product * coeffs, axis=0, keepdims=True)
        over_norm = lax.rsqrt(norm_sq)
        cosine = product[j : j + 1, :] * inverse[j : j + 1, :] * over_norm
        sine = jnp.sqrt(jnp.maximum(1.0 - cosine * cosine, 0.0))
        step = (
            (norm_sq * over_norm)
            * (targets_t[j : j + 1, :] * sine - cosine * roots[j : j + 1, :])
            * scale[j : j + 1, :]
        )
        step = jnp.where(allowed[j : j + 1, :] > 0.5, step, 0.0)
        coeffs = jnp.where(rows == j, coeffs + step, coeffs)
        product = product + gram[:, j : j + 1] * step
    weights = jnp.sum(coeffs, axis=1, keepdims=True)
    along = jnp.sum(product, axis=1, keepdims=True)
    quad = jnp.sum(weights * along, axis=0, keepdims=True)
    mean_square = jnp.maximum(quad, 0.0) / (2.0 * D * FF)
    factor = jnp.minimum(1.0, clip_level / jnp.sqrt(mean_square + 1e-06))
    return weights * factor, cos_pairs


def kernel(
    tok_ref, cot_ref, len_hbm, wup_hbm, wdn_hbm, tgt_hbm, acc_hbm,
    up_out, dn_out, nt_out,
    x_buf, c_buf, x_two, c_two, wup, wdn, wdn_t, tgt, acc, lens, v_buf, hp, h_t, p_t,
    out_dn, out_up, in_dn, in_up, relay, pairs, st1, st2, st3, wv, comb,
    local_sem, cols_sem, sems,
    d_send, d_recv, u_send, u_recv, i_send, i_recv, r_send, r_recv,
    s1_send, s1_recv, s2_send, s2_recv, s3_send, s3_recv,
):
    z, y, f = lax.axis_index("lang"), lax.axis_index("dp"), lax.axis_index("fsdp")
    x, core = f // 2, lax.rem(f, 2)

    barrier = pltpu.get_barrier_semaphore()
    for axis, count, me in (("fsdp", NF, f), ("dp", NY, y), ("lang", LANGS, z)):
        for r in range(1, count):
            pl.semaphore_signal(
                barrier, inc=1, device_id={axis: lax.rem(me + r, count)}, device_id_type=MESH
            )

    def owner(number, k):
        return lax.rem(z + pick(k, NEAR[number]), LANGS)

    def columns(block):
        return pl.ds(pl.multiple_of(block * DS, DS), DS)

    def source_columns(k):
        return columns(lax.rem(z + COLUMN_ORDER[k % 8] + 8 * (k // 8), LANGS))

    plane = Plane(x, y, core)
    tok, cot = tok_ref.at[0], cot_ref.at[0]
    cot_copies = [
        pltpu.make_async_copy(
            cot.at[:, source_columns(k)], c_buf.at[0, 0, 0, :, pl.ds(k * DS, DS)], cols_sem.at[k]
        )
        for k in range(LANGS)
    ]
    lens_copy = pltpu.make_async_copy(len_hbm, lens, local_sem.at[5])
    local = [
        pltpu.make_async_copy(tok, x_buf.at[0, 0, 0], local_sem.at[0]),
        pltpu.make_async_copy(wdn_hbm, wdn, local_sem.at[1]),
        pltpu.make_async_copy(wup_hbm, wup, local_sem.at[2]),
        pltpu.make_async_copy(tgt_hbm, tgt, local_sem.at[3]),
        pltpu.make_async_copy(acc_hbm, acc, local_sem.at[4]),
    ]
    lens_copy.start()
    for copy in cot_copies + local:
        copy.start()

    early = EARLY * DS

    def gathers(number, own, x_ref, c_ref):
        start_rest = early if number else 0
        made = []
        for n, (src, buf, start, width) in enumerate(
            (
                (own, x_ref, 0, D),
                (c_ref.at[0, 0, 0, :, pl.ds(0, early)], c_ref, 0, early),
                (c_ref.at[0, 0, 0, :, pl.ds(start_rest, D - start_rest)], c_ref, start_rest, D - start_rest),
            )
        ):
            base = (3 * number + n) * 60
            parts = [sems.at[pl.ds(base + a, b)] for a, b in ((0, 20), (20, 32), (52, 4), (56, 4))]
            made.append(Gather(plane, src, buf, start, width, *parts))
        return made

    tokens, _, rest = gathers(0, tok, x_buf, c_buf)
    tokens2, first2, rest2 = gathers(1, x_two.at[0, 0, 0], x_two, c_two)

    def remote(src, dst, send, recv, to):
        return pltpu.make_async_remote_copy(
            src_ref=src, dst_ref=dst, send_sem=send, recv_sem=recv, device_id={"lang": to}, device_id_type=MESH
        )

    def columns_half(ref, n):
        return ref.at[:, pl.ds(n * HALF, HALF)]

    def leg_to(n):
        return lax.rem(z + (4 if n % 2 == 0 else 12), LANGS)

    def first_leg(n):
        src = columns_half(tok if n < 2 else c_buf.at[0, 0, 0], n % 2)
        return remote(src, relay.at[n], i_send.at[n], i_recv.at[n], leg_to(n))

    def second_leg(n):
        dst = columns_half(x_two.at[0, 0, 0], n) if n < 2 else columns_half(c_two.at[0, 0, 0], 3 - n)
        return remote(relay.at[n], dst, r_send.at[n], r_recv.at[n], leg_to(n))

    def forward(n):
        first_leg(n).wait_recv()
        second_leg(n).start()

    pl.semaphore_wait(barrier, (NF - 1) + (NY - 1) + (LANGS - 1))
    tokens.ready((0, 0))
    first_leg(0).start()
    first_leg(1).start()

    lens_copy.wait()
    for copy in cot_copies:
        copy.wait()
    token = (y * NF + x * 2 + core) * ROWS
    slot = token // SEQ
    here, after = lens[0, slot], lens[0, jnp.minimum(slot + 1, 11)]
    place = lax.broadcasted_iota(jnp.int32, (ROWS, D), 0) + (token - slot * SEQ)
    kept = place < jnp.where(place < SEQ, here, after + SEQ)
    mine = c_buf[0, 0, 0].astype(jnp.float32)
    c_buf[0, 0, 0] = jnp.where(kept, mine, 0.0).astype(jnp.bfloat16)
    first_leg(2).start()
    first_leg(3).start()

    for copy in local:
        copy.wait()

    @pl.loop(0, 8)
    def _(k):
        low = lax.rem(z + pick(k, COLUMN_ORDER), LANGS)
        wdn_t[pl.ds(pl.multiple_of(k * DS, DS), DS), :] = wdn[:, columns(low)].T
        high = lax.rem(low + 8, LANGS)
        wdn_t[pl.ds(pl.multiple_of(HALF + k * DS, DS), DS), :] = wdn[:, columns(high)].T

    def activate(x_ref, which, second):
        base = (which * 4 + second) * 192
        v_buf[pl.ds(base, 192), :] = jnp.dot(
            x_ref[which, second].reshape(192, D), wup[...], preferred_element_type=jnp.float32
        )

        @pl.loop(0, 4)
        def _(i):
            rows = pl.ds(pl.multiple_of(base + i * ROWS, 16), ROWS)
            v = v_buf[rows, :]
            k = 0.7978845608028654
            sq = v * v
            t = jnp.tanh(k * (v + 0.044715 * (sq * v)))
            cdf = 0.5 * (1.0 + t)
            v_buf[rows, :] = cdf + 0.5 * v * (1.0 - t * t) * (k * (1.0 + 3.0 * 0.044715 * sq))
            hp[rows, :] = (v * cdf).astype(jnp.bfloat16)

    def turn(dst, start, count):
        @pl.loop(start, start + count)
        def _(i):
            part = pl.ds(pl.multiple_of(i * 128, 128), 128)
            dst[:, part] = hp[part, :].T

    def down(c_ref, k):
        return jnp.dot(
            h_t[...],
            c_ref[:, :, :, :, columns(k)].reshape(LTOK, DS),
            preferred_element_type=jnp.float32,
        ).astype(jnp.bfloat16)

    def up(x_ref, block):
        return jnp.dot(
            p_t[...],
            x_ref[:, :, :, :, columns(block)].reshape(LTOK, DS),
            preferred_element_type=jnp.float32,
        ).astype(jnp.bfloat16)

    def grad_copy(sign, number, k, source):
        out, inbox = (out_dn, in_dn) if sign else (out_up, in_up)
        send, recv = (d_send, d_recv) if sign else (u_send, u_recv)
        index = number * len(NEAR[0]) + k
        return remote(
            out.at[index],
            inbox.at[lax.rem(source + 8 * number, LANGS)],
            send.at[index],
            recv.at[index],
            owner(number, k),
        )

    def send_down(number, c_ref, start, stop):
        @pl.loop(start, stop)
        def _(k):
            place = pick(k, tuple(COLUMN_OF[d] for d in NEAR[number]))
            out_dn[number * len(NEAR[0]) + k] = down(c_ref, place)
            grad_copy(1, number, k, z).start()

    def send_up(number, x_ref, start, stop):
        @pl.loop(start, stop)
        def _(k):
            out_up[number * len(NEAR[0]) + k] = up(x_ref, owner(number, k))
            grad_copy(0, number, k, z).start()

    def preact_grad(c_ref, pair):
        which, second = pair // 2, 2 * (pair % 2)
        hg = jnp.dot(
            c_ref[which, second : second + 2].reshape(384, D), wdn_t[...], preferred_element_type=jnp.float32
        )
        rows = pl.ds(pair * 384, 384)
        hp[rows, :] = (hg * v_buf[rows, :]).astype(jnp.bfloat16)
        turn(p_t, pair * 3, 3)

    def with_tokens(gather_x, gather_c, x_ref, extra):
        for n, roles in enumerate(ARRIVALS):
            gather_x.step(roles)
            if gather_c is not None:
                gather_c.step(roles)
            for piece in extra.get(n, ()):
                piece()
            if n == 8:
                gather_x.from_sibling(0)
                activate(x_ref, 0, 0)
            elif n == 9:
                activate(x_ref, 1, 0)
            elif n == 10:
                activate(x_ref, 0, 1)
            elif n == 11:
                gather_x.from_sibling(1)
                activate(x_ref, 1, 1)
            elif n == 12:
                activate(x_ref, 0, 2)
            elif n == 13:
                gather_x.from_sibling(2)
                activate(x_ref, 1, 2)
        turn(h_t, 0, 3)
        turn(h_t, 6, 3)
        activate(x_ref, 0, 3)
        gather_x.from_sibling(3)
        activate(x_ref, 1, 3)
        turn(h_t, 3, 3)
        turn(h_t, 9, 3)
        if gather_c is not None:
            for second in range(4):
                gather_c.from_sibling(second)

    def begin_two():
        second_leg(0).wait_recv()
        second_leg(1).wait_recv()
        tokens2.ready((0, 0))

    with_tokens(
        tokens, None, x_buf,
        {
            4: [lambda: rest.ready((0, 0))],
            5: [lambda: forward(0), lambda: forward(1)],
            10: [lambda: forward(2), lambda: forward(3)],
        },
    )
    for n, roles in enumerate(ARRIVALS):
        rest.step(roles)
        if n == 8:
            begin_two()
        elif n == 11:
            rest.from_sibling(0)
            rest.from_sibling(1)
            preact_grad(c_buf, 0)
        elif n == 12:
            preact_grad(c_buf, 2)
    second_leg(2).wait_recv()
    second_leg(3).wait_recv()
    first2.ready((0, 0))
    rest.from_sibling(2)
    rest.from_sibling(3)

    def own_down():
        in_dn[z] = down(c_buf, OWN_COLUMNS)

    def own_up():
        in_up[z] = up(x_buf, z)

    with_tokens(
        tokens2, first2, x_two,
        {
            0: [functools.partial(send_down, 0, c_buf, 5, 8)],
            1: [functools.partial(send_down, 0, c_buf, 8, 10)],
            2: [functools.partial(send_down, 0, c_buf, 0, 5)],
            3: [functools.partial(preact_grad, c_buf, 1)],
            4: [functools.partial(preact_grad, c_buf, 3), lambda: rest2.ready((0, 0))],
            5: [functools.partial(send_up, 0, x_buf, 5, 8)],
            6: [functools.partial(send_up, 0, x_buf, 8, 10)],
            7: [functools.partial(send_up, 0, x_buf, 0, 5), own_down],
        },
    )
    send_down(1, c_two, 0, 4)
    for n, roles in enumerate(ARRIVALS):
        rest2.step(roles)
        if n == 2:
            own_up()
        elif n == 11:
            rest2.from_sibling(0)
            rest2.from_sibling(1)
            preact_grad(c_two, 0)
        elif n == 12:
            preact_grad(c_two, 2)
    rest2.from_sibling(2)
    rest2.from_sibling(3)
    preact_grad(c_two, 1)
    preact_grad(c_two, 3)
    send_up(1, x_two, 0, 4)
    opposite = lax.rem(z + 8, LANGS)
    in_up[opposite] = up(x_two, z)
    in_dn[opposite] = down(c_two, OWN_COLUMNS)

    pairs[...] = jnp.zeros_like(pairs)
    targets_t = tgt[...].T
    accept_t = acc[...].T

    for sign, inbox in ((1, in_dn), (0, in_up)):
        for number in range(2):

            @pl.loop(0, len(NEAR[number]))
            def _(k):
                source = lax.rem(z + LANGS - pick(k, NEAR[number]), LANGS)
                grad_copy(sign, number, k, source).wait_recv()

        @pl.loop(0, 2)
        def _(g):
            a = jnp.concatenate(
                [
                    inbox[:, pl.ds(pl.multiple_of(g * 128 + i * 16, 16), 16), :].reshape(256, DS)
                    for i in range(8)
                ],
                axis=1,
            )
            pairs[...] += lax.dot_general(
                a, a, (((1,), (1,)), ((), ())), preferred_element_type=jnp.float32
            )

    ri = lax.broadcasted_iota(jnp.int32, (256, 256), 0)
    ci = lax.broadcasted_iota(jnp.int32, (256, 256), 1)
    same = jnp.where(lax.rem(ri, 16) == lax.rem(ci, 16), pairs[...], 0.0)
    by_row = jnp.sum(same.reshape(LANGS, 16, 256), axis=1)
    li = lax.broadcasted_iota(jnp.int32, (256, 128), 0) // 16
    lj = lax.broadcasted_iota(jnp.int32, (256, 128), 1)
    select = (li == lj).astype(jnp.float32)
    st1[f] = jnp.dot(
        by_row, select, precision=lax.Precision.HIGHEST, preferred_element_type=jnp.float32
    )
    sends = exchange(st1, "fsdp", NF, f, s1_send, s1_recv)
    st2[y] = jnp.sum(st1[...], axis=0)
    sends += exchange(st2, "dp", NY, y, s2_send, s2_recv)
    st3[z] = jnp.sum(st2[...], axis=0)
    sends += exchange(st3, "lang", LANGS, z, s3_send, s3_recv)
    gram = jnp.sum(st3[...], axis=0)[:, :LANGS]

    weights, cos_pairs = vaccinate(gram, targets_t, accept_t)
    nt_out[...] = (1.0 - ema_rate) * tgt[...] + ema_rate * cos_pairs
    wv[...] = jnp.broadcast_to(weights, (LANGS, DS))

    for inbox, half in ((in_up, 0), (in_dn, 1)):

        @pl.loop(0, 4)
        def _(r):
            rows = pl.ds(pl.multiple_of(r * 64, 64), 64)
            total = jnp.zeros((64, DS), jnp.float32)
            for l in range(LANGS):
                total = total + wv[l : l + 1, :] * inbox[l, rows, :].astype(jnp.float32)
            if half == 0:
                comb[rows, :] = total
            else:
                dn_out[rows, :] = total

    up_out[...] = comb[...].T

    for copy in sends:
        copy.wait_send()

    for gather in (tokens, rest, tokens2, first2, rest2):
        for copy in gather.started:
            copy.wait_send()
    for n in range(4):
        first_leg(n).wait_send()
        second_leg(n).wait_send()
    for number in range(2):

        @pl.loop(0, len(NEAR[number]))
        def _(k):
            grad_copy(1, number, k, z).wait_send()
            grad_copy(0, number, k, z).wait_send()


def on_device(tokens, cotangent, lengths, up_weight, down_weight, targets, accept):
    bf16, f32 = jnp.bfloat16, jnp.float32
    dma = pltpu.SemaphoreType.DMA
    hbm = pl.BlockSpec(memory_space=pl.ANY)
    vmem = pl.BlockSpec(memory_space=pltpu.VMEM)
    return pl.pallas_call(
        kernel,
        out_shape=(
            jax.ShapeDtypeStruct((DS, HID), f32),
            jax.ShapeDtypeStruct((HID, DS), f32),
            jax.ShapeDtypeStruct((LANGS, LANGS), f32),
        ),
        in_specs=[hbm] * 7,
        out_specs=(vmem, vmem, vmem),
        scratch_shapes=[
            pltpu.VMEM((2, 4, 4, ROWS, D), bf16),
            pltpu.VMEM((2, 4, 4, ROWS, D), bf16),
            pltpu.VMEM((2, 4, 4, ROWS, D), bf16),
            pltpu.VMEM((2, 4, 4, ROWS, D), bf16),
            pltpu.VMEM((D, HID), bf16),
            pltpu.VMEM((HID, D), bf16),
            pltpu.VMEM((D, HID), bf16),
            pltpu.VMEM((LANGS, LANGS), f32),
            pltpu.VMEM((LANGS, LANGS), jnp.int32),
            pltpu.SMEM((1, 12), jnp.int32),
            pltpu.VMEM((LTOK, HID), f32),
            pltpu.VMEM((LTOK, HID), bf16),
            pltpu.VMEM((HID, LTOK), bf16),
            pltpu.VMEM((HID, LTOK), bf16),
            pltpu.VMEM((14, HID, DS), bf16),
            pltpu.VMEM((14, HID, DS), bf16),
            pltpu.VMEM((LANGS, HID, DS), bf16),
            pltpu.VMEM((LANGS, HID, DS), bf16),
            pltpu.VMEM((4, ROWS, HALF), bf16),
            pltpu.VMEM((256, 256), f32),
            pltpu.VMEM((NF, LANGS, 128), f32),
            pltpu.VMEM((NY, LANGS, 128), f32),
            pltpu.VMEM((LANGS, LANGS, 128), f32),
            pltpu.VMEM((LANGS, DS), f32),
            pltpu.VMEM((HID, DS), f32),
            dma((6,)), dma((LANGS,)), dma((360,)),
            dma((14,)), dma((14,)), dma((14,)), dma((14,)),
            dma((4,)), dma((4,)), dma((4,)), dma((4,)),
            dma((NF,)), dma((NF,)), dma((NY,)), dma((NY,)), dma((LANGS,)), dma((LANGS,)),
        ],
        compiler_params=pltpu.CompilerParams(
            collective_id=0, has_side_effects=True, vmem_limit_bytes=60 * 1024 * 1024
        ),
        cost_estimate=pl.CostEstimate(
            flops=4 * 2 * LTOK * D * HID, bytes_accessed=4 * 1024 * 1024, transcendentals=LTOK * HID
        ),
        name="vaccine_step",
    )(tokens, cotangent, lengths, up_weight, down_weight, targets, accept)


def solution(mesh):
    in_specs = (
        P("lang", ("dp", "fsdp"), None),
        P("lang", ("dp", "fsdp"), None),
        P("lang", None),
        P(None, ("dp", "fsdp")),
        P(("dp", "fsdp"), None),
        P(),
        P(),
    )
    out_specs = (P("lang", ("dp", "fsdp")), P(("dp", "fsdp"), "lang"), P())
    return jax.shard_map(
        on_device, mesh=mesh, in_specs=in_specs, out_specs=out_specs, check_vma=False
    )
```

```python
import functools

import jax
import jax.numpy as jnp
from jax import lax
from jax.experimental import pallas as pl
from jax.experimental.pallas import tpu as pltpu
from jax.sharding import PartitionSpec as P

D = 2048
FF = 8192
SEQ = 128
LTOK = 1536
LANGS = 16
NY = 4
NX = 4
NF = 8
ROWS = 48
HID = 256
DS = 128
HALF = D // 2

ema_rate = 0.01
clip_level = 0.25
MESH = pl.DeviceIdType.MESH

OFFSETS = (0, 3, 1, 2)
ARRIVALS = (
    (0, 1), (0, 2), (1, 0), (2, 0), (0, 3), (1, 1), (2, 1), (1, 2), (2, 2),
    (1, 3), (2, 3), (3, 0), (3, 1), (3, 2), (3, 3),
)
EARLY = 6


class Plane:
    def __init__(self, x, y, core):
        self.x, self.y, self.core = x, y, core
        self.next = {}
        for ring in (0, 1):
            for step in (1, 3):
                dx = jnp.where(core == ring, step, 0)
                self.next[ring, step] = {
                    "dp": lax.rem(y + step - dx, 4),
                    "fsdp": lax.rem(x + dx, 4) * 2 + core,
                }
        self.sibling = {"fsdp": x * 2 + (1 - core)}


class Gather:
    def __init__(self, plane, own, buf, start, width, send, recv, sib_send, sib_recv):
        self.plane, self.own, self.buf, self.start, self.width = plane, own, buf, start, width
        self.send, self.recv, self.sib_send, self.sib_recv = send, recv, sib_send, sib_recv
        self.started = []

    def part(self, roles, half):
        if half is None:
            return self.buf.at[0, roles[0], roles[1], :, pl.ds(self.start, self.width)]
        width = self.width // 2
        return self.buf.at[0, roles[0], roles[1], :, pl.ds(self.start + half * width, width)]

    def copy(self, roles, half, ring, step, send_index, there):
        src = self.own if roles == (0, 0) else self.part(roles, half)
        copy = pltpu.make_async_remote_copy(
            src_ref=src,
            dst_ref=self.part(there, half),
            send_sem=self.send.at[send_index],
            recv_sem=self.recv.at[2 * (4 * there[0] + there[1]) + (half or 0)],
            device_id=self.plane.next[ring, step],
            device_id_type=MESH,
        )
        copy.start()
        self.started.append(copy)

    def sibling_copy(self, second):
        cols = pl.ds(self.start, self.width)
        return pltpu.make_async_remote_copy(
            src_ref=self.buf.at[0, second, :, :, cols],
            dst_ref=self.buf.at[1, second, :, :, cols],
            send_sem=self.sib_send.at[second],
            recv_sem=self.sib_recv.at[second],
            device_id=self.plane.sibling,
            device_id_type=MESH,
        )

    def to_sibling(self, second):
        copy = self.sibling_copy(second)
        copy.start()
        self.started.append(copy)

    def from_sibling(self, second):
        self.sibling_copy(second).wait_recv()

    def ready(self, roles):
        second, first = roles
        base = 4 + 4 * first
        if second == 0:
            if first == 0:
                self.copy(roles, None, 0, 1, 0, (0, 1))
                self.copy(roles, None, 0, 3, 1, (0, 2))
            elif first == 1:
                self.copy(roles, 0, 0, 1, 2, (0, 3))
            elif first == 2:
                self.copy(roles, 1, 0, 3, 3, (0, 3))
            self.copy(roles, None, 1, 1, base, (1, first))
            self.copy(roles, None, 1, 3, base + 1, (2, first))
        elif second == 1:
            self.copy(roles, 0, 1, 1, base + 2, (3, first))
        elif second == 2:
            self.copy(roles, 1, 1, 3, base + 3, (3, first))

    def arrive(self, roles):
        for half in (0, 1) if roles[0] == 3 or roles == (0, 3) else (None,):
            ref = self.part(roles, half)
            pltpu.make_async_remote_copy(
                src_ref=ref,
                dst_ref=ref,
                send_sem=self.send.at[0],
                recv_sem=self.recv.at[2 * (4 * roles[0] + roles[1]) + (half or 0)],
                device_id=self.plane.next[0, 1],
                device_id_type=MESH,
            ).wait_recv()

    def step(self, roles):
        self.arrive(roles)
        self.ready(roles)
        if roles in ((0, 3), (1, 3), (2, 3), (3, 3)):
            self.to_sibling(roles[0])


NEAR = ((5, 11, 12, 4, 13, 3, 2, 14, 1, 15), (2, 14, 1, 15))
COLUMN_ORDER = (2, 14, 1, 15, 0, 3, 12, 5)
OWN_COLUMNS = 4
COLUMN_OF = {d: i for i, d in enumerate(COLUMN_ORDER + tuple((d + 8) % 16 for d in COLUMN_ORDER))}


def pick(k, values):
    if isinstance(k, int):
        return values[k]
    found = jnp.int32(values[-1])
    for i, value in enumerate(values[:-1]):
        found = jnp.where(k == i, value, found)
    return found


def exchange(buf, axis, count, me, send, recv):
    copies = []
    for r in range(1, count):
        copy = pltpu.make_async_remote_copy(
            src_ref=buf.at[me],
            dst_ref=buf.at[me],
            send_sem=send.at[r],
            recv_sem=recv.at[r],
            device_id={axis: lax.rem(me + r, count)},
            device_id_type=MESH,
        )
        copy.start()
        copies.append(copy)
    for r in range(1, count):
        ref = buf.at[lax.rem(me + count - r, count)]
        pltpu.make_async_remote_copy(
            src_ref=ref,
            dst_ref=ref,
            send_sem=send.at[r],
            recv_sem=recv.at[r],
            device_id={axis: lax.rem(me + r, count)},
            device_id_type=MESH,
        ).wait_recv()
    return copies


def vaccinate(gram, targets_t, accept_t):
    rows = lax.broadcasted_iota(jnp.int32, (LANGS, LANGS), 0)
    cols = lax.broadcasted_iota(jnp.int32, (LANGS, LANGS), 1)
    identity = (rows == cols).astype(jnp.float32)
    roots = jnp.sqrt(1.0 - targets_t * targets_t)
    diag_col = jnp.sum(gram * identity, axis=1, keepdims=True)
    diag_row = jnp.sum(gram * identity, axis=0, keepdims=True)
    cos_pairs = gram / jnp.sqrt(diag_col * diag_row)
    inverse = 1.0 / jnp.sqrt(diag_col)
    scale = inverse / roots
    allowed = accept_t.astype(jnp.float32) * (1.0 - identity)
    coeffs, product = identity, gram
    for j in range(LANGS):
        norm_sq = jnp.sum(product * coeffs, axis=0, keepdims=True)
        over_norm = lax.rsqrt(norm_sq)
        cosine = product[j : j + 1, :] * inverse[j : j + 1, :] * over_norm
        sine = jnp.sqrt(jnp.maximum(1.0 - cosine * cosine, 0.0))
        step = (
            (norm_sq * over_norm)
            * (targets_t[j : j + 1, :] * sine - cosine * roots[j : j + 1, :])
            * scale[j : j + 1, :]
        )
        step = jnp.where(allowed[j : j + 1, :] > 0.5, step, 0.0)
        coeffs = jnp.where(rows == j, coeffs + step, coeffs)
        product = product + gram[:, j : j + 1] * step
    weights = jnp.sum(coeffs, axis=1, keepdims=True)
    along = jnp.sum(product, axis=1, keepdims=True)
    quad = jnp.sum(weights * along, axis=0, keepdims=True)
    mean_square = jnp.maximum(quad, 0.0) / (2.0 * D * FF)
    factor = jnp.minimum(1.0, clip_level / jnp.sqrt(mean_square + 1e-06))
    return weights * factor, cos_pairs


def kernel(
    tok_ref, cot_ref, len_hbm, wup_hbm, wdn_hbm, tgt_hbm, acc_hbm,
    up_out, dn_out, nt_out,
    x_buf, c_buf, x_two, c_two, wup, wdn, wdn_t, tgt, acc, lens, v_buf, hp, h_t, p_t,
    out_dn, out_up, in_dn, in_up, relay, pairs, st1, st2, st3, wv, comb,
    local_sem, cols_sem, sems,
    d_send, d_recv, u_send, u_recv, i_send, i_recv, r_send, r_recv,
    s1_send, s1_recv, s2_send, s2_recv, s3_send, s3_recv,
):
    z, y, f = lax.axis_index("lang"), lax.axis_index("dp"), lax.axis_index("fsdp")
    x, core = f // 2, lax.rem(f, 2)

    barrier = pltpu.get_barrier_semaphore()
    for axis, count, me in (("fsdp", NF, f), ("dp", NY, y), ("lang", LANGS, z)):
        for r in range(1, count):
            pl.semaphore_signal(
                barrier, inc=1, device_id={axis: lax.rem(me + r, count)}, device_id_type=MESH
            )

    def owner(number, k):
        return lax.rem(z + pick(k, NEAR[number]), LANGS)

    def columns(block):
        return pl.ds(pl.multiple_of(block * DS, DS), DS)

    def source_columns(k):
        return columns(lax.rem(z + COLUMN_ORDER[k % 8] + 8 * (k // 8), LANGS))

    plane = Plane(x, y, core)
    tok, cot = tok_ref.at[0], cot_ref.at[0]
    cot_copies = [
        pltpu.make_async_copy(
            cot.at[:, source_columns(k)], c_buf.at[0, 0, 0, :, pl.ds(k * DS, DS)], cols_sem.at[k]
        )
        for k in range(LANGS)
    ]
    lens_copy = pltpu.make_async_copy(len_hbm, lens, local_sem.at[5])
    local = [
        pltpu.make_async_copy(tok, x_buf.at[0, 0, 0], local_sem.at[0]),
        pltpu.make_async_copy(wdn_hbm, wdn, local_sem.at[1]),
        pltpu.make_async_copy(wup_hbm, wup, local_sem.at[2]),
        pltpu.make_async_copy(tgt_hbm, tgt, local_sem.at[3]),
        pltpu.make_async_copy(acc_hbm, acc, local_sem.at[4]),
    ]
    lens_copy.start()
    for copy in cot_copies + local:
        copy.start()

    early = EARLY * DS

    def gathers(number, own, x_ref, c_ref):
        start_rest = early if number else 0
        made = []
        for n, (src, buf, start, width) in enumerate(
            (
                (own, x_ref, 0, D),
                (c_ref.at[0, 0, 0, :, pl.ds(0, early)], c_ref, 0, early),
                (c_ref.at[0, 0, 0, :, pl.ds(start_rest, D - start_rest)], c_ref, start_rest, D - start_rest),
            )
        ):
            base = (3 * number + n) * 60
            parts = [sems.at[pl.ds(base + a, b)] for a, b in ((0, 20), (20, 32), (52, 4), (56, 4))]
            made.append(Gather(plane, src, buf, start, width, *parts))
        return made

    tokens, _, rest = gathers(0, tok, x_buf, c_buf)
    tokens2, first2, rest2 = gathers(1, x_two.at[0, 0, 0], x_two, c_two)

    def remote(src, dst, send, recv, to):
        return pltpu.make_async_remote_copy(
            src_ref=src, dst_ref=dst, send_sem=send, recv_sem=recv, device_id={"lang": to}, device_id_type=MESH
        )

    def columns_half(ref, n):
        return ref.at[:, pl.ds(n * HALF, HALF)]

    def leg_to(n):
        return lax.rem(z + (4 if n % 2 == 0 else 12), LANGS)

    def first_leg(n):
        src = columns_half(tok if n < 2 else c_buf.at[0, 0, 0], n % 2)
        return remote(src, relay.at[n], i_send.at[n], i_recv.at[n], leg_to(n))

    def second_leg(n):
        dst = columns_half(x_two.at[0, 0, 0], n) if n < 2 else columns_half(c_two.at[0, 0, 0], 3 - n)
        return remote(relay.at[n], dst, r_send.at[n], r_recv.at[n], leg_to(n))

    def forward(n):
        first_leg(n).wait_recv()
        second_leg(n).start()

    pl.semaphore_wait(barrier, (NF - 1) + (NY - 1) + (LANGS - 1))
    tokens.ready((0, 0))
    first_leg(0).start()
    first_leg(1).start()

    lens_copy.wait()
    for copy in cot_copies:
        copy.wait()
    token = (y * NF + x * 2 + core) * ROWS
    slot = token // SEQ
    here, after = lens[0, slot], lens[0, jnp.minimum(slot + 1, 11)]
    place = lax.broadcasted_iota(jnp.int32, (ROWS, D), 0) + (token - slot * SEQ)
    kept = place < jnp.where(place < SEQ, here, after + SEQ)
    mine = c_buf[0, 0, 0].astype(jnp.float32)
    c_buf[0, 0, 0] = jnp.where(kept, mine, 0.0).astype(jnp.bfloat16)
    first_leg(2).start()
    first_leg(3).start()

    for copy in local:
        copy.wait()

    @pl.loop(0, 8)
    def _(k):
        low = lax.rem(z + pick(k, COLUMN_ORDER), LANGS)
        wdn_t[pl.ds(pl.multiple_of(k * DS, DS), DS), :] = wdn[:, columns(low)].T
        high = lax.rem(low + 8, LANGS)
        wdn_t[pl.ds(pl.multiple_of(HALF + k * DS, DS), DS), :] = wdn[:, columns(high)].T

    def activate(x_ref, which, second):
        base = (which * 4 + second) * 192
        v_buf[pl.ds(base, 192), :] = jnp.dot(
            x_ref[which, second].reshape(192, D), wup[...], preferred_element_type=jnp.float32
        )

        @pl.loop(0, 4)
        def _(i):
            rows = pl.ds(pl.multiple_of(base + i * ROWS, 16), ROWS)
            v = v_buf[rows, :]
            k = 0.7978845608028654
            sq = v * v
            t = jnp.tanh(k * (v + 0.044715 * (sq * v)))
            cdf = 0.5 * (1.0 + t)
            v_buf[rows, :] = cdf + 0.5 * v * (1.0 - t * t) * (k * (1.0 + 3.0 * 0.044715 * sq))
            hp[rows, :] = (v * cdf).astype(jnp.bfloat16)

    def turn(dst, start, count):
        @pl.loop(start, start + count)
        def _(i):
            part = pl.ds(pl.multiple_of(i * 128, 128), 128)
            dst[:, part] = hp[part, :].T

    def product(grads_t, rows_ref, *blocks):
        cols = [rows_ref[:, :, :, :, columns(b)].reshape(LTOK, DS) for b in blocks]
        return jnp.dot(
            grads_t[...],
            cols[0] if len(cols) == 1 else jnp.concatenate(cols, axis=1),
            preferred_element_type=jnp.float32,
        ).astype(jnp.bfloat16)

    def down(c_ref, *places):
        return product(h_t, c_ref, *places)

    def up(x_ref, *blocks):
        return product(p_t, x_ref, *blocks)

    def grad_copy(sign, number, k, source):
        out, inbox = (out_dn, in_dn) if sign else (out_up, in_up)
        send, recv = (d_send, d_recv) if sign else (u_send, u_recv)
        index = number * len(NEAR[0]) + k
        return remote(
            out.at[index],
            inbox.at[lax.rem(source + 8 * number, LANGS)],
            send.at[index],
            recv.at[index],
            owner(number, k),
        )

    def send_down(number, c_ref, start, stop):
        places = tuple(COLUMN_OF[d] for d in NEAR[number])

        @pl.loop(start, stop)
        def _(pair):
            k = 2 * pair
            both = down(c_ref, pick(k, places), pick(k + 1, places))
            for n in range(2):
                out_dn[number * len(NEAR[0]) + k + n] = both[:, n * DS : (n + 1) * DS]
                grad_copy(1, number, k + n, z).start()

    def send_up(number, x_ref, start, stop):
        @pl.loop(start, stop)
        def _(pair):
            k = 2 * pair
            both = up(x_ref, owner(number, k), owner(number, k + 1))
            for n in range(2):
                out_up[number * len(NEAR[0]) + k + n] = both[:, n * DS : (n + 1) * DS]
                grad_copy(0, number, k + n, z).start()

    def preact_grad_group(c_ref, which, second):
        hg = jnp.dot(
            c_ref[which, second].reshape(192, D), wdn_t[...], preferred_element_type=jnp.float32
        )
        rows = pl.ds((which * 4 + second) * 192, 192)
        hp[rows, :] = (hg * v_buf[rows, :]).astype(jnp.bfloat16)

    def preact_grad(c_ref, pair):
        which, second = pair // 2, 2 * (pair % 2)
        hg = jnp.dot(
            c_ref[which, second : second + 2].reshape(384, D), wdn_t[...], preferred_element_type=jnp.float32
        )
        rows = pl.ds(pair * 384, 384)
        hp[rows, :] = (hg * v_buf[rows, :]).astype(jnp.bfloat16)
        turn(p_t, pair * 3, 3)

    def with_tokens(gather_x, gather_c, x_ref, extra, following):
        for n, roles in enumerate(ARRIVALS):
            gather_x.step(roles)
            if gather_c is not None:
                gather_c.step(roles)
            for piece in extra.get(n, ()):
                piece()
            if n == 8:
                gather_x.from_sibling(0)
                activate(x_ref, 0, 0)
            elif n == 9:
                activate(x_ref, 1, 0)
            elif n == 10:
                activate(x_ref, 0, 1)
            elif n == 11:
                gather_x.from_sibling(1)
                activate(x_ref, 1, 1)
            elif n == 12:
                activate(x_ref, 0, 2)
            elif n == 13:
                gather_x.from_sibling(2)
                activate(x_ref, 1, 2)
        following.step(ARRIVALS[0])
        activate(x_ref, 0, 3)
        following.step(ARRIVALS[1])
        turn(h_t, 0, 3)
        turn(h_t, 6, 3)
        following.step(ARRIVALS[2])
        gather_x.from_sibling(3)
        activate(x_ref, 1, 3)
        following.step(ARRIVALS[3])
        turn(h_t, 3, 3)
        turn(h_t, 9, 3)
        following.step(ARRIVALS[4])
        if gather_c is not None:
            for second in range(4):
                gather_c.from_sibling(second)

    def begin_two():
        second_leg(0).wait_recv()
        second_leg(1).wait_recv()
        tokens2.ready((0, 0))

    with_tokens(
        tokens, None, x_buf,
        {
            4: [lambda: rest.ready((0, 0))],
            5: [lambda: forward(0), lambda: forward(1)],
            10: [lambda: forward(2), lambda: forward(3)],
        },
        rest,
    )
    for n, roles in enumerate(ARRIVALS):
        if n < 5:
            continue
        rest.step(roles)
        if n == 8:
            begin_two()
        elif n == 11:
            rest.from_sibling(0)
            rest.from_sibling(1)
            preact_grad(c_buf, 0)
        elif n == 12:
            preact_grad(c_buf, 2)
    second_leg(2).wait_recv()
    second_leg(3).wait_recv()
    first2.ready((0, 0))
    rest.from_sibling(2)
    rest.from_sibling(3)

    def own_down():
        in_dn[z] = down(c_buf, OWN_COLUMNS)

    def own_up():
        in_up[z] = up(x_buf, z)

    with_tokens(
        tokens2, first2, x_two,
        {
            0: [functools.partial(send_down, 0, c_buf, 0, 2)],
            1: [functools.partial(send_down, 0, c_buf, 2, 4)],
            2: [functools.partial(send_down, 0, c_buf, 4, 5), own_down],
            3: [functools.partial(preact_grad, c_buf, 1)],
            4: [functools.partial(preact_grad, c_buf, 3), lambda: rest2.ready((0, 0))],
            5: [functools.partial(send_up, 0, x_buf, 0, 2)],
            6: [functools.partial(send_up, 0, x_buf, 2, 4)],
            7: [functools.partial(send_up, 0, x_buf, 4, 5)],
        },
        rest2,
    )
    send_down(1, c_two, 0, 2)
    for n, roles in enumerate(ARRIVALS):
        if n < 5:
            continue
        rest2.step(roles)
        if n == 6:
            own_up()
        elif n == 11:
            rest2.from_sibling(0)
            rest2.from_sibling(1)
            preact_grad(c_two, 0)
        elif n == 12:
            preact_grad(c_two, 2)
        elif n == 13:
            rest2.from_sibling(2)
            preact_grad_group(c_two, 0, 2)
        elif n == 14:
            preact_grad_group(c_two, 1, 2)
    preact_grad_group(c_two, 0, 3)
    turn(p_t, 3, 3)
    rest2.from_sibling(3)
    preact_grad_group(c_two, 1, 3)
    turn(p_t, 9, 3)
    send_up(1, x_two, 0, 2)
    opposite = lax.rem(z + 8, LANGS)
    in_up[opposite] = up(x_two, z)
    in_dn[opposite] = down(c_two, OWN_COLUMNS)

    pairs[...] = jnp.zeros_like(pairs)
    targets_t = tgt[...].T
    accept_t = acc[...].T

    for sign, inbox in ((1, in_dn), (0, in_up)):
        for number in range(2):

            @pl.loop(0, len(NEAR[number]))
            def _(k):
                source = lax.rem(z + LANGS - pick(k, NEAR[number]), LANGS)
                grad_copy(sign, number, k, source).wait_recv()

        @pl.loop(0, 2)
        def _(g):
            a = jnp.concatenate(
                [
                    inbox[:, pl.ds(pl.multiple_of(g * 128 + i * 16, 16), 16), :].reshape(256, DS)
                    for i in range(8)
                ],
                axis=1,
            )
            pairs[...] += lax.dot_general(
                a, a, (((1,), (1,)), ((), ())), preferred_element_type=jnp.float32
            )

    ri = lax.broadcasted_iota(jnp.int32, (256, 256), 0)
    ci = lax.broadcasted_iota(jnp.int32, (256, 256), 1)
    same = jnp.where(lax.rem(ri, 16) == lax.rem(ci, 16), pairs[...], 0.0)
    by_row = jnp.sum(same.reshape(LANGS, 16, 256), axis=1)
    li = lax.broadcasted_iota(jnp.int32, (256, 128), 0) // 16
    lj = lax.broadcasted_iota(jnp.int32, (256, 128), 1)
    select = (li == lj).astype(jnp.float32)
    st1[f] = jnp.dot(
        by_row, select, precision=lax.Precision.HIGHEST, preferred_element_type=jnp.float32
    )
    sends = exchange(st1, "fsdp", NF, f, s1_send, s1_recv)
    st2[y] = jnp.sum(st1[...], axis=0)
    sends += exchange(st2, "dp", NY, y, s2_send, s2_recv)
    st3[z] = jnp.sum(st2[...], axis=0)
    sends += exchange(st3, "lang", LANGS, z, s3_send, s3_recv)
    gram = jnp.sum(st3[...], axis=0)[:, :LANGS]

    weights, cos_pairs = vaccinate(gram, targets_t, accept_t)
    nt_out[...] = (1.0 - ema_rate) * tgt[...] + ema_rate * cos_pairs
    wv[...] = jnp.broadcast_to(weights, (LANGS, DS))

    for inbox, half in ((in_up, 0), (in_dn, 1)):

        @pl.loop(0, 4)
        def _(r):
            rows = pl.ds(pl.multiple_of(r * 64, 64), 64)
            total = jnp.zeros((64, DS), jnp.float32)
            for l in range(LANGS):
                total = total + wv[l : l + 1, :] * inbox[l, rows, :].astype(jnp.float32)
            if half == 0:
                comb[rows, :] = total
            else:
                dn_out[rows, :] = total

    up_out[...] = comb[...].T

    for copy in sends:
        copy.wait_send()

    for gather in (tokens, rest, tokens2, first2, rest2):
        for copy in gather.started:
            copy.wait_send()
    for n in range(4):
        first_leg(n).wait_send()
        second_leg(n).wait_send()
    for number in range(2):

        @pl.loop(0, len(NEAR[number]))
        def _(k):
            grad_copy(1, number, k, z).wait_send()
            grad_copy(0, number, k, z).wait_send()


def on_device(tokens, cotangent, lengths, up_weight, down_weight, targets, accept):
    bf16, f32 = jnp.bfloat16, jnp.float32
    dma = pltpu.SemaphoreType.DMA
    hbm = pl.BlockSpec(memory_space=pl.ANY)
    vmem = pl.BlockSpec(memory_space=pltpu.VMEM)
    return pl.pallas_call(
        kernel,
        out_shape=(
            jax.ShapeDtypeStruct((DS, HID), f32),
            jax.ShapeDtypeStruct((HID, DS), f32),
            jax.ShapeDtypeStruct((LANGS, LANGS), f32),
        ),
        in_specs=[hbm] * 7,
        out_specs=(vmem, vmem, vmem),
        scratch_shapes=[
            pltpu.VMEM((2, 4, 4, ROWS, D), bf16),
            pltpu.VMEM((2, 4, 4, ROWS, D), bf16),
            pltpu.VMEM((2, 4, 4, ROWS, D), bf16),
            pltpu.VMEM((2, 4, 4, ROWS, D), bf16),
            pltpu.VMEM((D, HID), bf16),
            pltpu.VMEM((HID, D), bf16),
            pltpu.VMEM((D, HID), bf16),
            pltpu.VMEM((LANGS, LANGS), f32),
            pltpu.VMEM((LANGS, LANGS), jnp.int32),
            pltpu.SMEM((1, 12), jnp.int32),
            pltpu.VMEM((LTOK, HID), f32),
            pltpu.VMEM((LTOK, HID), bf16),
            pltpu.VMEM((HID, LTOK), bf16),
            pltpu.VMEM((HID, LTOK), bf16),
            pltpu.VMEM((14, HID, DS), bf16),
            pltpu.VMEM((14, HID, DS), bf16),
            pltpu.VMEM((LANGS, HID, DS), bf16),
            pltpu.VMEM((LANGS, HID, DS), bf16),
            pltpu.VMEM((4, ROWS, HALF), bf16),
            pltpu.VMEM((256, 256), f32),
            pltpu.VMEM((NF, LANGS, 128), f32),
            pltpu.VMEM((NY, LANGS, 128), f32),
            pltpu.VMEM((LANGS, LANGS, 128), f32),
            pltpu.VMEM((LANGS, DS), f32),
            pltpu.VMEM((HID, DS), f32),
            dma((6,)), dma((LANGS,)), dma((360,)),
            dma((14,)), dma((14,)), dma((14,)), dma((14,)),
            dma((4,)), dma((4,)), dma((4,)), dma((4,)),
            dma((NF,)), dma((NF,)), dma((NY,)), dma((NY,)), dma((LANGS,)), dma((LANGS,)),
        ],
        compiler_params=pltpu.CompilerParams(
            collective_id=0, has_side_effects=True, vmem_limit_bytes=60 * 1024 * 1024
        ),
        cost_estimate=pl.CostEstimate(
            flops=4 * 2 * LTOK * D * HID, bytes_accessed=4 * 1024 * 1024, transcendentals=LTOK * HID
        ),
        name="vaccine_step",
    )(tokens, cotangent, lengths, up_weight, down_weight, targets, accept)


def solution(mesh):
    in_specs = (
        P("lang", ("dp", "fsdp"), None),
        P("lang", ("dp", "fsdp"), None),
        P("lang", None),
        P(None, ("dp", "fsdp")),
        P(("dp", "fsdp"), None),
        P(),
        P(),
    )
    out_specs = (P("lang", ("dp", "fsdp")), P(("dp", "fsdp"), "lang"), P())
    return jax.shard_map(
        on_device, mesh=mesh, in_specs=in_specs, out_specs=out_specs, check_vma=False
    )
```

```python
import functools

import jax
import jax.numpy as jnp
from jax import lax
from jax.experimental import pallas as pl
from jax.experimental.pallas import tpu as pltpu
from jax.sharding import PartitionSpec as P

D = 2048
FF = 8192
SEQ = 128
LTOK = 1536
LANGS = 16
NY = 4
NX = 4
NF = 8
ROWS = 48
HID = 256
DS = 128
HALF = D // 2

ema_rate = 0.01
clip_level = 0.25
MESH = pl.DeviceIdType.MESH

OFFSETS = (0, 3, 1, 2)
ARRIVALS = (
    (0, 1), (0, 2), (1, 0), (2, 0), (0, 3), (1, 1), (2, 1), (1, 2), (2, 2),
    (1, 3), (2, 3), (3, 0), (3, 1), (3, 2), (3, 3),
)
EARLY = 6


class Plane:
    def __init__(self, x, y, core):
        self.x, self.y, self.core = x, y, core
        self.next = {}
        for ring in (0, 1):
            for step in (1, 3):
                dx = jnp.where(core == ring, step, 0)
                self.next[ring, step] = {
                    "dp": lax.rem(y + step - dx, 4),
                    "fsdp": lax.rem(x + dx, 4) * 2 + core,
                }
        self.sibling = {"fsdp": x * 2 + (1 - core)}


class Gather:
    def __init__(self, plane, own, buf, start, width, send, recv, sib_send, sib_recv):
        self.plane, self.own, self.buf, self.start, self.width = plane, own, buf, start, width
        self.send, self.recv, self.sib_send, self.sib_recv = send, recv, sib_send, sib_recv
        self.started = []

    def part(self, roles, half):
        if half is None:
            return self.buf.at[0, roles[0], roles[1], :, pl.ds(self.start, self.width)]
        width = self.width // 2
        return self.buf.at[0, roles[0], roles[1], :, pl.ds(self.start + half * width, width)]

    def copy(self, roles, half, ring, step, send_index, there):
        src = self.own if roles == (0, 0) else self.part(roles, half)
        copy = pltpu.make_async_remote_copy(
            src_ref=src,
            dst_ref=self.part(there, half),
            send_sem=self.send.at[send_index],
            recv_sem=self.recv.at[2 * (4 * there[0] + there[1]) + (half or 0)],
            device_id=self.plane.next[ring, step],
            device_id_type=MESH,
        )
        copy.start()
        self.started.append(copy)

    def sibling_copy(self, second):
        cols = pl.ds(self.start, self.width)
        return pltpu.make_async_remote_copy(
            src_ref=self.buf.at[0, second, :, :, cols],
            dst_ref=self.buf.at[1, second, :, :, cols],
            send_sem=self.sib_send.at[second],
            recv_sem=self.sib_recv.at[second],
            device_id=self.plane.sibling,
            device_id_type=MESH,
        )

    def to_sibling(self, second):
        copy = self.sibling_copy(second)
        copy.start()
        self.started.append(copy)

    def from_sibling(self, second):
        self.sibling_copy(second).wait_recv()

    def ready(self, roles):
        second, first = roles
        base = 4 + 4 * first
        if second == 0:
            if first == 0:
                self.copy(roles, None, 0, 1, 0, (0, 1))
                self.copy(roles, None, 0, 3, 1, (0, 2))
            elif first == 1:
                self.copy(roles, 0, 0, 1, 2, (0, 3))
            elif first == 2:
                self.copy(roles, 1, 0, 3, 3, (0, 3))
            self.copy(roles, None, 1, 1, base, (1, first))
            self.copy(roles, None, 1, 3, base + 1, (2, first))
        elif second == 1:
            self.copy(roles, 0, 1, 1, base + 2, (3, first))
        elif second == 2:
            self.copy(roles, 1, 1, 3, base + 3, (3, first))

    def arrive(self, roles):
        for half in (0, 1) if roles[0] == 3 or roles == (0, 3) else (None,):
            ref = self.part(roles, half)
            pltpu.make_async_remote_copy(
                src_ref=ref,
                dst_ref=ref,
                send_sem=self.send.at[0],
                recv_sem=self.recv.at[2 * (4 * roles[0] + roles[1]) + (half or 0)],
                device_id=self.plane.next[0, 1],
                device_id_type=MESH,
            ).wait_recv()

    def step(self, roles):
        self.arrive(roles)
        self.ready(roles)
        if roles in ((0, 3), (1, 3), (2, 3), (3, 3)):
            self.to_sibling(roles[0])


NEAR = ((5, 11, 12, 4, 13, 3, 2, 14, 1, 15), (2, 14, 1, 15))
COLUMN_ORDER = (2, 14, 1, 15, 0, 3, 12, 5)
OWN_COLUMNS = 4
COLUMN_OF = {d: i for i, d in enumerate(COLUMN_ORDER + tuple((d + 8) % 16 for d in COLUMN_ORDER))}


def pick(k, values):
    if isinstance(k, int):
        return values[k]
    found = jnp.int32(values[-1])
    for i, value in enumerate(values[:-1]):
        found = jnp.where(k == i, value, found)
    return found


def exchange(buf, axis, count, me, send, recv):
    copies = []
    for r in range(1, count):
        copy = pltpu.make_async_remote_copy(
            src_ref=buf.at[me],
            dst_ref=buf.at[me],
            send_sem=send.at[r],
            recv_sem=recv.at[r],
            device_id={axis: lax.rem(me + r, count)},
            device_id_type=MESH,
        )
        copy.start()
        copies.append(copy)
    for r in range(1, count):
        ref = buf.at[lax.rem(me + count - r, count)]
        pltpu.make_async_remote_copy(
            src_ref=ref,
            dst_ref=ref,
            send_sem=send.at[r],
            recv_sem=recv.at[r],
            device_id={axis: lax.rem(me + r, count)},
            device_id_type=MESH,
        ).wait_recv()
    return copies


def vaccinate(gram, targets_t, accept_t):
    rows = lax.broadcasted_iota(jnp.int32, (LANGS, LANGS), 0)
    cols = lax.broadcasted_iota(jnp.int32, (LANGS, LANGS), 1)
    identity = (rows == cols).astype(jnp.float32)
    roots = jnp.sqrt(1.0 - targets_t * targets_t)
    diag_col = jnp.sum(gram * identity, axis=1, keepdims=True)
    diag_row = jnp.sum(gram * identity, axis=0, keepdims=True)
    cos_pairs = gram / jnp.sqrt(diag_col * diag_row)
    inverse = 1.0 / jnp.sqrt(diag_col)
    scale = inverse / roots
    allowed = accept_t.astype(jnp.float32) * (1.0 - identity)
    coeffs, product = identity, gram
    for j in range(LANGS):
        norm_sq = jnp.sum(product * coeffs, axis=0, keepdims=True)
        over_norm = lax.rsqrt(norm_sq)
        cosine = product[j : j + 1, :] * inverse[j : j + 1, :] * over_norm
        sine = jnp.sqrt(jnp.maximum(1.0 - cosine * cosine, 0.0))
        step = (
            (norm_sq * over_norm)
            * (targets_t[j : j + 1, :] * sine - cosine * roots[j : j + 1, :])
            * scale[j : j + 1, :]
        )
        step = jnp.where(allowed[j : j + 1, :] > 0.5, step, 0.0)
        coeffs = jnp.where(rows == j, coeffs + step, coeffs)
        product = product + gram[:, j : j + 1] * step
    weights = jnp.sum(coeffs, axis=1, keepdims=True)
    along = jnp.sum(product, axis=1, keepdims=True)
    quad = jnp.sum(weights * along, axis=0, keepdims=True)
    mean_square = jnp.maximum(quad, 0.0) / (2.0 * D * FF)
    factor = jnp.minimum(1.0, clip_level / jnp.sqrt(mean_square + 1e-06))
    return weights * factor, cos_pairs


def kernel(
    tok_ref, cot_ref, len_hbm, wup_hbm, wdn_hbm, tgt_hbm, acc_hbm,
    up_out, dn_out, nt_out,
    x_buf, c_buf, x_two, c_two, wup, wdn, wdn_t, tgt, acc, lens, v_buf, hp, h_t, p_t,
    out_dn, out_up, in_dn, in_up, relay, pairs, st1, st2, st3, wv, comb,
    local_sem, cols_sem, sems,
    d_send, d_recv, u_send, u_recv, i_send, i_recv, r_send, r_recv,
    s1_send, s1_recv, s2_send, s2_recv, s3_send, s3_recv,
):
    z, y, f = lax.axis_index("lang"), lax.axis_index("dp"), lax.axis_index("fsdp")
    x, core = f // 2, lax.rem(f, 2)

    barrier = pltpu.get_barrier_semaphore()
    for axis, count, me in (("fsdp", NF, f), ("dp", NY, y), ("lang", LANGS, z)):
        for r in range(1, count):
            pl.semaphore_signal(
                barrier, inc=1, device_id={axis: lax.rem(me + r, count)}, device_id_type=MESH
            )

    def owner(number, k):
        return lax.rem(z + pick(k, NEAR[number]), LANGS)

    def columns(block):
        return pl.ds(pl.multiple_of(block * DS, DS), DS)

    def source_columns(k):
        return columns(lax.rem(z + COLUMN_ORDER[k % 8] + 8 * (k // 8), LANGS))

    plane = Plane(x, y, core)
    tok, cot = tok_ref.at[0], cot_ref.at[0]
    cot_copies = [
        pltpu.make_async_copy(
            cot.at[:, source_columns(k)], c_buf.at[0, 0, 0, :, pl.ds(k * DS, DS)], cols_sem.at[k]
        )
        for k in range(LANGS)
    ]
    lens_copy = pltpu.make_async_copy(len_hbm, lens, local_sem.at[5])
    local = [
        pltpu.make_async_copy(tok, x_buf.at[0, 0, 0], local_sem.at[0]),
        pltpu.make_async_copy(wdn_hbm, wdn, local_sem.at[1]),
        pltpu.make_async_copy(wup_hbm, wup, local_sem.at[2]),
        pltpu.make_async_copy(tgt_hbm, tgt, local_sem.at[3]),
        pltpu.make_async_copy(acc_hbm, acc, local_sem.at[4]),
    ]
    lens_copy.start()
    for copy in cot_copies + local:
        copy.start()

    early = EARLY * DS

    def gathers(number, own, x_ref, c_ref):
        start_rest = early if number else 0
        made = []
        for n, (src, buf, start, width) in enumerate(
            (
                (own, x_ref, 0, D),
                (c_ref.at[0, 0, 0, :, pl.ds(0, early)], c_ref, 0, early),
                (c_ref.at[0, 0, 0, :, pl.ds(start_rest, D - start_rest)], c_ref, start_rest, D - start_rest),
            )
        ):
            base = (3 * number + n) * 60
            parts = [sems.at[pl.ds(base + a, b)] for a, b in ((0, 20), (20, 32), (52, 4), (56, 4))]
            made.append(Gather(plane, src, buf, start, width, *parts))
        return made

    tokens, _, rest = gathers(0, tok, x_buf, c_buf)
    tokens2, first2, rest2 = gathers(1, x_two.at[0, 0, 0], x_two, c_two)

    def remote(src, dst, send, recv, to):
        return pltpu.make_async_remote_copy(
            src_ref=src, dst_ref=dst, send_sem=send, recv_sem=recv, device_id={"lang": to}, device_id_type=MESH
        )

    def columns_half(ref, n):
        return ref.at[:, pl.ds(n * HALF, HALF)]

    def leg_to(n):
        return lax.rem(z + (4 if n % 2 == 0 else 12), LANGS)

    def first_leg(n):
        src = columns_half(tok if n < 2 else c_buf.at[0, 0, 0], n % 2)
        return remote(src, relay.at[n], i_send.at[n], i_recv.at[n], leg_to(n))

    def second_leg(n):
        dst = columns_half(x_two.at[0, 0, 0], n) if n < 2 else columns_half(c_two.at[0, 0, 0], 3 - n)
        return remote(relay.at[n], dst, r_send.at[n], r_recv.at[n], leg_to(n))

    def forward(n):
        first_leg(n).wait_recv()
        second_leg(n).start()

    pl.semaphore_wait(barrier, (NF - 1) + (NY - 1) + (LANGS - 1))
    tokens.ready((0, 0))
    first_leg(0).start()
    first_leg(1).start()

    lens_copy.wait()
    for copy in cot_copies:
        copy.wait()
    token = (y * NF + x * 2 + core) * ROWS
    slot = token // SEQ
    here, after = lens[0, slot], lens[0, jnp.minimum(slot + 1, 11)]
    place = lax.broadcasted_iota(jnp.int32, (ROWS, D), 0) + (token - slot * SEQ)
    kept = place < jnp.where(place < SEQ, here, after + SEQ)
    mine = c_buf[0, 0, 0].astype(jnp.float32)
    c_buf[0, 0, 0] = jnp.where(kept, mine, 0.0).astype(jnp.bfloat16)
    first_leg(2).start()
    first_leg(3).start()

    for copy in local:
        copy.wait()

    @pl.loop(0, 8)
    def _(k):
        low = lax.rem(z + pick(k, COLUMN_ORDER), LANGS)
        wdn_t[pl.ds(pl.multiple_of(k * DS, DS), DS), :] = wdn[:, columns(low)].T
        high = lax.rem(low + 8, LANGS)
        wdn_t[pl.ds(pl.multiple_of(HALF + k * DS, DS), DS), :] = wdn[:, columns(high)].T

    def activate(x_ref, which, second):
        base = (which * 4 + second) * 192
        v_buf[pl.ds(base, 192), :] = jnp.dot(
            x_ref[which, second].reshape(192, D), wup[...], preferred_element_type=jnp.float32
        )

        @pl.loop(0, 4)
        def _(i):
            rows = pl.ds(pl.multiple_of(base + i * ROWS, 16), ROWS)
            v = v_buf[rows, :]
            k = 0.7978845608028654
            sq = v * v
            t = jnp.tanh(k * (v + 0.044715 * (sq * v)))
            cdf = 0.5 * (1.0 + t)
            v_buf[rows, :] = cdf + 0.5 * v * (1.0 - t * t) * (k * (1.0 + 3.0 * 0.044715 * sq))
            hp[rows, :] = (v * cdf).astype(jnp.bfloat16)

    def turn(dst, start, count):
        @pl.loop(start, start + count)
        def _(i):
            part = pl.ds(pl.multiple_of(i * 128, 128), 128)
            dst[:, part] = hp[part, :].T

    def product(grads_t, rows_ref, *blocks):
        cols = [rows_ref[:, :, :, :, columns(b)].reshape(LTOK, DS) for b in blocks]
        return jnp.dot(
            grads_t[...],
            cols[0] if len(cols) == 1 else jnp.concatenate(cols, axis=1),
            preferred_element_type=jnp.float32,
        ).astype(jnp.bfloat16)

    def down(c_ref, *places):
        return product(h_t, c_ref, *places)

    def up(x_ref, *blocks):
        return product(p_t, x_ref, *blocks)

    def grad_copy(sign, number, k, source):
        out, inbox = (out_dn, in_dn) if sign else (out_up, in_up)
        send, recv = (d_send, d_recv) if sign else (u_send, u_recv)
        index = number * len(NEAR[0]) + k
        return remote(
            out.at[index],
            inbox.at[lax.rem(source + 8 * number, LANGS)],
            send.at[index],
            recv.at[index],
            owner(number, k),
        )

    def send_down(number, c_ref, start, stop):
        places = tuple(COLUMN_OF[d] for d in NEAR[number])

        @pl.loop(start, stop)
        def _(pair):
            k = 2 * pair
            both = down(c_ref, pick(k, places), pick(k + 1, places))
            for n in range(2):
                out_dn[number * len(NEAR[0]) + k + n] = both[:, n * DS : (n + 1) * DS]
                grad_copy(1, number, k + n, z).start()

    def send_up(number, x_ref, start, stop):
        @pl.loop(start, stop)
        def _(pair):
            k = 2 * pair
            both = up(x_ref, owner(number, k), owner(number, k + 1))
            for n in range(2):
                out_up[number * len(NEAR[0]) + k + n] = both[:, n * DS : (n + 1) * DS]
                grad_copy(0, number, k + n, z).start()

    def preact_grad_group(c_ref, which, second):
        hg = jnp.dot(
            c_ref[which, second].reshape(192, D), wdn_t[...], preferred_element_type=jnp.float32
        )
        rows = pl.ds((which * 4 + second) * 192, 192)
        hp[rows, :] = (hg * v_buf[rows, :]).astype(jnp.bfloat16)

    def preact_grad(c_ref, pair):
        which, second = pair // 2, 2 * (pair % 2)
        hg = jnp.dot(
            c_ref[which, second : second + 2].reshape(384, D), wdn_t[...], preferred_element_type=jnp.float32
        )
        rows = pl.ds(pair * 384, 384)
        hp[rows, :] = (hg * v_buf[rows, :]).astype(jnp.bfloat16)
        turn(p_t, pair * 3, 3)

    def with_tokens(gather_x, gather_c, x_ref, start, extra, following):
        for n, roles in enumerate(ARRIVALS):
            if n < start:
                continue
            gather_x.step(roles)
            if gather_c is not None:
                gather_c.step(roles)
            for piece in extra.get(n, ()):
                piece()
            if n == 8:
                gather_x.from_sibling(0)
                activate(x_ref, 0, 0)
            elif n == 9:
                activate(x_ref, 1, 0)
            elif n == 10:
                activate(x_ref, 0, 1)
            elif n == 11:
                gather_x.from_sibling(1)
                activate(x_ref, 1, 1)
            elif n == 12:
                activate(x_ref, 0, 2)
            elif n == 13:
                gather_x.from_sibling(2)
                activate(x_ref, 1, 2)
        following.step(ARRIVALS[0])
        activate(x_ref, 0, 3)
        following.step(ARRIVALS[1])
        turn(h_t, 0, 3)
        turn(h_t, 6, 3)
        following.step(ARRIVALS[2])
        gather_x.from_sibling(3)
        activate(x_ref, 1, 3)
        following.step(ARRIVALS[3])
        turn(h_t, 3, 3)
        turn(h_t, 9, 3)
        following.step(ARRIVALS[4])
        if gather_c is not None:
            for second in range(4):
                gather_c.from_sibling(second)

    def begin_two():
        second_leg(0).wait_recv()
        second_leg(1).wait_recv()
        tokens2.ready((0, 0))

    with_tokens(
        tokens, None, x_buf, 0,
        {
            4: [lambda: rest.ready((0, 0))],
            5: [lambda: forward(0), lambda: forward(1)],
            10: [lambda: forward(2), lambda: forward(3)],
        },
        rest,
    )
    for n, roles in enumerate(ARRIVALS):
        if n < 5:
            continue
        rest.step(roles)
        if n == 5:
            begin_two()
        elif n == 9:
            second_leg(2).wait_recv()
            second_leg(3).wait_recv()
            first2.ready((0, 0))
        elif n == 11:
            rest.from_sibling(0)
            rest.from_sibling(1)
            preact_grad(c_buf, 0)
        elif n == 12:
            preact_grad(c_buf, 2)
        if n >= 10:
            tokens2.step(ARRIVALS[n - 10])
            first2.step(ARRIVALS[n - 10])
    rest.from_sibling(2)
    rest.from_sibling(3)

    def own_down():
        in_dn[z] = down(c_buf, OWN_COLUMNS)

    def own_up():
        in_up[z] = up(x_buf, z)

    with_tokens(
        tokens2, first2, x_two, 5,
        {
            5: [functools.partial(send_down, 0, c_buf, 0, 4)],
            6: [
                functools.partial(send_down, 0, c_buf, 4, 5),
                own_down,
                functools.partial(preact_grad, c_buf, 1),
            ],
            7: [functools.partial(preact_grad, c_buf, 3), lambda: rest2.ready((0, 0))],
            8: [functools.partial(send_up, 0, x_buf, 0, 2)],
            9: [functools.partial(send_up, 0, x_buf, 2, 4)],
            10: [functools.partial(send_up, 0, x_buf, 4, 5)],
        },
        rest2,
    )
    send_down(1, c_two, 0, 2)
    for n, roles in enumerate(ARRIVALS):
        if n < 5:
            continue
        rest2.step(roles)
        if n == 6:
            own_up()
        elif n == 11:
            rest2.from_sibling(0)
            rest2.from_sibling(1)
            preact_grad(c_two, 0)
        elif n == 12:
            preact_grad(c_two, 2)
        elif n == 13:
            rest2.from_sibling(2)
            preact_grad_group(c_two, 0, 2)
        elif n == 14:
            preact_grad_group(c_two, 1, 2)
    preact_grad_group(c_two, 0, 3)
    turn(p_t, 3, 3)
    rest2.from_sibling(3)
    preact_grad_group(c_two, 1, 3)
    turn(p_t, 9, 3)
    send_up(1, x_two, 0, 2)
    opposite = lax.rem(z + 8, LANGS)
    in_up[opposite] = up(x_two, z)
    in_dn[opposite] = down(c_two, OWN_COLUMNS)

    pairs[...] = jnp.zeros_like(pairs)
    targets_t = tgt[...].T
    accept_t = acc[...].T

    for sign, inbox in ((1, in_dn), (0, in_up)):
        for number in range(2):

            @pl.loop(0, len(NEAR[number]))
            def _(k):
                source = lax.rem(z + LANGS - pick(k, NEAR[number]), LANGS)
                grad_copy(sign, number, k, source).wait_recv()

        @pl.loop(0, 2)
        def _(g):
            a = jnp.concatenate(
                [
                    inbox[:, pl.ds(pl.multiple_of(g * 128 + i * 16, 16), 16), :].reshape(256, DS)
                    for i in range(8)
                ],
                axis=1,
            )
            pairs[...] += lax.dot_general(
                a, a, (((1,), (1,)), ((), ())), preferred_element_type=jnp.float32
            )

    ri = lax.broadcasted_iota(jnp.int32, (256, 256), 0)
    ci = lax.broadcasted_iota(jnp.int32, (256, 256), 1)
    same = jnp.where(lax.rem(ri, 16) == lax.rem(ci, 16), pairs[...], 0.0)
    by_row = jnp.sum(same.reshape(LANGS, 16, 256), axis=1)
    li = lax.broadcasted_iota(jnp.int32, (256, 128), 0) // 16
    lj = lax.broadcasted_iota(jnp.int32, (256, 128), 1)
    select = (li == lj).astype(jnp.float32)
    st1[f] = jnp.dot(
        by_row, select, precision=lax.Precision.HIGHEST, preferred_element_type=jnp.float32
    )
    sends = exchange(st1, "fsdp", NF, f, s1_send, s1_recv)
    st2[y] = jnp.sum(st1[...], axis=0)
    sends += exchange(st2, "dp", NY, y, s2_send, s2_recv)
    st3[z] = jnp.sum(st2[...], axis=0)
    sends += exchange(st3, "lang", LANGS, z, s3_send, s3_recv)
    gram = jnp.sum(st3[...], axis=0)[:, :LANGS]

    weights, cos_pairs = vaccinate(gram, targets_t, accept_t)
    nt_out[...] = (1.0 - ema_rate) * tgt[...] + ema_rate * cos_pairs
    wv[...] = jnp.broadcast_to(weights, (LANGS, DS))

    for inbox, half in ((in_up, 0), (in_dn, 1)):

        @pl.loop(0, 4)
        def _(r):
            rows = pl.ds(pl.multiple_of(r * 64, 64), 64)
            total = jnp.zeros((64, DS), jnp.float32)
            for l in range(LANGS):
                total = total + wv[l : l + 1, :] * inbox[l, rows, :].astype(jnp.float32)
            if half == 0:
                comb[rows, :] = total
            else:
                dn_out[rows, :] = total

    up_out[...] = comb[...].T

    for copy in sends:
        copy.wait_send()

    for gather in (tokens, rest, tokens2, first2, rest2):
        for copy in gather.started:
            copy.wait_send()
    for n in range(4):
        first_leg(n).wait_send()
        second_leg(n).wait_send()
    for number in range(2):

        @pl.loop(0, len(NEAR[number]))
        def _(k):
            grad_copy(1, number, k, z).wait_send()
            grad_copy(0, number, k, z).wait_send()


def on_device(tokens, cotangent, lengths, up_weight, down_weight, targets, accept):
    bf16, f32 = jnp.bfloat16, jnp.float32
    dma = pltpu.SemaphoreType.DMA
    hbm = pl.BlockSpec(memory_space=pl.ANY)
    vmem = pl.BlockSpec(memory_space=pltpu.VMEM)
    return pl.pallas_call(
        kernel,
        out_shape=(
            jax.ShapeDtypeStruct((DS, HID), f32),
            jax.ShapeDtypeStruct((HID, DS), f32),
            jax.ShapeDtypeStruct((LANGS, LANGS), f32),
        ),
        in_specs=[hbm] * 7,
        out_specs=(vmem, vmem, vmem),
        scratch_shapes=[
            pltpu.VMEM((2, 4, 4, ROWS, D), bf16),
            pltpu.VMEM((2, 4, 4, ROWS, D), bf16),
            pltpu.VMEM((2, 4, 4, ROWS, D), bf16),
            pltpu.VMEM((2, 4, 4, ROWS, D), bf16),
            pltpu.VMEM((D, HID), bf16),
            pltpu.VMEM((HID, D), bf16),
            pltpu.VMEM((D, HID), bf16),
            pltpu.VMEM((LANGS, LANGS), f32),
            pltpu.VMEM((LANGS, LANGS), jnp.int32),
            pltpu.SMEM((1, 12), jnp.int32),
            pltpu.VMEM((LTOK, HID), f32),
            pltpu.VMEM((LTOK, HID), bf16),
            pltpu.VMEM((HID, LTOK), bf16),
            pltpu.VMEM((HID, LTOK), bf16),
            pltpu.VMEM((14, HID, DS), bf16),
            pltpu.VMEM((14, HID, DS), bf16),
            pltpu.VMEM((LANGS, HID, DS), bf16),
            pltpu.VMEM((LANGS, HID, DS), bf16),
            pltpu.VMEM((4, ROWS, HALF), bf16),
            pltpu.VMEM((256, 256), f32),
            pltpu.VMEM((NF, LANGS, 128), f32),
            pltpu.VMEM((NY, LANGS, 128), f32),
            pltpu.VMEM((LANGS, LANGS, 128), f32),
            pltpu.VMEM((LANGS, DS), f32),
            pltpu.VMEM((HID, DS), f32),
            dma((6,)), dma((LANGS,)), dma((360,)),
            dma((14,)), dma((14,)), dma((14,)), dma((14,)),
            dma((4,)), dma((4,)), dma((4,)), dma((4,)),
            dma((NF,)), dma((NF,)), dma((NY,)), dma((NY,)), dma((LANGS,)), dma((LANGS,)),
        ],
        compiler_params=pltpu.CompilerParams(
            collective_id=0, has_side_effects=True, vmem_limit_bytes=60 * 1024 * 1024
        ),
        cost_estimate=pl.CostEstimate(
            flops=4 * 2 * LTOK * D * HID, bytes_accessed=4 * 1024 * 1024, transcendentals=LTOK * HID
        ),
        name="vaccine_step",
    )(tokens, cotangent, lengths, up_weight, down_weight, targets, accept)


def solution(mesh):
    in_specs = (
        P("lang", ("dp", "fsdp"), None),
        P("lang", ("dp", "fsdp"), None),
        P("lang", None),
        P(None, ("dp", "fsdp")),
        P(("dp", "fsdp"), None),
        P(),
        P(),
    )
    out_specs = (P("lang", ("dp", "fsdp")), P(("dp", "fsdp"), "lang"), P())
    return jax.shard_map(
        on_device, mesh=mesh, in_specs=in_specs, out_specs=out_specs, check_vma=False
    )
```

```python
import functools

import jax
import jax.numpy as jnp
from jax import lax
from jax.experimental import pallas as pl
from jax.experimental.pallas import tpu as pltpu
from jax.sharding import PartitionSpec as P

D = 2048
FF = 8192
SEQ = 128
LTOK = 1536
LANGS = 16
NY = 4
NX = 4
NF = 8
ROWS = 48
HID = 256
DS = 128
HALF = D // 2

ema_rate = 0.01
clip_level = 0.25
MESH = pl.DeviceIdType.MESH

OFFSETS = (0, 3, 1, 2)
ARRIVALS = (
    (0, 1), (0, 2), (1, 0), (2, 0), (0, 3), (1, 1), (2, 1), (1, 2), (2, 2),
    (1, 3), (2, 3), (3, 0), (3, 1), (3, 2), (3, 3),
)
EARLY = 6
LAG = 5


class Plane:
    def __init__(self, x, y, core):
        self.x, self.y, self.core = x, y, core
        self.next = {}
        for ring in (0, 1):
            for step in (1, 3):
                dx = jnp.where(core == ring, step, 0)
                self.next[ring, step] = {
                    "dp": lax.rem(y + step - dx, 4),
                    "fsdp": lax.rem(x + dx, 4) * 2 + core,
                }
        self.sibling = {"fsdp": x * 2 + (1 - core)}


class Gather:
    def __init__(self, plane, own, buf, start, width, send, recv, sib_send, sib_recv):
        self.plane, self.own, self.buf, self.start, self.width = plane, own, buf, start, width
        self.send, self.recv, self.sib_send, self.sib_recv = send, recv, sib_send, sib_recv
        self.started = []

    def part(self, roles, half):
        if half is None:
            return self.buf.at[0, roles[0], roles[1], :, pl.ds(self.start, self.width)]
        width = self.width // 2
        return self.buf.at[0, roles[0], roles[1], :, pl.ds(self.start + half * width, width)]

    def copy(self, roles, half, ring, step, send_index, there):
        src = self.own if roles == (0, 0) else self.part(roles, half)
        copy = pltpu.make_async_remote_copy(
            src_ref=src,
            dst_ref=self.part(there, half),
            send_sem=self.send.at[send_index],
            recv_sem=self.recv.at[2 * (4 * there[0] + there[1]) + (half or 0)],
            device_id=self.plane.next[ring, step],
            device_id_type=MESH,
        )
        copy.start()
        self.started.append(copy)

    def sibling_copy(self, second):
        cols = pl.ds(self.start, self.width)
        return pltpu.make_async_remote_copy(
            src_ref=self.buf.at[0, second, :, :, cols],
            dst_ref=self.buf.at[1, second, :, :, cols],
            send_sem=self.sib_send.at[second],
            recv_sem=self.sib_recv.at[second],
            device_id=self.plane.sibling,
            device_id_type=MESH,
        )

    def to_sibling(self, second):
        copy = self.sibling_copy(second)
        copy.start()
        self.started.append(copy)

    def from_sibling(self, second):
        self.sibling_copy(second).wait_recv()

    def ready(self, roles):
        second, first = roles
        base = 4 + 4 * first
        if second == 0:
            if first == 0:
                self.copy(roles, None, 0, 1, 0, (0, 1))
                self.copy(roles, None, 0, 3, 1, (0, 2))
            elif first == 1:
                self.copy(roles, 0, 0, 1, 2, (0, 3))
            elif first == 2:
                self.copy(roles, 1, 0, 3, 3, (0, 3))
            self.copy(roles, None, 1, 1, base, (1, first))
            self.copy(roles, None, 1, 3, base + 1, (2, first))
        elif second == 1:
            self.copy(roles, 0, 1, 1, base + 2, (3, first))
        elif second == 2:
            self.copy(roles, 1, 1, 3, base + 3, (3, first))

    def arrive(self, roles):
        for half in (0, 1) if roles[0] == 3 or roles == (0, 3) else (None,):
            ref = self.part(roles, half)
            pltpu.make_async_remote_copy(
                src_ref=ref,
                dst_ref=ref,
                send_sem=self.send.at[0],
                recv_sem=self.recv.at[2 * (4 * roles[0] + roles[1]) + (half or 0)],
                device_id=self.plane.next[0, 1],
                device_id_type=MESH,
            ).wait_recv()

    def step(self, roles):
        self.arrive(roles)
        self.ready(roles)
        if roles in ((0, 3), (1, 3), (2, 3), (3, 3)):
            self.to_sibling(roles[0])


NEAR = ((5, 11, 12, 4, 13, 3, 2, 14, 1, 15), (2, 14, 1, 15))
COLUMN_ORDER = (2, 14, 1, 15, 0, 3, 12, 5)
OWN_COLUMNS = 4
COLUMN_OF = {d: i for i, d in enumerate(COLUMN_ORDER + tuple((d + 8) % 16 for d in COLUMN_ORDER))}


def pick(k, values):
    if isinstance(k, int):
        return values[k]
    found = jnp.int32(values[-1])
    for i, value in enumerate(values[:-1]):
        found = jnp.where(k == i, value, found)
    return found


def exchange(buf, axis, count, me, send, recv):
    copies = []
    for r in range(1, count):
        copy = pltpu.make_async_remote_copy(
            src_ref=buf.at[me],
            dst_ref=buf.at[me],
            send_sem=send.at[r],
            recv_sem=recv.at[r],
            device_id={axis: lax.rem(me + r, count)},
            device_id_type=MESH,
        )
        copy.start()
        copies.append(copy)
    for r in range(1, count):
        ref = buf.at[lax.rem(me + count - r, count)]
        pltpu.make_async_remote_copy(
            src_ref=ref,
            dst_ref=ref,
            send_sem=send.at[r],
            recv_sem=recv.at[r],
            device_id={axis: lax.rem(me + r, count)},
            device_id_type=MESH,
        ).wait_recv()
    return copies


def vaccinate(gram, targets_t, accept_t):
    rows = lax.broadcasted_iota(jnp.int32, (LANGS, LANGS), 0)
    cols = lax.broadcasted_iota(jnp.int32, (LANGS, LANGS), 1)
    identity = (rows == cols).astype(jnp.float32)
    roots = jnp.sqrt(1.0 - targets_t * targets_t)
    diag_col = jnp.sum(gram * identity, axis=1, keepdims=True)
    diag_row = jnp.sum(gram * identity, axis=0, keepdims=True)
    cos_pairs = gram / jnp.sqrt(diag_col * diag_row)
    inverse = 1.0 / jnp.sqrt(diag_col)
    scale = inverse / roots
    allowed = accept_t.astype(jnp.float32) * (1.0 - identity)
    coeffs, product = identity, gram
    for j in range(LANGS):
        norm_sq = jnp.sum(product * coeffs, axis=0, keepdims=True)
        over_norm = lax.rsqrt(norm_sq)
        cosine = product[j : j + 1, :] * inverse[j : j + 1, :] * over_norm
        sine = jnp.sqrt(jnp.maximum(1.0 - cosine * cosine, 0.0))
        step = (
            (norm_sq * over_norm)
            * (targets_t[j : j + 1, :] * sine - cosine * roots[j : j + 1, :])
            * scale[j : j + 1, :]
        )
        step = jnp.where(allowed[j : j + 1, :] > 0.5, step, 0.0)
        coeffs = jnp.where(rows == j, coeffs + step, coeffs)
        product = product + gram[:, j : j + 1] * step
    weights = jnp.sum(coeffs, axis=1, keepdims=True)
    along = jnp.sum(product, axis=1, keepdims=True)
    quad = jnp.sum(weights * along, axis=0, keepdims=True)
    mean_square = jnp.maximum(quad, 0.0) / (2.0 * D * FF)
    factor = jnp.minimum(1.0, clip_level / jnp.sqrt(mean_square + 1e-06))
    return weights * factor, cos_pairs


def kernel(
    tok_ref, cot_ref, len_hbm, wup_hbm, wdn_hbm, tgt_hbm, acc_hbm,
    up_out, dn_out, nt_out,
    x_buf, c_buf, x_two, c_two, wup, wdn, wdn_t, tgt, acc, lens, v_buf, hp, h_t, p_t,
    out_dn, out_up, in_dn, in_up, relay, pairs, st1, st2, st3, wv, comb,
    local_sem, cols_sem, sems,
    d_send, d_recv, u_send, u_recv, i_send, i_recv, r_send, r_recv,
    s1_send, s1_recv, s2_send, s2_recv, s3_send, s3_recv,
):
    z, y, f = lax.axis_index("lang"), lax.axis_index("dp"), lax.axis_index("fsdp")
    x, core = f // 2, lax.rem(f, 2)

    barrier = pltpu.get_barrier_semaphore()
    for axis, count, me in (("fsdp", NF, f), ("dp", NY, y), ("lang", LANGS, z)):
        for r in range(1, count):
            pl.semaphore_signal(
                barrier, inc=1, device_id={axis: lax.rem(me + r, count)}, device_id_type=MESH
            )

    def owner(number, k):
        return lax.rem(z + pick(k, NEAR[number]), LANGS)

    def columns(block):
        return pl.ds(pl.multiple_of(block * DS, DS), DS)

    def source_columns(k):
        return columns(lax.rem(z + COLUMN_ORDER[k % 8] + 8 * (k // 8), LANGS))

    plane = Plane(x, y, core)
    tok, cot = tok_ref.at[0], cot_ref.at[0]
    cot_copies = [
        pltpu.make_async_copy(
            cot.at[:, source_columns(k)], c_buf.at[0, 0, 0, :, pl.ds(k * DS, DS)], cols_sem.at[k]
        )
        for k in range(LANGS)
    ]
    lens_copy = pltpu.make_async_copy(len_hbm, lens, local_sem.at[5])
    local = [
        pltpu.make_async_copy(tok, x_buf.at[0, 0, 0], local_sem.at[0]),
        pltpu.make_async_copy(wdn_hbm, wdn, local_sem.at[1]),
        pltpu.make_async_copy(wup_hbm, wup, local_sem.at[2]),
        pltpu.make_async_copy(tgt_hbm, tgt, local_sem.at[3]),
        pltpu.make_async_copy(acc_hbm, acc, local_sem.at[4]),
    ]
    lens_copy.start()
    for copy in cot_copies + local:
        copy.start()

    early = EARLY * DS

    def gathers(number, own, x_ref, c_ref):
        start_rest = early if number else 0
        made = []
        for n, (src, buf, start, width) in enumerate(
            (
                (own, x_ref, 0, D),
                (c_ref.at[0, 0, 0, :, pl.ds(0, early)], c_ref, 0, early),
                (c_ref.at[0, 0, 0, :, pl.ds(start_rest, D - start_rest)], c_ref, start_rest, D - start_rest),
            )
        ):
            base = (3 * number + n) * 60
            parts = [sems.at[pl.ds(base + a, b)] for a, b in ((0, 20), (20, 32), (52, 4), (56, 4))]
            made.append(Gather(plane, src, buf, start, width, *parts))
        return made

    tokens, _, rest = gathers(0, tok, x_buf, c_buf)
    tokens2, first2, rest2 = gathers(1, x_two.at[0, 0, 0], x_two, c_two)

    def remote(src, dst, send, recv, to):
        return pltpu.make_async_remote_copy(
            src_ref=src, dst_ref=dst, send_sem=send, recv_sem=recv, device_id={"lang": to}, device_id_type=MESH
        )

    def columns_half(ref, n):
        return ref.at[:, pl.ds(n * HALF, HALF)]

    def leg_to(n):
        return lax.rem(z + (4 if n % 2 == 0 else 12), LANGS)

    def first_leg(n):
        src = columns_half(tok if n < 2 else c_buf.at[0, 0, 0], n % 2)
        return remote(src, relay.at[n], i_send.at[n], i_recv.at[n], leg_to(n))

    def second_leg(n):
        dst = columns_half(x_two.at[0, 0, 0], n) if n < 2 else columns_half(c_two.at[0, 0, 0], 3 - n)
        return remote(relay.at[n], dst, r_send.at[n], r_recv.at[n], leg_to(n))

    def forward(n):
        first_leg(n).wait_recv()
        second_leg(n).start()

    pl.semaphore_wait(barrier, (NF - 1) + (NY - 1) + (LANGS - 1))
    tokens.ready((0, 0))
    first_leg(0).start()
    first_leg(1).start()

    lens_copy.wait()
    for copy in cot_copies:
        copy.wait()
    token = (y * NF + x * 2 + core) * ROWS
    slot = token // SEQ
    here, after = lens[0, slot], lens[0, jnp.minimum(slot + 1, 11)]
    place = lax.broadcasted_iota(jnp.int32, (ROWS, D), 0) + (token - slot * SEQ)
    kept = place < jnp.where(place < SEQ, here, after + SEQ)
    mine = c_buf[0, 0, 0].astype(jnp.float32)
    c_buf[0, 0, 0] = jnp.where(kept, mine, 0.0).astype(jnp.bfloat16)
    first_leg(2).start()
    first_leg(3).start()

    for copy in local:
        copy.wait()

    @pl.loop(0, 8)
    def _(k):
        low = lax.rem(z + pick(k, COLUMN_ORDER), LANGS)
        wdn_t[pl.ds(pl.multiple_of(k * DS, DS), DS), :] = wdn[:, columns(low)].T
        high = lax.rem(low + 8, LANGS)
        wdn_t[pl.ds(pl.multiple_of(HALF + k * DS, DS), DS), :] = wdn[:, columns(high)].T

    def activate(x_ref, which, second):
        base = (which * 4 + second) * 192
        v_buf[pl.ds(base, 192), :] = jnp.dot(
            x_ref[which, second].reshape(192, D), wup[...], preferred_element_type=jnp.float32
        )

        @pl.loop(0, 4)
        def _(i):
            rows = pl.ds(pl.multiple_of(base + i * ROWS, 16), ROWS)
            v = v_buf[rows, :]
            k = 0.7978845608028654
            sq = v * v
            t = jnp.tanh(k * (v + 0.044715 * (sq * v)))
            cdf = 0.5 * (1.0 + t)
            v_buf[rows, :] = cdf + 0.5 * v * (1.0 - t * t) * (k * (1.0 + 3.0 * 0.044715 * sq))
            hp[rows, :] = (v * cdf).astype(jnp.bfloat16)

    def turn(dst, start, count):
        @pl.loop(start, start + count)
        def _(i):
            part = pl.ds(pl.multiple_of(i * 128, 128), 128)
            dst[:, part] = hp[part, :].T

    def product(grads_t, rows_ref, *blocks):
        cols = [rows_ref[:, :, :, :, columns(b)].reshape(LTOK, DS) for b in blocks]
        return jnp.dot(
            grads_t[...],
            cols[0] if len(cols) == 1 else jnp.concatenate(cols, axis=1),
            preferred_element_type=jnp.float32,
        ).astype(jnp.bfloat16)

    def down(c_ref, *places):
        return product(h_t, c_ref, *places)

    def up(x_ref, *blocks):
        return product(p_t, x_ref, *blocks)

    def grad_copy(sign, number, k, source):
        out, inbox = (out_dn, in_dn) if sign else (out_up, in_up)
        send, recv = (d_send, d_recv) if sign else (u_send, u_recv)
        index = number * len(NEAR[0]) + k
        return remote(
            out.at[index],
            inbox.at[lax.rem(source + 8 * number, LANGS)],
            send.at[index],
            recv.at[index],
            owner(number, k),
        )

    def send_down(number, c_ref, start, stop):
        places = tuple(COLUMN_OF[d] for d in NEAR[number])

        @pl.loop(start, stop)
        def _(pair):
            k = 2 * pair
            both = down(c_ref, pick(k, places), pick(k + 1, places))
            for n in range(2):
                out_dn[number * len(NEAR[0]) + k + n] = both[:, n * DS : (n + 1) * DS]
                grad_copy(1, number, k + n, z).start()

    def send_up(number, x_ref, start, stop):
        @pl.loop(start, stop)
        def _(pair):
            k = 2 * pair
            both = up(x_ref, owner(number, k), owner(number, k + 1))
            for n in range(2):
                out_up[number * len(NEAR[0]) + k + n] = both[:, n * DS : (n + 1) * DS]
                grad_copy(0, number, k + n, z).start()

    def preact_grad_group(c_ref, which, second):
        hg = jnp.dot(
            c_ref[which, second].reshape(192, D), wdn_t[...], preferred_element_type=jnp.float32
        )
        rows = pl.ds((which * 4 + second) * 192, 192)
        hp[rows, :] = (hg * v_buf[rows, :]).astype(jnp.bfloat16)

    def preact_grad(c_ref, pair):
        which, second = pair // 2, 2 * (pair % 2)
        hg = jnp.dot(
            c_ref[which, second : second + 2].reshape(384, D), wdn_t[...], preferred_element_type=jnp.float32
        )
        rows = pl.ds(pair * 384, 384)
        hp[rows, :] = (hg * v_buf[rows, :]).astype(jnp.bfloat16)
        turn(p_t, pair * 3, 3)

    def with_tokens(gather_x, gather_c, x_ref, extra, following):
        for n, roles in enumerate(ARRIVALS):
            gather_x.step(roles)
            if gather_c is not None and n >= LAG:
                gather_c.step(ARRIVALS[n - LAG])
            for piece in extra.get(n, ()):
                piece()
            if n == 8:
                gather_x.from_sibling(0)
                activate(x_ref, 0, 0)
            elif n == 9:
                activate(x_ref, 1, 0)
            elif n == 10:
                activate(x_ref, 0, 1)
            elif n == 11:
                gather_x.from_sibling(1)
                activate(x_ref, 1, 1)
            elif n == 12:
                activate(x_ref, 0, 2)
            elif n == 13:
                gather_x.from_sibling(2)
                activate(x_ref, 1, 2)
        def next_step(n):
            if gather_c is not None:
                gather_c.step(ARRIVALS[len(ARRIVALS) - LAG + n])
            following.step(ARRIVALS[n])

        next_step(0)
        activate(x_ref, 0, 3)
        next_step(1)
        turn(h_t, 0, 3)
        turn(h_t, 6, 3)
        next_step(2)
        gather_x.from_sibling(3)
        activate(x_ref, 1, 3)
        next_step(3)
        turn(h_t, 3, 3)
        turn(h_t, 9, 3)
        next_step(4)
        if gather_c is not None:
            for second in range(4):
                gather_c.from_sibling(second)

    def begin_two():
        second_leg(0).wait_recv()
        second_leg(1).wait_recv()
        tokens2.ready((0, 0))

    with_tokens(
        tokens, None, x_buf,
        {
            4: [lambda: rest.ready((0, 0))],
            5: [lambda: forward(0), lambda: forward(1)],
            10: [lambda: forward(2), lambda: forward(3)],
        },
        rest,
    )
    for n, roles in enumerate(ARRIVALS):
        if n < 5:
            continue
        rest.step(roles)
        if n == 8:
            begin_two()
        elif n == 11:
            rest.from_sibling(0)
            rest.from_sibling(1)
            preact_grad(c_buf, 0)
        elif n == 12:
            preact_grad(c_buf, 2)

    def begin_first_two():
        second_leg(2).wait_recv()
        second_leg(3).wait_recv()
        first2.ready((0, 0))

    rest.from_sibling(2)
    rest.from_sibling(3)

    def own_down():
        in_dn[z] = down(c_buf, OWN_COLUMNS)

    def own_up():
        in_up[z] = up(x_buf, z)

    with_tokens(
        tokens2, first2, x_two,
        {
            0: [functools.partial(send_down, 0, c_buf, 0, 2)],
            1: [functools.partial(send_down, 0, c_buf, 2, 4)],
            2: [functools.partial(send_down, 0, c_buf, 4, 5), own_down],
            3: [functools.partial(preact_grad, c_buf, 1), begin_first_two],
            4: [functools.partial(preact_grad, c_buf, 3), lambda: rest2.ready((0, 0))],
            5: [functools.partial(send_up, 0, x_buf, 0, 2)],
            6: [functools.partial(send_up, 0, x_buf, 2, 4)],
            7: [functools.partial(send_up, 0, x_buf, 4, 5)],
        },
        rest2,
    )
    send_down(1, c_two, 0, 2)
    for n, roles in enumerate(ARRIVALS):
        if n < 5:
            continue
        rest2.step(roles)
        if n == 6:
            own_up()
        elif n == 11:
            rest2.from_sibling(0)
            rest2.from_sibling(1)
            preact_grad(c_two, 0)
        elif n == 12:
            preact_grad(c_two, 2)
        elif n == 13:
            rest2.from_sibling(2)
            preact_grad_group(c_two, 0, 2)
        elif n == 14:
            preact_grad_group(c_two, 1, 2)
    preact_grad_group(c_two, 0, 3)
    turn(p_t, 3, 3)
    rest2.from_sibling(3)
    preact_grad_group(c_two, 1, 3)
    turn(p_t, 9, 3)
    send_up(1, x_two, 0, 2)
    opposite = lax.rem(z + 8, LANGS)
    in_up[opposite] = up(x_two, z)
    in_dn[opposite] = down(c_two, OWN_COLUMNS)

    pairs[...] = jnp.zeros_like(pairs)
    targets_t = tgt[...].T
    accept_t = acc[...].T

    for sign, inbox in ((1, in_dn), (0, in_up)):
        for number in range(2):

            @pl.loop(0, len(NEAR[number]))
            def _(k):
                source = lax.rem(z + LANGS - pick(k, NEAR[number]), LANGS)
                grad_copy(sign, number, k, source).wait_recv()

        @pl.loop(0, 2)
        def _(g):
            a = jnp.concatenate(
                [
                    inbox[:, pl.ds(pl.multiple_of(g * 128 + i * 16, 16), 16), :].reshape(256, DS)
                    for i in range(8)
                ],
                axis=1,
            )
            pairs[...] += lax.dot_general(
                a, a, (((1,), (1,)), ((), ())), preferred_element_type=jnp.float32
            )

    ri = lax.broadcasted_iota(jnp.int32, (256, 256), 0)
    ci = lax.broadcasted_iota(jnp.int32, (256, 256), 1)
    same = jnp.where(lax.rem(ri, 16) == lax.rem(ci, 16), pairs[...], 0.0)
    by_row = jnp.sum(same.reshape(LANGS, 16, 256), axis=1)
    li = lax.broadcasted_iota(jnp.int32, (256, 128), 0) // 16
    lj = lax.broadcasted_iota(jnp.int32, (256, 128), 1)
    select = (li == lj).astype(jnp.float32)
    st1[f] = jnp.dot(
        by_row, select, precision=lax.Precision.HIGHEST, preferred_element_type=jnp.float32
    )
    sends = exchange(st1, "fsdp", NF, f, s1_send, s1_recv)
    st2[y] = jnp.sum(st1[...], axis=0)
    sends += exchange(st2, "dp", NY, y, s2_send, s2_recv)
    st3[z] = jnp.sum(st2[...], axis=0)
    sends += exchange(st3, "lang", LANGS, z, s3_send, s3_recv)
    gram = jnp.sum(st3[...], axis=0)[:, :LANGS]

    weights, cos_pairs = vaccinate(gram, targets_t, accept_t)
    nt_out[...] = (1.0 - ema_rate) * tgt[...] + ema_rate * cos_pairs
    wv[...] = jnp.broadcast_to(weights, (LANGS, DS))

    for inbox, half in ((in_up, 0), (in_dn, 1)):

        @pl.loop(0, 4)
        def _(r):
            rows = pl.ds(pl.multiple_of(r * 64, 64), 64)
            total = jnp.zeros((64, DS), jnp.float32)
            for l in range(LANGS):
                total = total + wv[l : l + 1, :] * inbox[l, rows, :].astype(jnp.float32)
            if half == 0:
                comb[rows, :] = total
            else:
                dn_out[rows, :] = total

    up_out[...] = comb[...].T

    for copy in sends:
        copy.wait_send()

    for gather in (tokens, rest, tokens2, first2, rest2):
        for copy in gather.started:
            copy.wait_send()
    for n in range(4):
        first_leg(n).wait_send()
        second_leg(n).wait_send()
    for number in range(2):

        @pl.loop(0, len(NEAR[number]))
        def _(k):
            grad_copy(1, number, k, z).wait_send()
            grad_copy(0, number, k, z).wait_send()


def on_device(tokens, cotangent, lengths, up_weight, down_weight, targets, accept):
    bf16, f32 = jnp.bfloat16, jnp.float32
    dma = pltpu.SemaphoreType.DMA
    hbm = pl.BlockSpec(memory_space=pl.ANY)
    vmem = pl.BlockSpec(memory_space=pltpu.VMEM)
    return pl.pallas_call(
        kernel,
        out_shape=(
            jax.ShapeDtypeStruct((DS, HID), f32),
            jax.ShapeDtypeStruct((HID, DS), f32),
            jax.ShapeDtypeStruct((LANGS, LANGS), f32),
        ),
        in_specs=[hbm] * 7,
        out_specs=(vmem, vmem, vmem),
        scratch_shapes=[
            pltpu.VMEM((2, 4, 4, ROWS, D), bf16),
            pltpu.VMEM((2, 4, 4, ROWS, D), bf16),
            pltpu.VMEM((2, 4, 4, ROWS, D), bf16),
            pltpu.VMEM((2, 4, 4, ROWS, D), bf16),
            pltpu.VMEM((D, HID), bf16),
            pltpu.VMEM((HID, D), bf16),
            pltpu.VMEM((D, HID), bf16),
            pltpu.VMEM((LANGS, LANGS), f32),
            pltpu.VMEM((LANGS, LANGS), jnp.int32),
            pltpu.SMEM((1, 12), jnp.int32),
            pltpu.VMEM((LTOK, HID), f32),
            pltpu.VMEM((LTOK, HID), bf16),
            pltpu.VMEM((HID, LTOK), bf16),
            pltpu.VMEM((HID, LTOK), bf16),
            pltpu.VMEM((14, HID, DS), bf16),
            pltpu.VMEM((14, HID, DS), bf16),
            pltpu.VMEM((LANGS, HID, DS), bf16),
            pltpu.VMEM((LANGS, HID, DS), bf16),
            pltpu.VMEM((4, ROWS, HALF), bf16),
            pltpu.VMEM((256, 256), f32),
            pltpu.VMEM((NF, LANGS, 128), f32),
            pltpu.VMEM((NY, LANGS, 128), f32),
            pltpu.VMEM((LANGS, LANGS, 128), f32),
            pltpu.VMEM((LANGS, DS), f32),
            pltpu.VMEM((HID, DS), f32),
            dma((6,)), dma((LANGS,)), dma((360,)),
            dma((14,)), dma((14,)), dma((14,)), dma((14,)),
            dma((4,)), dma((4,)), dma((4,)), dma((4,)),
            dma((NF,)), dma((NF,)), dma((NY,)), dma((NY,)), dma((LANGS,)), dma((LANGS,)),
        ],
        compiler_params=pltpu.CompilerParams(
            collective_id=0, has_side_effects=True, vmem_limit_bytes=60 * 1024 * 1024
        ),
        cost_estimate=pl.CostEstimate(
            flops=4 * 2 * LTOK * D * HID, bytes_accessed=4 * 1024 * 1024, transcendentals=LTOK * HID
        ),
        name="vaccine_step",
    )(tokens, cotangent, lengths, up_weight, down_weight, targets, accept)


def solution(mesh):
    in_specs = (
        P("lang", ("dp", "fsdp"), None),
        P("lang", ("dp", "fsdp"), None),
        P("lang", None),
        P(None, ("dp", "fsdp")),
        P(("dp", "fsdp"), None),
        P(),
        P(),
    )
    out_specs = (P("lang", ("dp", "fsdp")), P(("dp", "fsdp"), "lang"), P())
    return jax.shard_map(
        on_device, mesh=mesh, in_specs=in_specs, out_specs=out_specs, check_vma=False
    )
```
